32 devices in a mesh: section: 2 (over x), dp: 16 (over z, y, core).
Axes of the slice: x: 2, y: 2, z: 4, core: 2. Of those that a mesh axis runs over, the one named last changes fastest.
Arguments:
- inputs: bfloat16 [2, 16, 512, 768], P(None, 'dp'), may hold values from -6 to 6
- cotangent: bfloat16 [2, 16, 512, 768], P(None, 'dp'), may hold values from -6 to 6
- segments: int32 [2, 16, 512], P(None, 'dp'), may hold values from 0 to 3, never falling along the last dimension, each value on 1 to 256 neighbouring positions
- norm1_gain: bfloat16 [2, 768], P('section'), may hold values from 0.5 to 1.5
- norm1_shift: bfloat16 [2, 768], P('section'), may hold values from -1.75 to 1.75
- w_qkv: bfloat16 [2, 768, 2304], P('section'), may hold values from -0.21875 to 0.21875
- bias_query: bfloat16 [2, 768], P('section'), may hold values from -1.75 to 1.75
- bias_value: bfloat16 [2, 768], P('section'), may hold values from -1.75 to 1.75
- w_out: bfloat16 [2, 768, 768], P('section'), may hold values from -1.75 to 1.75
- bias_out: bfloat16 [2, 768], P('section'), may hold values from -1.75 to 1.75
- norm2_gain: bfloat16 [2, 768], P('section'), may hold values from 0.5 to 1.5
- norm2_shift: bfloat16 [2, 768], P('section'), may hold values from -1.75 to 1.75
- w_up: bfloat16 [2, 768, 3072], P('section'), may hold values from -0.21875 to 0.21875
- bias_up: bfloat16 [2, 3072], P('section'), may hold values from -3 to 3
- w_down: bfloat16 [2, 3072, 768], P('section'), may hold values from -0.109375 to 0.109375
- bias_down: bfloat16 [2, 768], P('section'), may hold values from -1.75 to 1.75
Outputs:
- block_out: bfloat16 [2, 2, 16, 512, 768], P('section', None, 'dp')
- input_grad: float32 [2, 2, 16, 512, 768], P('section', None, 'dp')
- grad_norm1_gain: float32 [2, 768], P('section')
- grad_norm1_shift: float32 [2, 768], P('section')
- grad_w_qkv: float32 [2, 768, 2304], P('section')
- grad_bias_query: float32 [2, 768], P('section')
- grad_bias_value: float32 [2, 768], P('section')
- grad_w_out: float32 [2, 768, 768], P('section')
- grad_bias_out: float32 [2, 768], P('section')
- grad_norm2_gain: float32 [2, 768], P('section')
- grad_norm2_shift: float32 [2, 768], P('section')
- grad_w_up: float32 [2, 768, 3072], P('section')
- grad_bias_up: float32 [2, 3072], P('section')
- grad_w_down: float32 [2, 3072, 768], P('section')
- grad_bias_down: float32 [2, 768], P('section')
The draws below stay inside these ranges and needn't reach their ends.
Inputs may be any that keep to these rules, and one draw needn't show every extreme that they name: `segments`: in each sequence the segment numbers never fall; positions with equal numbers form one packed text-image pair and attend only to one another; a pair has at most 256 positions.
All inputs are finite; a program needn't handle non-finite values.
Results may differ from the reference program's by a relative error of at most 0.017.
Values may be sent and summed in bfloat16 or wider, within the bound.
A program may use at most 320 MiB of HBM per device.

```python
import math
import jax
import jax.numpy as jnp
import numpy as np
from jax import lax

D = 768
HEAD_DIM = 64
FF = 3072
LEN = 512
NMB = 2
SEQS = 16
N_SECTION = 2


def block_levels(rng, shape, shards, least, high):
    gain = 1.0
    for axis_at, blocks in shards:
        draws = jax.random.uniform(jax.random.fold_in(jax.random.fold_in(rng, 6), axis_at), (blocks,), jnp.float32, least / len(shards), high / len(shards))
        gain = gain * jnp.repeat(jnp.exp(draws), shape[axis_at] // blocks).reshape((-1,) + (1,) * (len(shape) - 1 - axis_at))
    return gain


def length_profile(amount, total, limit, skew):
    loads = [(1 << 20) // math.isqrt(standing ** skew) + 1 for standing in range(2, amount + 1)]
    surplus, holding = total - limit - (amount - 1), [1] * (amount - 1)
    while surplus > 0:
        movable = [i for i in range(amount - 1) if holding[i] < limit]
        whole, budget = sum([loads[i] for i in movable]), surplus
        for i in movable:
            addition = min(limit - holding[i], max(1, budget * loads[i] // whole), surplus)
            holding[i] = holding[i] + addition
            surplus = surplus - addition
    return np.array([limit] + holding)


def ragged(key, number_of, total, limit, skew):
    if number_of == 2:
        one = jax.random.randint(key, (), max(1, total - limit), min(limit, total - 1) + 1)
        return jnp.stack([one, total - one])
    sizes = jnp.asarray(length_profile(number_of, total, limit, skew), jnp.int32)
    couples = (number_of - 1) // 2
    donor, taker = sizes[1:1 + 2 * couples:2], sizes[2:2 + 2 * couples:2]
    room = jnp.minimum(donor - 1, limit - taker)
    passed = jax.random.randint(jax.random.fold_in(key, 1), (couples,), 0, 1 << 20) % (room + 1)
    sizes = sizes.at[1:1 + 2 * couples:2].set(donor - passed).at[2:2 + 2 * couples:2].set(taker + passed)
    return sizes[jax.random.permutation(jax.random.fold_in(key, 2), number_of)]


def noise(key, shape, scale, most, shards=(), dtype=jnp.bfloat16):
    array = jax.random.normal(key, shape, jnp.float32) * scale
    if len(shards) > 0:
        array = block_levels(key, shape, shards, -0.22, 0.18) * array
    return jnp.clip(array, min=-most, max=most).astype(dtype)


def setup_inputs(seed: int = 0) -> dict:
    splits = jax.random.split(jax.random.key(seed), 17)
    inputs = noise(splits[0], (NMB, SEQS, LEN, D), 1.0, 6.0, ((1, 16),))
    cotangent = noise(splits[1], (NMB, SEQS, LEN, D), 1.0, 6.0, ((1, 16),))
    segments = jax.vmap(lambda own: jnp.searchsorted(jnp.cumsum(ragged(own, 4, LEN, LEN // 2, 1)), jnp.arange(LEN), side="right"))(jax.random.split(splits[2], NMB * SEQS)).reshape((NMB, SEQS, LEN)).astype(jnp.int32)
    norm1_gain = jnp.clip(1.0 + 0.1 * jax.random.normal(splits[3], (N_SECTION, D), jnp.float32), 0.5, 1.5).astype(jnp.bfloat16)
    norm1_shift = noise(splits[4], (N_SECTION, D), 0.3, 1.75, ((0, 2),))
    w_qkv = noise(splits[5], (N_SECTION, D, 3 * D), D ** -0.5, 0.21875, ((0, 2),))
    bias_query = noise(splits[6], (N_SECTION, D), 0.3, 1.75, ((0, 2),))
    bias_value = noise(splits[7], (N_SECTION, D), 0.3, 1.75, ((0, 2),))
    w_out = noise(splits[8], (N_SECTION, D, D), (D // HEAD_DIM) ** -0.5, 1.75, ((0, 2),))
    bias_out = noise(splits[9], (N_SECTION, D), 0.3, 1.75, ((0, 2),))
    norm2_gain = jnp.clip(1.0 + 0.1 * jax.random.normal(splits[10], (N_SECTION, D), jnp.float32), 0.5, 1.5).astype(jnp.bfloat16)
    norm2_shift = noise(splits[11], (N_SECTION, D), 0.3, 1.75, ((0, 2),))
    w_up = noise(splits[12], (N_SECTION, D, FF), D ** -0.5, 0.21875, ((0, 2),))
    bias_up = noise(splits[13], (N_SECTION, FF), 0.5, 3.0, ((0, 2),))
    w_down = noise(splits[14], (N_SECTION, FF, D), FF ** -0.5, 0.109375, ((0, 2),))
    bias_down = noise(splits[15], (N_SECTION, D), 0.3, 1.75, ((0, 2),))
    return {"inputs": inputs, "cotangent": cotangent, "segments": segments, "norm1_gain": norm1_gain, "norm1_shift": norm1_shift, "w_qkv": w_qkv, "bias_query": bias_query, "bias_value": bias_value, "w_out": w_out, "bias_out": bias_out, "norm2_gain": norm2_gain, "norm2_shift": norm2_shift, "w_up": w_up, "bias_up": bias_up, "w_down": w_down, "bias_down": bias_down}


@jax.custom_vjp
def low(v):
    return lax.optimization_barrier(v.astype(jnp.bfloat16)).astype(jnp.float32)

@jax.custom_vjp
def low_back(v):
    return v

def low_keep(v):
    return (low(v), None)

def low_pass(kept, grad):
    return (grad,)

def back_keep(v):
    return (v, None)

def back_low(kept, grad):
    return (low(grad),)
low.defvjp(low_keep, low_pass)
low_back.defvjp(back_keep, back_low)
group_seqs = 4

def layer_norm(values, norm_gain, norm_shift):
    centred = values - lax.optimization_barrier(jnp.mean(values, axis=-1, keepdims=True))
    spread = lax.optimization_barrier(jnp.mean(centred * centred, axis=-1, keepdims=True))
    return centred * lax.rsqrt(spread + 1e-06) * norm_gain + norm_shift

def matmul(left, weight):
    return jnp.einsum('bld,de->ble', left, weight, precision=lax.Precision.HIGHEST)

def layer(layer_in, params, seg_ids):
    norm1_gain, norm1_shift, w_qkv, bias_query, bias_value, w_out, bias_out, norm2_gain, norm2_shift, w_up, bias_up, w_down, bias_down = params
    batch, length, features = layer_in.shape
    head_count = features // HEAD_DIM
    split_shape = (batch, length, head_count, HEAD_DIM)
    normed_one = low(layer_norm(layer_in, norm1_gain, norm1_shift))
    projected = matmul(normed_one, w_qkv)
    queries = low(low_back((projected[..., :features] + bias_query) * HEAD_DIM ** (-0.5))).reshape(split_shape)
    key_rows = low(low_back(projected[..., features:2 * features])).reshape(split_shape)
    value_rows = low(low_back(projected[..., 2 * features:] + bias_value)).reshape(split_shape)
    scores = low_back(jnp.einsum('bqhd,bkhd->bhqk', queries, key_rows, precision=lax.Precision.HIGHEST))
    same_pair = (seg_ids[:, :, None] == seg_ids[:, None, :])[:, None]
    scores = jnp.where(same_pair, scores, -1000000000.0)
    row_top = lax.optimization_barrier(jnp.max(scores, axis=-1, keepdims=True))
    expo = jnp.exp(scores - row_top)
    probs = expo / lax.optimization_barrier(jnp.sum(expo, axis=-1, keepdims=True))
    mixed = jnp.einsum('bhqk,bkhd->bqhd', low(probs), value_rows, precision=lax.Precision.HIGHEST)
    mixed = low(low_back(mixed.reshape(batch, length, features)))
    residual = layer_in + low_back(matmul(mixed, w_out) + bias_out)
    normed_two = low(layer_norm(residual, norm2_gain, norm2_shift))
    upper_in = low_back(matmul(normed_two, w_up) + bias_up)
    hidden = low(jax.nn.gelu(upper_in, approximate=False))
    return residual + low_back(matmul(hidden, w_down) + bias_down)

def reference(inputs, cotangent, segments, norm1_gain, norm1_shift, w_qkv, bias_query, bias_value, w_out, bias_out, norm2_gain, norm2_shift, w_up, bias_up, w_down, bias_down):
    weights = tuple((item.astype(jnp.float32) for item in (norm1_gain, norm1_shift, w_qkv, bias_query, bias_value, w_out, bias_out, norm2_gain, norm2_shift, w_up, bias_up, w_down, bias_down)))
    first_params = tuple((item[0] for item in weights))
    second_params = tuple((item[1] for item in weights))
    micro_count, seq_count, length, features = inputs.shape
    groups = micro_count * seq_count // group_seqs
    input_blocks = inputs.reshape(groups, group_seqs, length, features)
    cot_blocks = cotangent.reshape(groups, group_seqs, length, features)
    seg_blocks = segments.reshape(groups, group_seqs, length)

    def one_group(grad_accum, block):
        block_in, block_cot, block_seg = block
        start = block_in.astype(jnp.float32)

        def stacked_layers(layer_in, params_one, params_two, offset):
            middle = layer(layer_in, params_one, block_seg)
            second_in = low_back(low(middle)) + offset
            return (middle, layer(second_in, params_two, block_seg))
        (middle, final), pull = jax.vjp(stacked_layers, start, first_params, second_params, jnp.zeros_like(start))
        grad_in, grads_one, grads_two, grad_mid = pull((jnp.zeros_like(middle), block_cot.astype(jnp.float32)))
        grad_accum = jax.tree.map(jnp.add, grad_accum, (grads_one, grads_two))
        return (grad_accum, (middle.astype(jnp.bfloat16), final.astype(jnp.bfloat16), grad_in, grad_mid))
    start_accum = jax.tree.map(jnp.zeros_like, (first_params, second_params))
    totals, (middles, finals, grad_ins, grad_mids) = lax.scan(one_group, start_accum, (input_blocks, cot_blocks, seg_blocks))
    full_shape = (micro_count, seq_count, length, features)
    block_out = jnp.stack([middles.reshape(full_shape), finals.reshape(full_shape)])
    input_grad = jnp.stack([grad_ins.reshape(full_shape), grad_mids.reshape(full_shape)])
    grads = tuple((jnp.stack([one_grad, two_grad]) for one_grad, two_grad in zip(totals[0], totals[1])))
    return (block_out, input_grad, grads[0], grads[1], grads[2], grads[3], grads[4], grads[5], grads[6], grads[7], grads[8], grads[9], grads[10], grads[11], grads[12])
```

```python
import functools
import math

import jax
import jax.numpy as jnp
from jax import lax
from jax.experimental import pallas as pl
from jax.experimental.pallas import tpu as pltpu
from jax.sharding import PartitionSpec as P

HEAD_DIM = 64
BF = jnp.bfloat16
F32 = jnp.float32
FAR = float(2**30)
VMEM_LIMIT = 60 * 2**20
ANY = pl.BlockSpec(memory_space=pl.ANY)
VM = pl.BlockSpec(memory_space=pltpu.VMEM)


def nn(left, right):
    return lax.dot_general(left, right, (((1,), (0,)), ((), ())), preferred_element_type=F32)


def nt(left, right):
    return lax.dot_general(left, right, (((1,), (1,)), ((), ())), preferred_element_type=F32)


def tn(left, right):
    return lax.dot_general(left, right, (((0,), (0,)), ((), ())), preferred_element_type=F32)


def gelu_pair(u):
    d = 1.0 + (0.3275911 / math.sqrt(2.0)) * jnp.abs(u)
    t = pl.reciprocal(d, approx=True)
    t = t * (2.0 - d * t)
    e = jnp.exp(u * u * -0.5)
    poly = 0.5 * 1.061405429
    for c in (-1.453152027, 1.421413741, -0.284496736, 0.254829592):
        poly = poly * t + 0.5 * c
    tail = poly * t * e
    cdf = jnp.where(u >= 0, 1.0 - tail, tail)
    return u * cdf, cdf + u * (e * (1.0 / math.sqrt(2.0 * math.pi)))


def normed(x):
    centred = x - jnp.mean(x, axis=-1, keepdims=True)
    rstd = lax.rsqrt(jnp.mean(centred * centred, axis=-1, keepdims=True) + 1e-06)
    return centred * rstd, rstd


def norm_back(x, gain, cot):
    xh, rstd = normed(x)
    dy = cot * gain
    m1 = jnp.mean(dy, axis=-1, keepdims=True)
    m2 = jnp.mean(dy * xh, axis=-1, keepdims=True)
    return rstd * (dy - m1 - xh * m2), cot * xh


def half_masks(length):
    lane = lax.broadcasted_iota(jnp.int32, (length, 128), 1)
    low = (lane < HEAD_DIM).astype(F32)
    return low.astype(BF), (1.0 - low).astype(BF)


class Outs:
    def __init__(self, sems):
        self.sems = sems
        self.sites = {}

    def start(self, site, src, dst):
        self.sites.setdefault(site, len(self.sites))
        copy = pltpu.make_async_copy(src, dst, self.sems.at[self.sites[site]])
        copy.start()

    def wait(self, site, src, dst):
        self.sites.setdefault(site, len(self.sites))
        pltpu.make_async_copy(src, dst, self.sems.at[self.sites[site]]).wait()


def relay_kernel(seg_ref, x_hbm, cot_hbm, wqkv_hbm, wout_hbm, wup_hbm, wdn_hbm, g1, b1, bq, bv, bo, g2, b2, bu, bd,
                 out_o, gin_o, n1_o, st_o, mt_o, rl_o, n2_o, ul_o, hid_o, dl_o, ln_o, qkv_o, e_o, li_o, rs_o, gp_o,
                 wqkv, wout, wup, wdn, xs, dls, out2, gs, n1, qkv, vt, e_v, li, mt, rs, n2, gp, hid, acc, u_v, s_v, rl, mlt, st, ds_v,
                 k2t_v, dot_v, ln, qc, kc, sem_i, sem_x, sem_o, sem_l, fs, fr, bs, br):
    sec = lax.axis_index("section")
    other = (1 - sec, lax.axis_index("dp"))
    micro, length, feats = xs.shape
    ff = hid.shape[1]
    heads = feats // HEAD_DIM
    half = length // 2
    quarter = length // 4
    chunks = ff // feats

    def remote(src, dst, s_sem, r_sem):
        return pltpu.make_async_remote_copy(
            src_ref=src, dst_ref=dst, send_sem=s_sem, recv_sem=r_sem, device_id=other, device_id_type=pl.DeviceIdType.MESH)

    def send_out(m, r):
        rows = pl.ds(r * half, half)
        return remote(out2.at[m, rows], xs.at[m, rows], fs.at[m, r], fr.at[m, r])

    def send_grad(m, r):
        rows = pl.ds(r * quarter, quarter)
        return remote(gs.at[m, rows], dls.at[m, rows], bs.at[m, r], br.at[m, r])

    def load_x(m):
        return pltpu.make_async_copy(x_hbm.at[m, 0], xs.at[m], sem_x.at[m])

    def load_cot(m):
        return pltpu.make_async_copy(cot_hbm.at[m, 0], dls.at[m], sem_x.at[m])

    barrier = pltpu.get_barrier_semaphore()
    pl.semaphore_signal(barrier, inc=1, device_id=other, device_id_type=pl.DeviceIdType.MESH)
    w_qkv, w_out, w_up, w_dn = [
        pltpu.make_async_copy(src.at[0], dst, sem_i.at[i])
        for i, (src, dst) in enumerate(((wqkv_hbm, wqkv), (wout_hbm, wout), (wup_hbm, wup), (wdn_hbm, wdn)))]

    @pl.when(sec == 0)
    def _():
        load_x(0).start()

    for c in (w_qkv, w_out, w_up, w_dn):
        c.start()

    @pl.when(sec == 0)
    def _():
        for m in range(1, micro):
            load_x(m).start()

    @pl.when(sec != 0)
    def _():
        for m in range(micro):
            load_cot(m).start()

    pl.semaphore_wait(barrier, 1)
    outs = Outs(sem_o)
    lows = half_masks(length)
    row_low = (lax.broadcasted_iota(jnp.int32, (128, length), 0) < HEAD_DIM).astype(F32)
    row_lows = (row_low.astype(BF), (1.0 - row_low).astype(BF))

    @pl.loop(0, micro)
    def _(m):
        def before(*sites):
            @pl.when(m > 0)
            def _():
                for site, src, dst in sites:
                    outs.wait(site, src, dst)

        seg = jnp.broadcast_to(seg_ref[pl.ds(m, 1), :], (128, length))
        row = lax.broadcasted_iota(jnp.int32, (128, length), 0) % HEAD_DIM
        kcode = (seg == row).astype(F32)
        qcode = jnp.where(row < 4, -FAR * (1.0 - kcode), 0.0)
        kc[...] = kcode.T.astype(BF)
        qc[...] = qcode.T.astype(BF)

        @pl.when(sec == 0)
        def _():
            load_x(m).wait()

        before(("n1", n1, n1_o.at[0]), ("qkv", qkv, qkv_o))
        for r in range(2):
            @pl.when(sec != 0)
            def _():
                send_out(m, r).wait_recv()

            @pl.loop(0, half // 128)
            def _(i):
                rows = pl.ds(pl.multiple_of(r * half + i * 128, 128), 128)
                xh, _ = normed(xs[m, rows, :].astype(F32))
                n1[rows, :] = (xh * g1[...].astype(F32) + b1[...].astype(F32)).astype(BF)

            if r == 0:
                @pl.when(m == 0)
                def _():
                    w_qkv.wait()
            rows = slice(r * half, (r + 1) * half)
            q = (nn(n1[rows, :], wqkv[:, :feats]) + bq[...].astype(F32)) * HEAD_DIM ** -0.5
            qkv[rows, :feats] = q.astype(BF)
            qkv[rows, feats:2 * feats] = nn(n1[rows, :], wqkv[:, feats:2 * feats]).astype(BF)
            v = nn(n1[rows, :], wqkv[:, 2 * feats:]) + bv[...].astype(F32)
            qkv[rows, 2 * feats:] = v.astype(BF)
            vt[:, rows] = v.T.astype(BF)
        outs.start("n1", n1, n1_o.at[m])
        before(("e", e_v, e_o), ("li", li, li_o), ("mt", mt, mt_o.at[0]))

        def score(i):
            p, h = divmod(i, 2)
            at = p * 128
            qa = qkv[:, at:at + 128] * lows[h] + qc[...] * lows[1 - h]
            ka = qkv[:, feats + at:feats + at + 128] * lows[h] + kc[...] * lows[1 - h]
            s_v[i % 2] = nt(ka, qa)

        def expo(i):
            scores = s_v[i % 2]
            e_v[i] = jnp.exp(scores - jnp.max(scores, axis=0, keepdims=True)).astype(BF)

        def mix(i):
            p, h = divmod(i, 2)
            at = p * 128
            ot = nn(vt[at:at + 128, :] * row_lows[h] + row_lows[1 - h], e_v[i])
            mine, ones = (slice(0, 64), slice(64, 65)) if h == 0 else (slice(64, 128), slice(0, 1))
            inv = 1.0 / ot[ones]
            li[i:i + 1, :] = inv
            mt[i * HEAD_DIM:(i + 1) * HEAD_DIM, :] = (ot[mine] * inv).astype(BF)

        for t in range(heads + 2):
            if t < heads:
                score(t)
            if 0 <= t - 2:
                mix(t - 2)
            if 0 <= t - 1 < heads:
                expo(t - 1)

        outs.start("mt", mt, mt_o.at[m])
        before(("rs", rs, rs_o), ("n2", n2, n2_o.at[0]))

        @pl.when(m == 0)
        def _():
            w_out.wait()

        rs[...] = xs[m].astype(F32) + tn(mt[...], wout[...]) + bo[...].astype(F32)

        @pl.loop(0, length // 128)
        def _(i):
            rows = pl.ds(pl.multiple_of(i * 128, 128), 128)
            xh, _ = normed(rs[rows, :])
            n2[rows, :] = (xh * g2[...].astype(F32) + b2[...].astype(F32)).astype(BF)

        outs.start("n2", n2, n2_o.at[m])
        before(("gp", gp, gp_o), ("hid", hid, hid_o.at[0]))

        @pl.when(m == 0)
        def _():
            w_up.wait()
            w_dn.wait()
            outs.start("qkv", qkv, qkv_o)
            outs.start("e", e_v, e_o)
            outs.start("li", li, li_o)
            outs.start("rs", rs, rs_o)

        tiles = [(r, j) for r in range(2) for j in range(chunks)]

        def place(t):
            r, j = tiles[t]
            return slice(r * half, (r + 1) * half), slice(j * feats, (j + 1) * feats)

        def up(t):
            rows, cols = place(t)
            u_v[t % 2] = nn(n2[rows, :], wup[:, cols])

        def act(t):
            rows, cols = place(t)
            h, g = gelu_pair(u_v[t % 2] + bu[:, cols].astype(F32))
            hid[rows, cols] = h.astype(BF)
            gp[rows, cols] = g.astype(BF)

        def down(t):
            rows, cols = place(t)
            term = nn(hid[rows, cols], wdn[cols, :])
            r, j = tiles[t]
            if j == 0:
                acc[rows, :] = rs[rows, :] + bd[...].astype(F32) + term
            elif j < chunks - 1:
                acc[rows, :] = acc[rows, :] + term
            else:
                out2[m, rows, :] = (acc[rows, :] + term).astype(BF)

                @pl.when(sec == 0)
                def _():
                    send_out(m, r).start()

        for t in range(len(tiles) + 2):
            if t < len(tiles):
                up(t)
            if 0 <= t - 2:
                down(t - 2)
            if 0 <= t - 1 < len(tiles):
                act(t - 1)

        before(("out", out2.at[0], out_o.at[0]))
        outs.start("out", out2.at[m], out_o.at[m])
        outs.start("hid", hid, hid_o.at[m])

        @pl.when(m == 0)
        def _():
            outs.start("gp", gp, gp_o)

    for site, src, dst in (("n1", n1, n1_o.at[0]), ("mt", mt, mt_o.at[0]), ("n2", n2, n2_o.at[0]), ("hid", hid, hid_o.at[0]),
                           ("out", out2.at[0], out_o.at[0])):
        outs.wait(site, src, dst)

    lane = lax.broadcasted_iota(jnp.int32, (length, 128), 1)
    ones = ((jnp.logical_and(lane >= 64, lane < 66)).astype(F32).astype(BF), (lane < 2).astype(F32).astype(BF))
    low_f = lane < HEAD_DIM
    fill = jnp.zeros((62, length), BF)
    ul = hid

    @pl.loop(0, micro)
    def _(step):
        m = micro - 1 - step

        def before(*sites):
            @pl.when(step > 0)
            def _():
                for site, src, dst in sites:
                    outs.wait(site, src, dst)

        loads = [pltpu.make_async_copy(a, b, sem_l.at[i]) for i, (a, b) in enumerate(
            ((gp_o, gp), (rs_o, rs), (mt_o.at[0], mt), (li_o, li), (qkv_o, qkv), (e_o, e_v)))]
        l_gp, l_rs, l_mt, l_li, l_qkv, l_e = loads

        def loaded(*copies):
            @pl.when(step > 0)
            def _():
                for c in copies:
                    c.wait()

        before(("gin", rs, gin_o.at[0]))

        @pl.when(step > 0)
        def _():
            for c in loads:
                c.start()

        @pl.when(sec != 0)
        def _():
            load_cot(m).wait()

        loaded(l_gp)
        before(("ul", ul, ul_o.at[0]))
        for r in range(2):
            @pl.when(sec == 0)
            def _():
                send_grad(m, 2 * r).wait_recv()
                send_grad(m, 2 * r + 1).wait_recv()

            rows = slice(r * half, (r + 1) * half)
            for j in range(chunks):
                cols = slice(j * feats, (j + 1) * feats)
                ul[rows, cols] = (nt(dls[m, rows, :], wdn[cols, :]) * gp[rows, cols].astype(F32)).astype(BF)
        acc[...] = nt(ul[...], wup[...])
        before(("dl", dls.at[0], dl_o.at[0]), ("rl", rl, rl_o.at[0]), ("ln", ln, ln_o.at[0]))
        outs.start("dl", dls.at[m], dl_o.at[m])
        outs.start("ul", ul, ul_o.at[m])
        loaded(l_rs)
        ln[...] = jnp.zeros_like(ln)

        @pl.loop(0, length // 128)
        def _(i):
            rows = pl.ds(pl.multiple_of(i * 128, 128), 128)
            cot = acc[rows, :]
            dx, gx = norm_back(rs[rows, :], g2[...].astype(F32), cot)
            ln[2:3, :] += jnp.sum(gx, axis=0, keepdims=True)
            ln[3:4, :] += jnp.sum(cot, axis=0, keepdims=True)
            res = dls[m, rows, :].astype(F32) + dx
            rs[rows, :] = res
            rl[rows, :] = res.astype(BF)

        outs.start("rl", rl, rl_o.at[m])
        mlt[...] = nt(wout[...], rl[...]).astype(BF)
        loaded(l_mt, l_li, l_qkv, l_e)
        before(("st", st, st_o.at[0]))
        keep = {}

        def probe(i):
            p, h = divmod(i, 2)
            at = p * 128
            if h == 0:
                k2t_v[p % 2] = qkv[:, feats + at:feats + at + 128].astype(F32).T.astype(BF)
                scale = jnp.concatenate([jnp.broadcast_to(li[i + g:i + g + 1, :], (64, length)) for g in (0, 1)], axis=0)
                dot_v[p % 2] = (mlt[at:at + 128, :].astype(F32) * scale).astype(BF)
            mine = dot_v[p % 2, 64 * h:64 * h + 64, :]
            delta = -jnp.sum(mine.astype(F32) * mt[i * 64:(i + 1) * 64, :].astype(F32), axis=0, keepdims=True)
            d_hi = delta.astype(BF)
            d_lo = (delta - d_hi.astype(F32)).astype(BF)
            extra = jnp.concatenate([d_hi, d_lo, fill], axis=0)
            da = jnp.concatenate((mine, extra) if h == 0 else (extra, mine), axis=0)
            va = qkv[:, 2 * feats + at:2 * feats + at + 128] * lows[h] + ones[h]
            s_v[i % 2] = nn(va, da)

        def scale_back(i):
            ds_v[i % 2] = (e_v[i].astype(F32) * s_v[i % 2]).astype(BF)

        def spread(i):
            p, h = divmod(i, 2)
            at = p * 128
            ds = ds_v[i % 2]
            dv = nt(e_v[i], dot_v[p % 2])
            dk = nn(ds, qkv[:, at:at + 128])
            dq = nn(k2t_v[p % 2], ds)[64 * h:64 * h + 64]
            if h == 0:
                keep[p] = (dv, dk, dq)
                return
            first = keep.pop(p)
            st[:, 2 * feats + at:2 * feats + at + 128] = jnp.where(low_f, first[0], dv).astype(BF)
            st[:, feats + at:feats + at + 128] = jnp.where(low_f, first[1], dk).astype(BF)
            q = jnp.concatenate([first[2], dq], axis=0).astype(BF).astype(F32) * HEAD_DIM ** -0.5
            st[:, at:at + 128] = q.T.astype(BF)

        for t in range(heads + 1):
            if t < heads:
                probe(t)
            if 0 <= t - 1:
                scale_back(t - 1)
                spread(t - 1)

        outs.start("st", st, st_o.at[m])
        for r in range(4):
            rows = slice(r * quarter, (r + 1) * quarter)
            cot = nt(st[rows, :], wqkv[...])
            dx, gx = norm_back(xs[m, rows, :].astype(F32), g1[...].astype(F32), cot)
            ln[0:1, :] += jnp.sum(gx, axis=0, keepdims=True)
            ln[1:2, :] += jnp.sum(cot, axis=0, keepdims=True)
            res = rs[rows, :] + dx
            rs[rows, :] = res
            gs[m, rows, :] = res.astype(BF)

            @pl.when(sec != 0)
            def _():
                send_grad(m, r).start()

        outs.start("gin", rs, gin_o.at[m])
        outs.start("ln", ln, ln_o.at[m])

    for site, src, dst in (("dl", dls.at[0], dl_o.at[0]), ("rl", rl, rl_o.at[0]), ("ln", ln, ln_o.at[0]), ("st", st, st_o.at[0]),
                           ("gin", rs, gin_o.at[0]), ("ul", ul, ul_o.at[0])):
        outs.wait(site, src, dst)

    @pl.when(sec == 0)
    def _():
        for m in range(micro):
            for r in range(2):
                send_out(m, r).wait_send()

    @pl.when(sec != 0)
    def _():
        for m in range(micro):
            for r in range(4):
                send_grad(m, r).wait_send()


def relay(seg, x, cot, weights, vecs):
    micro, _, length, feats = x.shape
    ff = weights[2].shape[2]
    heads = feats // HEAD_DIM
    sds = jax.ShapeDtypeStruct

    def vmem(dtype, *shape):
        return pltpu.VMEM(shape, dtype)

    outs = [
        sds((micro, length, feats), BF),
        sds((micro, length, feats), F32),
        sds((micro, length, feats), BF),
        sds((micro, length, 3 * feats), BF),
        sds((micro, feats, length), BF),
        sds((micro, length, feats), BF),
        sds((micro, length, feats), BF),
        sds((micro, length, ff), BF),
        sds((micro, length, ff), BF),
        sds((micro, length, feats), BF),
        sds((micro, 8, feats), F32),
        sds((length, 3 * feats), BF),
        sds((heads, length, length), BF),
        sds((16, length), F32),
        sds((length, feats), F32),
        sds((length, ff), BF),
    ]
    dma = pltpu.SemaphoreType.DMA
    return pl.pallas_call(
        relay_kernel,
        out_shape=outs,
        in_specs=[VM] + [ANY] * 6 + [VM] * 9,
        out_specs=[ANY] * len(outs),
        scratch_shapes=[
            vmem(BF, feats, 3 * feats), vmem(BF, feats, feats), vmem(BF, feats, ff), vmem(BF, ff, feats),
            vmem(BF, micro, length, feats), vmem(BF, micro, length, feats), vmem(BF, micro, length, feats), vmem(BF, micro, length, feats),
            vmem(BF, length, feats), vmem(BF, length, 3 * feats), vmem(BF, feats, length), vmem(BF, heads, length, length),
            vmem(F32, 16, length), vmem(BF, feats, length), vmem(F32, length, feats), vmem(BF, length, feats),
            vmem(BF, length, ff), vmem(BF, length, ff), vmem(F32, length, feats), vmem(F32, 2, length // 2, feats),
            vmem(F32, 2, length, length), vmem(BF, length, feats), vmem(BF, feats, length), vmem(BF, length, 3 * feats),
            vmem(BF, 2, length, length), vmem(BF, 2, 128, length), vmem(BF, 2, 128, length), vmem(F32, 8, feats),
            vmem(BF, length, 128), vmem(BF, length, 128),
            dma((4,)), dma((micro,)), dma((16,)), dma((6,)),
            dma((micro, 2)), dma((micro, 2)), dma((micro, 4)), dma((micro, 4)),
        ],
        compiler_params=pltpu.CompilerParams(vmem_limit_bytes=VMEM_LIMIT, collective_id=1, has_side_effects=True),
        name="layer_relay",
    )(seg, x, cot, *weights, *vecs)


INNER = 16
ORDER_A, ORDER_C = (1, 2, 4, 8), (1, 4, 2, 8)
LAGS = dict(s1=1, s2=3, s3=4, s4=5, a1=6, a2=7, a3=9, a4=10)


def exchange_kernel(group, n1_hbm, st_hbm, mt_hbm, rl_hbm, n2_hbm, ul_hbm, hid_hbm, dl_hbm, ln_ref, gq_o, go_o, gu_o, gd_o, small_o,
                    a_v, b_v, mt_v, own, sb0, sb1, sb2, sb3, rb0, rb1, rb2, rb3, xb, gath, small, rsm, xsm, ld_sem, out_sem,
                    ss, rs, as_, ar, ms, mr, xs, xr):
    sec = lax.axis_index("section")
    me = lax.axis_index("dp")
    size = gath.shape[1]
    outer = group // INNER
    kq, ku, kd = gq_o.shape[1] // size, gu_o.shape[1] // size, gd_o.shape[0] // size

    def bit(mask):
        return (me // mask) % 2

    def peer(mask):
        return (sec, me + mask - 2 * mask * bit(mask))

    def outer_peer(k):
        return (sec, (me + k * INNER) % group)

    barrier = pltpu.get_barrier_semaphore()
    for mask in ORDER_A:
        pl.semaphore_signal(barrier, inc=1, device_id=peer(mask), device_id_type=pl.DeviceIdType.MESH)
    for k in range(1, outer):
        pl.semaphore_signal(barrier, inc=1, device_id=outer_peer(k), device_id_type=pl.DeviceIdType.MESH)

    units = [("down", j) for j in range(kd)] + [("up", j) for j in range(ku)] + [("out", 0)] + [("qkv", j) for j in range(kq)]
    count = len(units)
    orders = [ORDER_C if u % 4 == 1 else ORDER_A for u in range(count)]
    places = {
        "down": lambda j: gd_o.at[pl.ds(j * size, size), :],
        "up": lambda j: gu_o.at[:, pl.ds(j * size, size)],
        "out": lambda j: go_o,
        "qkv": lambda j: gq_o.at[:, pl.ds(j * size, size)],
    }

    def remote(src, dst, s_sem, r_sem, device):
        return pltpu.make_async_remote_copy(
            src_ref=src, dst_ref=dst, send_sem=s_sem, recv_sem=r_sem, device_id=device, device_id_type=pl.DeviceIdType.MESH)

    def loads(u):
        kind, j = units[u]
        slot = u % 2
        cols = pl.ds(j * size, size)
        src_a, src_b = {
            "down": lambda: (hid_hbm.at[:, :, cols], dl_hbm),
            "up": lambda: (n2_hbm, ul_hbm.at[:, :, cols]),
            "out": lambda: (mt_hbm, rl_hbm),
            "qkv": lambda: (n1_hbm, st_hbm.at[:, :, cols]),
        }[kind]()
        dst_a = mt_v if kind == "out" else a_v.at[slot]
        return (pltpu.make_async_copy(src_a, dst_a, ld_sem.at[slot, 0]),
                pltpu.make_async_copy(src_b, b_v.at[slot], ld_sem.at[slot, 1]))

    live = {}
    sends = (sb0, sb1, sb2, sb3)
    recvs = (rb0, rb1, rb2, rb3)

    def own_slot(u):
        return own.at[u % own.shape[0]]

    def offsets(u):
        first, rows, out = 0, size, [(0, size)]
        for mask in orders[u]:
            rows = rows // 2
            first = first + bit(mask) * rows
            out.append((first, rows))
        return out

    def send_part(u, stage, value):
        buf = sends[stage]
        slot = u % buf.shape[0]
        buf[slot] = value.astype(BF)
        cp = remote(buf.at[slot], recvs[stage].at[u], ss.at[u, stage], rs.at[u, stage], peer(orders[u][stage]))
        cp.start()
        live[u, stage] = cp

    def rows_of(first, rows):
        return pl.ds(pl.multiple_of(first, 16), rows)

    def compute(u):
        kind, j = units[u]
        slot = u % 2
        for c in live.pop(("ld", u)):
            c.wait()
        if u + 1 < count:
            live["ld", u + 1] = loads(u + 1)
            for c in live["ld", u + 1]:
                c.start()
        half = size // 2
        mine = bit(1)

        def product(which):
            cols = pl.ds(pl.multiple_of(which * half, half), half)
            if kind == "out":
                total = None
                for k in range(mt_v.shape[0]):
                    term = nn(mt_v[k, cols, :], b_v[slot, k])
                    total = term if total is None else total + term
                return total
            left = a_v[slot, :, :, cols]
            right = b_v[slot]
            tokens = left.shape[0] * left.shape[1]
            return tn(left.reshape(tokens, half), right.reshape(tokens, size))

        send_part(u, 0, product(1 - mine))
        own_slot(u)[...] = product(mine)

        def column():
            return jnp.sum(jnp.sum(b_v[slot].astype(F32), axis=0), axis=0, keepdims=True)

        if kind == "down" and j == 0:
            small[4:5, :] = column()
        if kind == "out":
            small[5:6, :] = column()
        if kind == "qkv" and j == 0:
            small[6:7, :] = column()
        if kind == "qkv" and j == 2:
            small[7:8, :] = column()
        if kind == "up":
            small[8 + j:9 + j, :] = column()

    def reduce_step(u, stage):
        at = offsets(u)
        base = at[1][0]
        live.pop((u, stage - 1)).wait()
        first, rows = at[stage][0] - base, at[stage][1]
        ref = own_slot(u)
        if stage < 4:
            half = rows // 2
            b = bit(orders[u][stage])
            got = recvs[stage - 1]
            other = rows_of(first + (1 - b) * half, half)
            send_part(u, stage, ref[other, :] + got[u, rows_of((1 - b) * half, half), :].astype(F32))
            keep = rows_of(first + b * half, half)
            ref[keep, :] = ref[keep, :] + got[u, rows_of(b * half, half), :].astype(F32)
            return
        total = ref[rows_of(first, rows), :] + recvs[3][u].astype(F32)
        if outer > 1:
            xb[u, 0] = total.astype(BF)
            copies = [remote(xb.at[u, 0], xb.at[u, k], xs.at[u, k], xr.at[u, k], outer_peer(k)) for k in range(1, outer)]
            for c in copies:
                c.start()
            for c in copies:
                c.wait()
            slots = [(k - me // INNER) % outer for k in range(outer)]
            total = None
            for k in range(outer):
                term = xb[u, (outer - slots[k]) % outer].astype(F32)
                total = term if total is None else total + term
        gath[u, rows_of(at[4][0], rows), :] = total.astype(BF)
        gather_send(u, 1)

    def gather_send(u, step):
        first, rows = offsets(u)[5 - step]
        part = gath.at[u, rows_of(first, rows), :]
        cp = remote(part, part, as_.at[u, step - 1], ar.at[u, step - 1], peer(orders[u][4 - step]))
        cp.start()
        live[u, "a", step] = cp

    def gather_step(u, step):
        live.pop((u, "a", step)).wait()
        if step < 4:
            gather_send(u, step + 1)
        else:
            kind, j = units[u]
            cp = pltpu.make_async_copy(gath.at[u], places[kind](j), out_sem.at[u])
            cp.start()
            live["out", u] = cp

    def small_send(stage):
        cp = remote(small, rsm.at[stage], ms.at[stage], mr.at[stage], peer(ORDER_A[stage]))
        cp.start()
        live["small", stage] = cp

    def small_step(stage):
        live.pop(("small", stage)).wait()
        small[...] = small[...] + rsm[stage]
        if stage < 3:
            small_send(stage + 1)
            return
        if outer > 1:
            xsm[0] = small[...]
            copies = [remote(xsm.at[0], xsm.at[k], xs.at[count, k], xr.at[count, k], outer_peer(k)) for k in range(1, outer)]
            for c in copies:
                c.start()
            for c in copies:
                c.wait()
            total = None
            for k in range(outer):
                term = xsm[(outer - (k - me // INNER) % outer) % outer]
                total = term if total is None else total + term
            small[...] = total
        small_o[...] = small[...]

    live["ld", 0] = loads(0)
    for c in live["ld", 0]:
        c.start()
    small[...] = jnp.zeros_like(small)
    small[0:4, :] = jnp.sum(ln_ref[...], axis=0)[0:4, :]
    pl.semaphore_wait(barrier, len(ORDER_A) + outer - 1)
    for tau in range(count + LAGS["a4"]):
        for step in (4, 3, 2, 1):
            u = tau - LAGS[f"a{step}"]
            if 0 <= u < count:
                gather_step(u, step)
        for stage in (4, 3, 2, 1):
            u = tau - LAGS[f"s{stage}"]
            if 0 <= u < count:
                reduce_step(u, stage)
        if tau < count:
            compute(tau)
            if tau == count - 1:
                small_send(0)
        if count < tau <= count + 4:
            small_step(tau - count - 1)
    for u in range(count):
        live.pop(("out", u)).wait()


def exchange(group, n1, st, mt, rl, n2, ul, hid, dl, ln):
    micro, length, feats = n1.shape
    ff = ul.shape[2]
    outer = group // INNER
    count = st.shape[2] // feats + 2 * (ff // feats) + 1
    sds = jax.ShapeDtypeStruct

    def vmem(dtype, *shape):
        return pltpu.VMEM(shape, dtype)

    dma = pltpu.SemaphoreType.DMA
    return pl.pallas_call(
        functools.partial(exchange_kernel, group),
        out_shape=[sds((feats, 3 * feats), BF), sds((feats, feats), BF), sds((feats, ff), BF), sds((ff, feats), BF), sds((16, feats), F32)],
        in_specs=[ANY] * 8 + [VM],
        out_specs=[ANY] * 4 + [VM],
        scratch_shapes=[
            vmem(BF, 2, micro, length, feats),
            vmem(BF, 2, micro, length, feats),
            vmem(BF, micro, feats, length),
            vmem(F32, 6, feats // 2, feats),
            vmem(BF, 2, feats // 2, feats),
            vmem(BF, 3, feats // 4, feats),
            vmem(BF, 2, feats // 8, feats),
            vmem(BF, 2, feats // 16, feats),
            vmem(BF, count, feats // 2, feats),
            vmem(BF, count, feats // 4, feats),
            vmem(BF, count, feats // 8, feats),
            vmem(BF, count, feats // 16, feats),
            vmem(BF, count, outer, feats // 16, feats) if outer > 1 else vmem(BF, 16, 128),
            vmem(BF, count, feats, feats),
            vmem(F32, 16, feats),
            vmem(F32, 4, 16, feats),
            vmem(F32, outer, 16, feats),
            dma((2, 2)),
            dma((count,)),
            dma((count, 4)),
            dma((count, 4)),
            dma((count, 4)),
            dma((count, 4)),
            dma((4,)),
            dma((4,)),
            dma((count + 1, outer)),
            dma((count + 1, outer)),
        ],
        compiler_params=pltpu.CompilerParams(vmem_limit_bytes=VMEM_LIMIT, collective_id=0, has_side_effects=True),
        name="grad_exchange",
    )(n1, st, mt, rl, n2, ul, hid, dl, ln)


def per_device(inputs, cotangent, segments, norm1_gain, norm1_shift, w_qkv, bias_query, bias_value, w_out, bias_out,
               norm2_gain, norm2_shift, w_up, bias_up, w_down, bias_down):
    micro, seqs, length, feats = inputs.shape
    weights = (w_qkv, w_out, w_up, w_down)
    vecs = (norm1_gain, norm1_shift, bias_query, bias_value, bias_out, norm2_gain, norm2_shift, bias_up, bias_down)
    seg = segments.reshape(micro, length)
    block_out, gin, n1, st, mt, rl, n2, ul, hid, dl, ln = relay(seg, inputs, cotangent, weights, vecs)[:11]
    group = lax.axis_size("dp")
    gq, go, gu, gd, small = exchange(group, n1, st, mt, rl, n2, ul, hid, dl, ln)
    wide = [g.astype(F32)[None] for g in (gq, go, gu, gd)]
    reduced = (
        small[0:1], small[1:2], wide[0], small[6:7], small[7:8], wide[1], small[5:6], small[2:3], small[3:4],
        wide[2], small[8:8 + gu.shape[1] // feats].reshape(1, -1), wide[3], small[4:5],
    )
    shape = (1, micro, seqs, length, feats)
    return (block_out.reshape(shape), gin.reshape(shape)) + reduced


def solution(mesh):
    data, seg, vec, mat = P(None, "dp", None, None), P(None, "dp", None), P("section", None), P("section", None, None)
    act = P("section", None, "dp", None, None)
    in_specs = (data, data, seg, vec, vec, mat, vec, vec, mat, vec, vec, vec, mat, vec, mat, vec)
    out_specs = (act, act, vec, vec, mat, vec, vec, mat, vec, vec, vec, mat, vec, mat, vec)
    return jax.shard_map(per_device, mesh=mesh, in_specs=in_specs, out_specs=out_specs, check_vma=False)
```

```python
import functools
import math

import jax
import jax.numpy as jnp
from jax import lax
from jax.experimental import pallas as pl
from jax.experimental.pallas import tpu as pltpu
from jax.sharding import PartitionSpec as P

HEAD_DIM = 64
BF = jnp.bfloat16
F32 = jnp.float32
FAR = float(2**30)
VMEM_LIMIT = 60 * 2**20
ANY = pl.BlockSpec(memory_space=pl.ANY)
VM = pl.BlockSpec(memory_space=pltpu.VMEM)


def nn(left, right):
    return lax.dot_general(left, right, (((1,), (0,)), ((), ())), preferred_element_type=F32)


def nt(left, right):
    return lax.dot_general(left, right, (((1,), (1,)), ((), ())), preferred_element_type=F32)


def tn(left, right):
    return lax.dot_general(left, right, (((0,), (0,)), ((), ())), preferred_element_type=F32)


def gelu_pair(u):
    d = 1.0 + (0.3275911 / math.sqrt(2.0)) * jnp.abs(u)
    t = pl.reciprocal(d, approx=True)
    t = t * (2.0 - d * t)
    e = jnp.exp(u * u * -0.5)
    poly = 0.5 * 1.061405429
    for c in (-1.453152027, 1.421413741, -0.284496736, 0.254829592):
        poly = poly * t + 0.5 * c
    tail = poly * t * e
    cdf = jnp.where(u >= 0, 1.0 - tail, tail)
    return u * cdf, cdf + u * (e * (1.0 / math.sqrt(2.0 * math.pi)))


def normed(x):
    centred = x - jnp.mean(x, axis=-1, keepdims=True)
    rstd = lax.rsqrt(jnp.mean(centred * centred, axis=-1, keepdims=True) + 1e-06)
    return centred * rstd, rstd


def norm_back(x, gain, cot):
    xh, rstd = normed(x)
    dy = cot * gain
    m1 = jnp.mean(dy, axis=-1, keepdims=True)
    m2 = jnp.mean(dy * xh, axis=-1, keepdims=True)
    return rstd * (dy - m1 - xh * m2), cot * xh


def half_masks(length):
    lane = lax.broadcasted_iota(jnp.int32, (length, 128), 1)
    low = (lane < HEAD_DIM).astype(F32)
    return low.astype(BF), (1.0 - low).astype(BF)


class Outs:
    def __init__(self, sems):
        self.sems = sems
        self.sites = {}

    def start(self, site, src, dst):
        self.sites.setdefault(site, len(self.sites))
        copy = pltpu.make_async_copy(src, dst, self.sems.at[self.sites[site]])
        copy.start()

    def wait(self, site, src, dst):
        self.sites.setdefault(site, len(self.sites))
        pltpu.make_async_copy(src, dst, self.sems.at[self.sites[site]]).wait()


def relay_kernel(seg_ref, x_hbm, cot_hbm, wqkv_hbm, wout_hbm, wup_hbm, wdn_hbm, g1, b1, bq, bv, bo, g2, b2, bu, bd,
                 out_o, gin_o, n1_o, st_o, mt_o, rl_o, n2_o, ul_o, hid_o, dl_o, ln_o, qkv_o, e_o, li_o, rs_o, gp_o,
                 wqkv, wout, wup, wdn, xs, dls, out2, gs, n1, qkv, vt, e_v, li, mt, rs, n2, gp, hid, ul, acc, u_v, s_v, rl, mlt, st, ds_v,
                 k2t_v, dot_v, ln, qc, kc, sem_i, sem_x, sem_o, sem_l, fs, fr, bs, br):
    sec = lax.axis_index("section")
    other = (1 - sec, lax.axis_index("dp"))
    micro, length, feats = xs.shape
    ff = hid.shape[1]
    heads = feats // HEAD_DIM
    half = length // 2
    quarter = length // 4
    chunks = ff // feats

    def remote(src, dst, s_sem, r_sem):
        return pltpu.make_async_remote_copy(
            src_ref=src, dst_ref=dst, send_sem=s_sem, recv_sem=r_sem, device_id=other, device_id_type=pl.DeviceIdType.MESH)

    def send_out(m, r):
        rows = pl.ds(r * half, half)
        return remote(out2.at[m, rows], xs.at[m, rows], fs.at[m, r], fr.at[m, r])

    def send_grad(m, r):
        rows = pl.ds(r * quarter, quarter)
        return remote(gs.at[m, rows], dls.at[m, rows], bs.at[m, r], br.at[m, r])

    def load_x(m):
        return pltpu.make_async_copy(x_hbm.at[m, 0], xs.at[m], sem_x.at[m])

    def load_cot(m):
        return pltpu.make_async_copy(cot_hbm.at[m, 0], dls.at[m], sem_x.at[m])

    barrier = pltpu.get_barrier_semaphore()
    pl.semaphore_signal(barrier, inc=1, device_id=other, device_id_type=pl.DeviceIdType.MESH)
    w_qkv, w_out, w_up, w_dn = [
        pltpu.make_async_copy(src.at[0], dst, sem_i.at[i])
        for i, (src, dst) in enumerate(((wqkv_hbm, wqkv), (wout_hbm, wout), (wup_hbm, wup), (wdn_hbm, wdn)))]

    @pl.when(sec == 0)
    def _():
        load_x(0).start()

    for c in (w_qkv, w_out, w_up, w_dn):
        c.start()

    @pl.when(sec == 0)
    def _():
        for m in range(1, micro):
            load_x(m).start()

    @pl.when(sec != 0)
    def _():
        for m in range(micro):
            load_cot(m).start()

    pl.semaphore_wait(barrier, 1)
    outs = Outs(sem_o)
    lows = half_masks(length)
    row_low = (lax.broadcasted_iota(jnp.int32, (128, length), 0) < HEAD_DIM).astype(F32)
    row_lows = (row_low.astype(BF), (1.0 - row_low).astype(BF))

    @pl.loop(0, micro)
    def _(m):
        def before(*sites):
            @pl.when(m > 0)
            def _():
                for site, src, dst in sites:
                    outs.wait(site, src, dst)

        seg = jnp.broadcast_to(seg_ref[m], (128, length))
        row = lax.broadcasted_iota(jnp.int32, (128, length), 0) % HEAD_DIM
        kcode = (seg == row).astype(F32)
        qcode = jnp.where(row < 4, -FAR * (1.0 - kcode), 0.0)
        kc[...] = kcode.T.astype(BF)
        qc[...] = qcode.T.astype(BF)

        @pl.when(sec == 0)
        def _():
            load_x(m).wait()

        before(("n1", n1, n1_o.at[0]), ("qkv", qkv, qkv_o))
        for r in range(2):
            @pl.when(sec != 0)
            def _():
                send_out(m, r).wait_recv()

            @pl.loop(0, half // 128)
            def _(i):
                rows = pl.ds(pl.multiple_of(r * half + i * 128, 128), 128)
                xh, _ = normed(xs[m, rows, :].astype(F32))
                n1[rows, :] = (xh * g1[...].astype(F32) + b1[...].astype(F32)).astype(BF)

            if r == 0:
                @pl.when(m == 0)
                def _():
                    w_qkv.wait()
            rows = slice(r * half, (r + 1) * half)
            q = (nn(n1[rows, :], wqkv[:, :feats]) + bq[...].astype(F32)) * HEAD_DIM ** -0.5
            qkv[rows, :feats] = q.astype(BF)
            qkv[rows, feats:2 * feats] = nn(n1[rows, :], wqkv[:, feats:2 * feats]).astype(BF)
            v = nn(n1[rows, :], wqkv[:, 2 * feats:]) + bv[...].astype(F32)
            qkv[rows, 2 * feats:] = v.astype(BF)
            vt[:, rows] = v.T.astype(BF)
        outs.start("n1", n1, n1_o.at[m])
        before(("e", e_v, e_o), ("li", li, li_o), ("mt", mt, mt_o.at[0]))

        def score(i):
            p, h = divmod(i, 2)
            at = p * 128
            qa = qkv[:, at:at + 128] * lows[h] + qc[...] * lows[1 - h]
            ka = qkv[:, feats + at:feats + at + 128] * lows[h] + kc[...] * lows[1 - h]
            s_v[i % 2] = nt(ka, qa)

        def expo(i):
            scores = s_v[i % 2]
            e_v[i] = jnp.exp(scores - jnp.max(scores, axis=0, keepdims=True)).astype(BF)

        def mix(i):
            p, h = divmod(i, 2)
            at = p * 128
            ot = nn(vt[at:at + 128, :] * row_lows[h] + row_lows[1 - h], e_v[i])
            mine, ones = (slice(0, 64), slice(64, 65)) if h == 0 else (slice(64, 128), slice(0, 1))
            inv = 1.0 / ot[ones]
            li[i:i + 1, :] = inv
            mt[i * HEAD_DIM:(i + 1) * HEAD_DIM, :] = (ot[mine] * inv).astype(BF)

        for t in range(heads + 2):
            if t < heads:
                score(t)
            if 0 <= t - 2:
                mix(t - 2)
            if 0 <= t - 1 < heads:
                expo(t - 1)

        outs.start("mt", mt, mt_o.at[m])
        before(("rs", rs, rs_o), ("n2", n2, n2_o.at[0]))

        @pl.when(m == 0)
        def _():
            w_out.wait()

        rs[...] = xs[m].astype(F32) + tn(mt[...], wout[...]) + bo[...].astype(F32)

        @pl.loop(0, length // 128)
        def _(i):
            rows = pl.ds(pl.multiple_of(i * 128, 128), 128)
            xh, _ = normed(rs[rows, :])
            n2[rows, :] = (xh * g2[...].astype(F32) + b2[...].astype(F32)).astype(BF)

        outs.start("n2", n2, n2_o.at[m])
        before(("gp", gp, gp_o), ("hid", hid, hid_o.at[0]))

        @pl.when(m == 0)
        def _():
            w_up.wait()
            w_dn.wait()
            outs.start("qkv", qkv, qkv_o)
            outs.start("e", e_v, e_o)
            outs.start("li", li, li_o)
            outs.start("rs", rs, rs_o)

        tiles = [(r, j) for r in range(2) for j in range(chunks)]

        def place(t):
            r, j = tiles[t]
            return slice(r * half, (r + 1) * half), slice(j * feats, (j + 1) * feats)

        def up(t):
            rows, cols = place(t)
            u_v[t % 2] = nn(n2[rows, :], wup[:, cols])

        def act(t):
            rows, cols = place(t)
            h, g = gelu_pair(u_v[t % 2] + bu[:, cols].astype(F32))
            hid[rows, cols] = h.astype(BF)
            gp[rows, cols] = g.astype(BF)

        def down(t):
            rows, cols = place(t)
            term = nn(hid[rows, cols], wdn[cols, :])
            r, j = tiles[t]
            if j == 0:
                acc[rows, :] = rs[rows, :] + bd[...].astype(F32) + term
            elif j < chunks - 1:
                acc[rows, :] = acc[rows, :] + term
            else:
                out2[m, rows, :] = (acc[rows, :] + term).astype(BF)

                @pl.when(sec == 0)
                def _():
                    send_out(m, r).start()

        for t in range(len(tiles) + 2):
            if t < len(tiles):
                up(t)
            if 0 <= t - 2:
                down(t - 2)
            if 0 <= t - 1 < len(tiles):
                act(t - 1)

        before(("out", out2.at[0], out_o.at[0]))
        outs.start("out", out2.at[m], out_o.at[m])
        outs.start("hid", hid, hid_o.at[m])

        @pl.when(m == 0)
        def _():
            outs.start("gp", gp, gp_o)

    lane = lax.broadcasted_iota(jnp.int32, (length, 128), 1)
    ones = ((jnp.logical_and(lane >= 64, lane < 66)).astype(F32).astype(BF), (lane < 2).astype(F32).astype(BF))
    low_f = lane < HEAD_DIM
    fill = jnp.zeros((62, length), BF)
    @pl.loop(0, micro)
    def _(step):
        m = micro - 1 - step

        def before(*sites):
            @pl.when(step > 0)
            def _():
                for site, src, dst in sites:
                    outs.wait(site, src, dst)

        loads = [pltpu.make_async_copy(a, b, sem_l.at[i]) for i, (a, b) in enumerate(
            ((gp_o, gp), (rs_o, rs), (mt_o.at[0], mt), (li_o, li), (qkv_o, qkv), (e_o, e_v)))]
        l_gp, l_rs, l_mt, l_li, l_qkv, l_e = loads

        def loaded(*copies):
            @pl.when(step > 0)
            def _():
                for c in copies:
                    c.wait()

        def fetch(*copies):
            @pl.when(step == 0)
            def _():
                for c in copies:
                    c.start()

        @pl.when(sec != 0)
        def _():
            load_cot(m).wait()

        loaded(l_gp)
        before(("ul", ul, ul_o.at[0]))
        for r in range(2):
            @pl.when(sec == 0)
            def _():
                send_grad(m, 2 * r).wait_recv()
                send_grad(m, 2 * r + 1).wait_recv()

            rows = slice(r * half, (r + 1) * half)
            for j in range(chunks):
                cols = slice(j * feats, (j + 1) * feats)
                ul[rows, cols] = (nt(dls[m, rows, :], wdn[cols, :]) * gp[rows, cols].astype(F32)).astype(BF)
        fetch(l_gp)
        before(("gin", rs, gin_o.at[0]))

        @pl.when(step > 0)
        def _():
            l_rs.start()

        acc[...] = nt(ul[...], wup[...])
        before(("dl", dls.at[0], dl_o.at[0]), ("rl", rl, rl_o.at[0]), ("ln", ln, ln_o.at[0]))
        outs.start("dl", dls.at[m], dl_o.at[m])
        outs.start("ul", ul, ul_o.at[m])
        loaded(l_rs)
        ln[...] = jnp.zeros_like(ln)

        @pl.loop(0, length // 128)
        def _(i):
            rows = pl.ds(pl.multiple_of(i * 128, 128), 128)
            cot = acc[rows, :]
            dx, gx = norm_back(rs[rows, :], g2[...].astype(F32), cot)
            ln[2:3, :] += jnp.sum(gx, axis=0, keepdims=True)
            ln[3:4, :] += jnp.sum(cot, axis=0, keepdims=True)
            res = dls[m, rows, :].astype(F32) + dx
            rs[rows, :] = res
            rl[rows, :] = res.astype(BF)

        outs.start("rl", rl, rl_o.at[m])
        mlt[...] = nt(wout[...], rl[...]).astype(BF)
        loaded(l_mt, l_li, l_qkv, l_e)
        before(("st", st, st_o.at[0]))
        keep = {}

        def probe(i):
            p, h = divmod(i, 2)
            at = p * 128
            if h == 0:
                k2t_v[p % 2] = qkv[:, feats + at:feats + at + 128].astype(F32).T.astype(BF)
                scale = jnp.concatenate([jnp.broadcast_to(li[i + g:i + g + 1, :], (64, length)) for g in (0, 1)], axis=0)
                dot_v[p % 2] = (mlt[at:at + 128, :].astype(F32) * scale).astype(BF)
            mine = dot_v[p % 2, 64 * h:64 * h + 64, :]
            delta = -jnp.sum(mine.astype(F32) * mt[i * 64:(i + 1) * 64, :].astype(F32), axis=0, keepdims=True)
            d_hi = delta.astype(BF)
            d_lo = (delta - d_hi.astype(F32)).astype(BF)
            extra = jnp.concatenate([d_hi, d_lo, fill], axis=0)
            da = jnp.concatenate((mine, extra) if h == 0 else (extra, mine), axis=0)
            va = qkv[:, 2 * feats + at:2 * feats + at + 128] * lows[h] + ones[h]
            s_v[i % 2] = nn(va, da)

        def scale_back(i):
            ds_v[i % 2] = (e_v[i].astype(F32) * s_v[i % 2]).astype(BF)

        def spread(i):
            p, h = divmod(i, 2)
            at = p * 128
            ds = ds_v[i % 2]
            dv = nt(e_v[i], dot_v[p % 2])
            dk = nn(ds, qkv[:, at:at + 128])
            dq = nn(k2t_v[p % 2], ds)[64 * h:64 * h + 64]
            if h == 0:
                keep[p] = (dv, dk, dq)
                return
            first = keep.pop(p)
            st[:, 2 * feats + at:2 * feats + at + 128] = jnp.where(low_f, first[0], dv).astype(BF)
            st[:, feats + at:feats + at + 128] = jnp.where(low_f, first[1], dk).astype(BF)
            q = jnp.concatenate([first[2], dq], axis=0).astype(BF).astype(F32) * HEAD_DIM ** -0.5
            st[:, at:at + 128] = q.T.astype(BF)

        for t in range(heads + 1):
            if t < heads:
                probe(t)
            if 0 <= t - 1:
                scale_back(t - 1)
                spread(t - 1)

        outs.start("st", st, st_o.at[m])

        @pl.when(step == 0)
        def _():
            outs.wait("mt", mt, mt_o.at[0])

        fetch(l_mt, l_li, l_qkv, l_e)
        for r in range(4):
            rows = slice(r * quarter, (r + 1) * quarter)
            cot = nt(st[rows, :], wqkv[...])
            dx, gx = norm_back(xs[m, rows, :].astype(F32), g1[...].astype(F32), cot)
            ln[0:1, :] += jnp.sum(gx, axis=0, keepdims=True)
            ln[1:2, :] += jnp.sum(cot, axis=0, keepdims=True)
            res = rs[rows, :] + dx
            rs[rows, :] = res
            gs[m, rows, :] = res.astype(BF)

            @pl.when(sec != 0)
            def _():
                send_grad(m, r).start()

        outs.start("gin", rs, gin_o.at[m])
        outs.start("ln", ln, ln_o.at[m])

    for site, src, dst in (("dl", dls.at[0], dl_o.at[0]), ("rl", rl, rl_o.at[0]), ("ln", ln, ln_o.at[0]), ("st", st, st_o.at[0]),
                           ("gin", rs, gin_o.at[0]), ("ul", ul, ul_o.at[0]), ("n1", n1, n1_o.at[0]), ("n2", n2, n2_o.at[0]),
                           ("hid", hid, hid_o.at[0]), ("out", out2.at[0], out_o.at[0])):
        outs.wait(site, src, dst)

    @pl.when(sec == 0)
    def _():
        for m in range(micro):
            for r in range(2):
                send_out(m, r).wait_send()

    @pl.when(sec != 0)
    def _():
        for m in range(micro):
            for r in range(4):
                send_grad(m, r).wait_send()


def relay(seg, x, cot, weights, vecs):
    micro, _, length, feats = x.shape
    ff = weights[2].shape[2]
    heads = feats // HEAD_DIM
    sds = jax.ShapeDtypeStruct

    def vmem(dtype, *shape):
        return pltpu.VMEM(shape, dtype)

    outs = [
        sds((micro, length, feats), BF),
        sds((micro, length, feats), F32),
        sds((micro, length, feats), BF),
        sds((micro, length, 3 * feats), BF),
        sds((micro, feats, length), BF),
        sds((micro, length, feats), BF),
        sds((micro, length, feats), BF),
        sds((micro, length, ff), BF),
        sds((micro, length, ff), BF),
        sds((micro, length, feats), BF),
        sds((micro, 8, feats), F32),
        sds((length, 3 * feats), BF),
        sds((heads, length, length), BF),
        sds((16, length), F32),
        sds((length, feats), F32),
        sds((length, ff), BF),
    ]
    dma = pltpu.SemaphoreType.DMA
    return pl.pallas_call(
        relay_kernel,
        out_shape=outs,
        in_specs=[VM] + [ANY] * 6 + [VM] * 9,
        out_specs=[ANY] * len(outs),
        scratch_shapes=[
            vmem(BF, feats, 3 * feats), vmem(BF, feats, feats), vmem(BF, feats, ff), vmem(BF, ff, feats),
            vmem(BF, micro, length, feats), vmem(BF, micro, length, feats), vmem(BF, micro, length, feats), vmem(BF, micro, length, feats),
            vmem(BF, length, feats), vmem(BF, length, 3 * feats), vmem(BF, feats, length), vmem(BF, heads, length, length),
            vmem(F32, 16, length), vmem(BF, feats, length), vmem(F32, length, feats), vmem(BF, length, feats),
            vmem(BF, length, ff), vmem(BF, length, ff), vmem(BF, length, ff), vmem(F32, length, feats), vmem(F32, 2, length // 2, feats),
            vmem(F32, 2, length, length), vmem(BF, length, feats), vmem(BF, feats, length), vmem(BF, length, 3 * feats),
            vmem(BF, 2, length, length), vmem(BF, 2, 128, length), vmem(BF, 2, 128, length), vmem(F32, 8, feats),
            vmem(BF, length, 128), vmem(BF, length, 128),
            dma((4,)), dma((micro,)), dma((16,)), dma((6,)),
            dma((micro, 2)), dma((micro, 2)), dma((micro, 4)), dma((micro, 4)),
        ],
        compiler_params=pltpu.CompilerParams(vmem_limit_bytes=VMEM_LIMIT, collective_id=1, has_side_effects=True),
        name="layer_relay",
    )(seg, x, cot, *weights, *vecs)


INNER = 16
MASKS = (1, 2, 4, 8)
LAG = dict(s1=1, s2=3, line1=4, line2=2, end2=7, ag1=7, age=7, agy2=9, core=12, done=14)


def exchange_kernel(group, n1_hbm, st_hbm, mt_hbm, rl_hbm, n2_hbm, ul_hbm, hid_hbm, dl_hbm, ln_ref, g_o, small_o, xb,
                    a_v, b_v, mt_v, own, sb0, rb0, sby, rby, line1, line2, sbe, rbe, gath, xv, small, rsm, xsm,
                    ld_sem, out_sem, cs, cr, ys, yr, ls, lr, es, er, as_, ar, ms, mr, xs, xr, xl):
    sec = lax.axis_index("section")
    me = lax.axis_index("dp")
    size = gath.shape[1]
    half, wide, q4, q8 = size // 2, size // 2, size // 4, size // 8
    outer = group // INNER
    kq, ku, kd = st_hbm.shape[2] // size, ul_hbm.shape[2] // size, hid_hbm.shape[2] // size
    kinds = (("down", 0, kd), ("up", kd, kd + ku), ("out", kd + ku, kd + ku + 1), ("qkv", kd + ku + 1, kd + ku + 1 + kq))
    count = kinds[-1][2]
    core, y, z = me % 2, (me // 2) % 2, (me // 4) % 4
    left, right = slice(0, wide), slice(wide, size)

    def to(device):
        return dict(device_id=(sec, device), device_id_type=pl.DeviceIdType.MESH)

    def peer(mask):
        return me + mask - 2 * mask * ((me // mask) % 2)

    def outer_peer(k):
        return (me + k * INNER) % group

    barrier = pltpu.get_barrier_semaphore()
    at_end = jnp.logical_or(z == 0, z == 3)
    for mask in MASKS:
        pl.semaphore_signal(barrier, inc=1, **to(peer(mask)))
    for k in range(1, outer):
        pl.semaphore_signal(barrier, inc=1, **to(outer_peer(k)))

    pl.semaphore_signal(barrier, inc=1, **to(me + 12 - 8 * z))

    def remote(src, dst, s_sem, r_sem, device):
        return pltpu.make_async_remote_copy(src_ref=src, dst_ref=dst, send_sem=s_sem, recv_sem=r_sem, **to(device))

    def rows_of(first, rows):
        return pl.ds(pl.multiple_of(first, 16), rows)

    def by_kind(u, fn):
        for kind, low, high in kinds:
            @pl.when(jnp.logical_and(u >= low, u < high))
            def _():
                fn(kind, u - low)

    def block(ref, j, axis):
        cols = pl.ds(pl.multiple_of(j * size, size), size)
        return ref.at[:, :, cols] if axis == 2 else ref.at[:, cols] if axis == 1 else ref.at[cols, :]

    def loads(u):
        def pair(kind, j, act):
            slot = u % 2
            src_a, src_b = {
                "down": lambda: (block(hid_hbm, j, 2), dl_hbm),
                "up": lambda: (n2_hbm, block(ul_hbm, j, 2)),
                "out": lambda: (mt_hbm, rl_hbm),
                "qkv": lambda: (n1_hbm, block(st_hbm, j, 2)),
            }[kind]()
            dst_a = mt_v if kind == "out" else a_v.at[slot]
            act(pltpu.make_async_copy(src_a, dst_a, ld_sem.at[slot, 0]))
            act(pltpu.make_async_copy(src_b, b_v.at[slot], ld_sem.at[slot, 1]))
        return pair

    def start_loads(u):
        by_kind(u, lambda kind, j: loads(u)(kind, j, lambda c: c.start()))

    def core_copy(u):
        return remote(sb0.at[u % 2], rb0.at[u], cs.at[u], cr.at[u], peer(1))

    def y_copy(u):
        return remote(sby.at[u], rby.at[u], ys.at[u], yr.at[u], peer(2))

    def end_copy(u):
        return remote(sbe.at[u], rbe.at[u], es.at[u], er.at[u], peer(2))

    def line_copy(u, part, up):
        ref = line1 if part == 0 else line2
        at = (u, int(up))
        sem = (u, 2 * part + int(up))
        return remote(ref.at[at], ref.at[at], ls.at[sem], lr.at[sem], me + 4 if up else me - 4)

    def compute(u):
        slot = u % 2
        by_kind(u, lambda kind, j: loads(u)(kind, j, lambda c: c.wait()))
        start_loads(u + 1)

        def column():
            return jnp.sum(jnp.sum(b_v[slot].astype(F32), axis=0), axis=0, keepdims=True)

        def products(transposed):
            def product(which):
                cols = pl.ds(pl.multiple_of(which * half, half), half)
                if transposed:
                    total = None
                    for k in range(mt_v.shape[0]):
                        term = nn(mt_v[k, cols, :], b_v[slot, k])
                        total = term if total is None else total + term
                    return total
                value = a_v[slot, :, :, cols]
                tokens = value.shape[0] * value.shape[1]
                return tn(value.reshape(tokens, half), b_v[slot].reshape(tokens, size))

            sb0[slot] = product(1 - core).astype(BF)
            core_copy(u).start()
            own[u % own.shape[0]] = product(core)

        low, high = kinds[2][1], kinds[2][2]
        is_out = jnp.logical_and(u >= low, u < high)

        @pl.when(is_out)
        def _():
            products(True)
            small[5:6, :] = column()

        @pl.when(jnp.logical_not(is_out))
        def _():
            products(False)

        @pl.when(u == 0)
        def _():
            small[4:5, :] = column()

        for j in range(ku):
            @pl.when(u == kinds[1][1] + j)
            def _():
                small[8 + j:9 + j, :] = column()

        for j, at in ((0, 6), (kq - 1, 7)):
            @pl.when(u == kinds[3][1] + j)
            def _():
                small[at:at + 1, :] = column()

    def add_core(u):
        core_copy(u).wait()
        ref = own.at[u % own.shape[0]]
        ref[...] = ref[...] + rb0[u].astype(F32)
        sby[u] = ref[rows_of((1 - y) * q4, q4), left].astype(BF)
        y_copy(u).start()

    def add_y(u):
        y_copy(u).wait()
        ref = own.at[u % own.shape[0]]
        rows = rows_of(y * q4, q4)
        ref[rows, left] = ref[rows, left] + rby[u].astype(F32)

    def along(u, part, up):
        buf = line1 if part == 0 else line2
        ref = own.at[u % own.shape[0]]
        place = z if up else 3 - z
        if part == 0:
            rows, cols = rows_of(y * q4 + (q8 if up else 0), q8), left
        else:
            rows, cols = rows_of(q4 if up else 0, q4), right

        @pl.when(place == 0)
        def _():
            buf[u, int(up)] = ref[rows, cols].astype(BF)

        @pl.when(place > 0)
        def _():
            line_copy(u, part, up).wait_recv()
            total = ref[rows, cols] + buf[u, int(up)].astype(F32)
            ref[rows, cols] = total

            @pl.when(place < 3)
            def _():
                buf[u, int(up)] = total.astype(BF)

        @pl.when(place < 3)
        def _():
            line_copy(u, part, up).start()

        @pl.when(place == 3)
        def _():
            if part == 0:
                rows_up = rows_of(core * half + y * q4 + (q8 if up else 0), q8)
                gath[u, rows_up, left] = over_outer(u, 0, ref[rows, cols]).astype(BF)
            else:
                first = q4 if up else 0
                sbe[u] = ref[rows_of(first + (1 - y) * q8, q8), right].astype(BF)
                end_copy(u).start()

    def over_outer(u, part, total):
        if outer == 1:
            return total
        at = 2 * u + part
        xv[0] = total.astype(BF)
        own_slot = pltpu.make_async_copy(xv.at[0], xb.at[at, 0], xl.at[0])
        own_slot.start()
        copies = [remote(xv.at[0], xb.at[at, k], xs.at[at, k], xr.at[at, k], outer_peer(k)) for k in range(1, outer)]
        for c in copies:
            c.start()
        own_slot.wait()
        for c in copies:
            c.wait()
        back = pltpu.make_async_copy(xb.at[at], xv, xl.at[1])
        back.start()
        back.wait()
        result = None
        for k in range(outer):
            term = xv[(me // INNER - k + outer) % outer].astype(F32)
            result = term if result is None else result + term
        return result

    def part_of(u, part, up):
        if part == 0:
            return gath.at[u, rows_of(core * half + y * q4 + (q8 if up else 0), q8), left]
        return gath.at[u, rows_of(core * half + (q4 if up else 0), q4), right]

    def gather_line(u, part, up):
        ref = part_of(u, part, up)
        sem = (u, 2 * part + int(up))
        return remote(ref, ref, as_.at[sem], ar.at[sem], me - 4 if up else me + 4)

    def gather_y(u, up):
        ref = part_of(u, 0, up)
        sem = (u, 4 + int(up))
        return remote(ref, ref, as_.at[sem], ar.at[sem], peer(2))

    def gather_end(u):
        ref = gath.at[u, rows_of(core * half + (z // 3) * q4 + y * q8, q8), right]
        sem = (u, 6)
        return remote(ref, ref, as_.at[sem], ar.at[sem], peer(2))

    def gather_core(u):
        ref = gath.at[u, rows_of(core * half, half), :]
        sem = (u, 7)
        return remote(ref, ref, as_.at[sem], ar.at[sem], peer(1))

    def finish_end(u):
        @pl.when(at_end)
        def _():
            end_copy(u).wait()
            ref = own.at[u % own.shape[0]]
            total = ref[rows_of((z // 3) * q4 + y * q8, q8), right] + rbe[u].astype(F32)
            gath[u, rows_of(core * half + (z // 3) * q4 + y * q8, q8), right] = over_outer(u, 1, total).astype(BF)

    def end_sent(u):
        @pl.when(at_end)
        def _():
            gather_end(u).start()

    def ends_joined(u):
        @pl.when(at_end)
        def _():
            gather_end(u).wait()

    def back_along(u, part, up):
        place = 3 - z if up else z

        @pl.when(place > 0)
        def _():
            gather_line(u, part, up).wait_recv()

        @pl.when(place < 3)
        def _():
            gather_line(u, part, up).start()

        if part == 0:
            gather_y(u, up).start()

    def to_core(u):
        gather_y(u, False).wait()
        gather_y(u, True).wait()
        gather_core(u).start()

    def out_copy(u):
        return pltpu.make_async_copy(gath.at[u], g_o.at[u], out_sem.at[u])

    def done(u):
        gather_core(u).wait()
        out_copy(u).start()

    def small_copy(stage):
        return remote(small, rsm.at[stage], ms.at[stage], mr.at[stage], peer(MASKS[stage]))

    def small_step(stage):
        small_copy(stage).wait()
        small[...] = small[...] + rsm[stage]
        if stage < 3:
            small_copy(stage + 1).start()
            return
        if outer > 1:
            xsm[0] = small[...]
            copies = [remote(xsm.at[0], xsm.at[k], xs.at[2 * count, k], xr.at[2 * count, k], outer_peer(k)) for k in range(1, outer)]
            for c in copies:
                c.start()
            for c in copies:
                c.wait()
            total = None
            for k in range(outer):
                term = xsm[(me // INNER - k + outer) % outer]
                total = term if total is None else total + term
            small[...] = total
        small_o[...] = small[...]

    start_loads(0)
    small[...] = jnp.zeros_like(small)
    small[0:4, :] = jnp.sum(ln_ref[...], axis=0)[0:4, :]
    pl.semaphore_wait(barrier, len(MASKS) + outer)

    @pl.loop(0, count + LAG["done"])
    def _(tau):
        def at(lag, fn):
            u = tau - lag

            @pl.when(jnp.logical_and(u >= 0, u < count))
            def _():
                fn(u)

        at(LAG["done"], done)
        at(LAG["agy2"], ends_joined)
        at(LAG["s1"], add_core)
        for up in (True, False):
            place = z if up else 3 - z
            at(LAG["line2"] + place, lambda u: along(u, 1, up))
            at(LAG["agy2"] + 3 - place, lambda u: back_along(u, 1, up))
        at(LAG["s2"], add_y)
        for up in (True, False):
            place = z if up else 3 - z
            at(LAG["line1"] + place, lambda u: along(u, 0, up))
        at(LAG["end2"], finish_end)
        at(LAG["age"], end_sent)
        for up in (True, False):
            place = z if up else 3 - z
            at(LAG["ag1"] + 3 - place, lambda u: back_along(u, 0, up))
        at(LAG["core"], to_core)
        at(0, compute)

        @pl.when(tau == count)
        def _():
            small_copy(0).start()

        for stage in range(4):
            @pl.when(tau == count + 2 + 2 * stage)
            def _():
                small_step(stage)

    @pl.loop(0, count)
    def _(u):
        out_copy(u).wait()
        for up in (True, False):
            place = z if up else 3 - z

            @pl.when(place < 3)
            def _():
                for part in (0, 1):
                    line_copy(u, part, up).wait_send()

            @pl.when(place > 0)
            def _():
                for part in (0, 1):
                    gather_line(u, part, up).wait_send()


def exchange(group, n1, st, mt, rl, n2, ul, hid, dl, ln):
    micro, length, feats = n1.shape
    ff = ul.shape[2]
    outer = group // INNER
    count = st.shape[2] // feats + 2 * (ff // feats) + 1
    half, q4, q8 = feats // 2, feats // 4, feats // 8
    sds = jax.ShapeDtypeStruct

    def vmem(dtype, *shape):
        return pltpu.VMEM(shape, dtype)

    dma = pltpu.SemaphoreType.DMA
    return pl.pallas_call(
        functools.partial(exchange_kernel, group),
        out_shape=[sds((count, feats, feats), BF), sds((16, feats), F32),
                   sds((2 * count, outer, q8, half) if outer > 1 else (16, 128), BF)],
        in_specs=[ANY] * 8 + [VM],
        out_specs=[ANY, VM, ANY],
        scratch_shapes=[
            vmem(BF, 2, micro, length, feats),
            vmem(BF, 2, micro, length, feats),
            vmem(BF, micro, feats, length),
            vmem(F32, 8, half, feats),
            vmem(BF, 2, half, feats),
            vmem(BF, count, half, feats),
            vmem(BF, count, q4, half),
            vmem(BF, count, q4, half),
            vmem(BF, count, 2, q8, half),
            vmem(BF, count, 2, q4, half),
            vmem(BF, count, q8, half),
            vmem(BF, count, q8, half),
            vmem(BF, count, feats, feats),
            vmem(BF, outer, q8, half),
            vmem(F32, 16, feats),
            vmem(F32, 4, 16, feats),
            vmem(F32, outer, 16, feats),
            dma((2, 2)),
            dma((count,)),
            dma((count,)), dma((count,)),
            dma((count,)), dma((count,)),
            dma((count, 4)), dma((count, 4)),
            dma((count,)), dma((count,)),
            dma((count, 8)), dma((count, 8)),
            dma((4,)), dma((4,)),
            dma((2 * count + 1, outer)), dma((2 * count + 1, outer)),
            dma((2,)),
        ],
        compiler_params=pltpu.CompilerParams(vmem_limit_bytes=VMEM_LIMIT, collective_id=0, has_side_effects=True),
        name="grad_exchange",
    )(n1, st, mt, rl, n2, ul, hid, dl, ln)[:2]


def finish_kernel(g, small, block_hbm, gin_hbm, block_o, gin_o, g1_o, s1_o, gq_o, bq_o, bv_o, go_o, bo_o, g2_o, s2_o, gu_o, bu_o, gd_o, bd_o,
                  narrow, stage, sem_g, sem, sem_b):
    size = g.shape[1]
    loads = [pltpu.make_async_copy(g.at[u], narrow.at[u], sem_g.at[u]) for u in range(g.shape[0])]
    for c in loads:
        c.start()
    copies = [pltpu.make_async_copy(block_hbm, block_o.at[0, :, 0], sem_b.at[0]), pltpu.make_async_copy(gin_hbm, gin_o.at[0, :, 0], sem_b.at[1])]
    for c in copies:
        c.start()
    places = [gd_o.at[0, pl.ds(j * size, size), :] for j in range(gd_o.shape[1] // size)]
    for ref in (gu_o, go_o, gq_o):
        places += [ref.at[0, :, pl.ds(j * size, size)] for j in range(ref.shape[2] // size)]
    slots = stage.shape[0]
    running = []
    for u, place in enumerate(places):
        if u >= slots:
            running[u - slots].wait()
        loads[u].wait()
        stage[u % slots] = narrow[u].astype(F32)
        c = pltpu.make_async_copy(stage.at[u % slots], place, sem.at[u])
        c.start()
        running.append(c)
    for ref, at in ((g1_o, 0), (s1_o, 1), (g2_o, 2), (s2_o, 3), (bd_o, 4), (bo_o, 5), (bq_o, 6), (bv_o, 7)):
        ref[...] = small[at:at + 1, :]
    for j in range(bu_o.shape[1] // size):
        bu_o[:, j * size:(j + 1) * size] = small[8 + j:9 + j, :]
    for c in running[-slots:] + copies:
        c.wait()


def finish(g, small, block_out, gin, ff):
    count, feats, _ = g.shape
    micro, length, _ = block_out.shape
    sds = jax.ShapeDtypeStruct
    vec = sds((1, feats), F32)
    outs = [sds((1, micro, 1, length, feats), BF), sds((1, micro, 1, length, feats), F32), vec, vec, sds((1, feats, 3 * feats), F32), vec, vec,
            sds((1, feats, feats), F32), vec, vec, vec, sds((1, feats, ff), F32), sds((1, ff), F32), sds((1, ff, feats), F32), vec]
    return pl.pallas_call(
        finish_kernel,
        out_shape=outs,
        in_specs=[ANY, VM, ANY, ANY],
        out_specs=[ANY if len(o.shape) > 2 else VM for o in outs],
        scratch_shapes=[pltpu.VMEM((count, feats, feats), BF), pltpu.VMEM((4, feats, feats), F32), pltpu.SemaphoreType.DMA((count,)),
                        pltpu.SemaphoreType.DMA((count,)), pltpu.SemaphoreType.DMA((2,))],
        compiler_params=pltpu.CompilerParams(vmem_limit_bytes=40 * 2**20),
        name="finish",
    )(g, small, block_out, gin)


def per_device(inputs, cotangent, segments, norm1_gain, norm1_shift, w_qkv, bias_query, bias_value, w_out, bias_out,
               norm2_gain, norm2_shift, w_up, bias_up, w_down, bias_down):
    weights = (w_qkv, w_out, w_up, w_down)
    vecs = (norm1_gain, norm1_shift, bias_query, bias_value, bias_out, norm2_gain, norm2_shift, bias_up, bias_down)
    block_out, gin, n1, st, mt, rl, n2, ul, hid, dl, ln = relay(segments, inputs, cotangent, weights, vecs)[:11]
    g, small = exchange(lax.axis_size("dp"), n1, st, mt, rl, n2, ul, hid, dl, ln)
    return tuple(finish(g, small, block_out, gin, w_up.shape[2]))


def solution(mesh):
    data, seg, vec, mat = P(None, "dp", None, None), P(None, "dp", None), P("section", None), P("section", None, None)
    act = P("section", None, "dp", None, None)
    in_specs = (data, data, seg, vec, vec, mat, vec, vec, mat, vec, vec, vec, mat, vec, mat, vec)
    out_specs = (act, act, vec, vec, mat, vec, vec, mat, vec, vec, vec, mat, vec, mat, vec)
    return jax.shard_map(per_device, mesh=mesh, in_specs=in_specs, out_specs=out_specs, check_vma=False)
```

```python
import functools
import math

import jax
import jax.numpy as jnp
from jax import lax
from jax.experimental import pallas as pl
from jax.experimental.pallas import tpu as pltpu
from jax.sharding import PartitionSpec as P

HEAD_DIM = 64
BF = jnp.bfloat16
F32 = jnp.float32
FAR = float(2**30)
VMEM_LIMIT = 60 * 2**20
ANY = pl.BlockSpec(memory_space=pl.ANY)
VM = pl.BlockSpec(memory_space=pltpu.VMEM)
HBM = pl.BlockSpec(memory_space=pltpu.HBM)


def nn(left, right):
    return lax.dot_general(left, right, (((1,), (0,)), ((), ())), preferred_element_type=F32)


def nt(left, right):
    return lax.dot_general(left, right, (((1,), (1,)), ((), ())), preferred_element_type=F32)


def tn(left, right):
    return lax.dot_general(left, right, (((0,), (0,)), ((), ())), preferred_element_type=F32)


def gelu_pair(u):
    d = 1.0 + (0.3275911 / math.sqrt(2.0)) * jnp.abs(u)
    t = pl.reciprocal(d, approx=True)
    t = t * (2.0 - d * t)
    e = jnp.exp(u * u * -0.5)
    poly = 0.5 * 1.061405429
    for c in (-1.453152027, 1.421413741, -0.284496736, 0.254829592):
        poly = poly * t + 0.5 * c
    tail = poly * t * e
    cdf = jnp.where(u >= 0, 1.0 - tail, tail)
    return u * cdf, cdf + u * (e * (1.0 / math.sqrt(2.0 * math.pi)))


def normed(x):
    centred = x - jnp.mean(x, axis=-1, keepdims=True)
    rstd = lax.rsqrt(jnp.mean(centred * centred, axis=-1, keepdims=True) + 1e-06)
    return centred * rstd, rstd


def norm_back(x, gain, cot):
    xh, rstd = normed(x)
    dy = cot * gain
    m1 = jnp.mean(dy, axis=-1, keepdims=True)
    m2 = jnp.mean(dy * xh, axis=-1, keepdims=True)
    return rstd * (dy - m1 - xh * m2), cot * xh


def half_masks(length):
    lane = lax.broadcasted_iota(jnp.int32, (length, 128), 1)
    low = (lane < HEAD_DIM).astype(F32)
    return low.astype(BF), (1.0 - low).astype(BF)


class Outs:
    def __init__(self, sems):
        self.sems = sems
        self.sites = {}

    def start(self, site, src, dst):
        self.sites.setdefault(site, len(self.sites))
        copy = pltpu.make_async_copy(src, dst, self.sems.at[self.sites[site]])
        copy.start()

    def wait(self, site, src, dst):
        self.sites.setdefault(site, len(self.sites))
        pltpu.make_async_copy(src, dst, self.sems.at[self.sites[site]]).wait()


def relay_kernel(seg_ref, x_hbm, cot_hbm, wqkv_hbm, wout_hbm, wup_hbm, wdn_hbm, g1, b1, bq, bv, bo, g2, b2, bu, bd,
                 out_o, gin_o, n1_o, st_o, mt_o, rl_o, n2_o, ul_o, hid_o, dl_o, ln_o, qkv_o, e_o, li_o, rs_o, gp_o,
                 wqkv, wout, wup, wdn, xs, dls, out2, gs, n1, qkv, vt, e_v, li, mt, rs, n2, gp, hid, ul, acc, u_v, s_v, rl, mlt, st, ds_v,
                 k2t_v, dot_v, ln, qc, kc, sem_i, sem_x, sem_o, sem_l, fs, fr, bs, br):
    sec = lax.axis_index("section")
    other = (1 - sec, lax.axis_index("dp"))
    micro, length, feats = xs.shape
    ff = hid.shape[1]
    heads = feats // HEAD_DIM
    half = length // 2
    quarter = length // 4
    chunks = ff // feats

    def remote(src, dst, s_sem, r_sem):
        return pltpu.make_async_remote_copy(
            src_ref=src, dst_ref=dst, send_sem=s_sem, recv_sem=r_sem, device_id=other, device_id_type=pl.DeviceIdType.MESH)

    def send_out(m, r):
        rows = pl.ds(r * half, half)
        return remote(out2.at[m, rows], xs.at[m, rows], fs.at[m, r], fr.at[m, r])

    def send_grad(m, r):
        rows = pl.ds(r * quarter, quarter)
        return remote(gs.at[m, rows], dls.at[m, rows], bs.at[m, r], br.at[m, r])

    def load_x(m):
        return pltpu.make_async_copy(x_hbm.at[m, 0], xs.at[m], sem_x.at[m])

    def load_cot(m):
        return pltpu.make_async_copy(cot_hbm.at[m, 0], dls.at[m], sem_x.at[m])

    barrier = pltpu.get_barrier_semaphore()
    pl.semaphore_signal(barrier, inc=1, device_id=other, device_id_type=pl.DeviceIdType.MESH)
    w_qkv, w_out, w_up, w_dn = [
        pltpu.make_async_copy(src.at[0], dst, sem_i.at[i])
        for i, (src, dst) in enumerate(((wqkv_hbm, wqkv), (wout_hbm, wout), (wup_hbm, wup), (wdn_hbm, wdn)))]

    @pl.when(sec == 0)
    def _():
        load_x(0).start()

    for c in (w_qkv, w_out, w_up, w_dn):
        c.start()

    @pl.when(sec == 0)
    def _():
        for m in range(1, micro):
            load_x(m).start()

    @pl.when(sec != 0)
    def _():
        for m in range(micro):
            load_cot(m).start()

    pl.semaphore_wait(barrier, 1)
    outs = Outs(sem_o)
    lows = half_masks(length)
    row_low = (lax.broadcasted_iota(jnp.int32, (128, length), 0) < HEAD_DIM).astype(F32)
    row_lows = (row_low.astype(BF), (1.0 - row_low).astype(BF))

    @pl.loop(0, micro)
    def _(m):
        def before(*sites):
            @pl.when(m > 0)
            def _():
                for site, src, dst in sites:
                    outs.wait(site, src, dst)

        seg = jnp.broadcast_to(seg_ref[m], (128, length))
        row = lax.broadcasted_iota(jnp.int32, (128, length), 0) % HEAD_DIM
        kcode = (seg == row).astype(F32)
        qcode = jnp.where(row < 4, -FAR * (1.0 - kcode), 0.0)
        kc[...] = kcode.T.astype(BF)
        qc[...] = qcode.T.astype(BF)

        @pl.when(sec == 0)
        def _():
            load_x(m).wait()

        before(("n1", n1, n1_o.at[0]), ("qkv", qkv, qkv_o))
        for r in range(2):
            @pl.when(sec != 0)
            def _():
                send_out(m, r).wait_recv()

            @pl.loop(0, half // 128)
            def _(i):
                rows = pl.ds(pl.multiple_of(r * half + i * 128, 128), 128)
                xh, _ = normed(xs[m, rows, :].astype(F32))
                n1[rows, :] = (xh * g1[...].astype(F32) + b1[...].astype(F32)).astype(BF)

            if r == 0:
                @pl.when(m == 0)
                def _():
                    w_qkv.wait()
            rows = slice(r * half, (r + 1) * half)
            q = (nn(n1[rows, :], wqkv[:, :feats]) + bq[...].astype(F32)) * HEAD_DIM ** -0.5
            qkv[rows, :feats] = q.astype(BF)
            qkv[rows, feats:2 * feats] = nn(n1[rows, :], wqkv[:, feats:2 * feats]).astype(BF)
            v = nn(n1[rows, :], wqkv[:, 2 * feats:]) + bv[...].astype(F32)
            qkv[rows, 2 * feats:] = v.astype(BF)
            vt[:, rows] = v.T.astype(BF)
        outs.start("n1", n1, n1_o.at[m])
        before(("e", e_v, e_o), ("li", li, li_o), ("mt", mt, mt_o.at[0]))

        def score(i):
            p, h = divmod(i, 2)
            at = p * 128
            qa = qkv[:, at:at + 128] * lows[h] + qc[...] * lows[1 - h]
            ka = qkv[:, feats + at:feats + at + 128] * lows[h] + kc[...] * lows[1 - h]
            s_v[i % 2] = nt(ka, qa)

        def expo(i):
            scores = s_v[i % 2]
            e_v[i] = jnp.exp(scores - jnp.max(scores, axis=0, keepdims=True)).astype(BF)

        def mix(i):
            p, h = divmod(i, 2)
            at = p * 128
            ot = nn(vt[at:at + 128, :] * row_lows[h] + row_lows[1 - h], e_v[i])
            mine, ones = (slice(0, 64), slice(64, 65)) if h == 0 else (slice(64, 128), slice(0, 1))
            inv = 1.0 / ot[ones]
            li[i:i + 1, :] = inv
            mt[i * HEAD_DIM:(i + 1) * HEAD_DIM, :] = (ot[mine] * inv).astype(BF)

        for t in range(heads + 2):
            if t < heads:
                score(t)
            if 0 <= t - 2:
                mix(t - 2)
            if 0 <= t - 1 < heads:
                expo(t - 1)

        outs.start("mt", mt, mt_o.at[m])
        before(("rs", rs, rs_o), ("n2", n2, n2_o.at[0]))

        @pl.when(m == 0)
        def _():
            w_out.wait()

        rs[...] = xs[m].astype(F32) + tn(mt[...], wout[...]) + bo[...].astype(F32)

        @pl.loop(0, length // 128)
        def _(i):
            rows = pl.ds(pl.multiple_of(i * 128, 128), 128)
            xh, _ = normed(rs[rows, :])
            n2[rows, :] = (xh * g2[...].astype(F32) + b2[...].astype(F32)).astype(BF)

        outs.start("n2", n2, n2_o.at[m])
        before(("gp", gp, gp_o), ("hid", hid, hid_o.at[0]))

        @pl.when(m == 0)
        def _():
            w_up.wait()
            w_dn.wait()
            outs.start("qkv", qkv, qkv_o)
            outs.start("e", e_v, e_o)
            outs.start("li", li, li_o)
            outs.start("rs", rs, rs_o)

        tiles = [(r, j) for r in range(2) for j in range(chunks)]

        def place(t):
            r, j = tiles[t]
            return slice(r * half, (r + 1) * half), slice(j * feats, (j + 1) * feats)

        def up(t):
            rows, cols = place(t)
            u_v[t % 2] = nn(n2[rows, :], wup[:, cols])

        def act(t):
            rows, cols = place(t)
            h, g = gelu_pair(u_v[t % 2] + bu[:, cols].astype(F32))
            hid[rows, cols] = h.astype(BF)
            gp[rows, cols] = g.astype(BF)

        def down(t):
            rows, cols = place(t)
            term = nn(hid[rows, cols], wdn[cols, :])
            r, j = tiles[t]
            if j == 0:
                acc[rows, :] = rs[rows, :] + bd[...].astype(F32) + term
            elif j < chunks - 1:
                acc[rows, :] = acc[rows, :] + term
            else:
                out2[m, rows, :] = (acc[rows, :] + term).astype(BF)

                @pl.when(sec == 0)
                def _():
                    send_out(m, r).start()

        for t in range(len(tiles) + 2):
            if t < len(tiles):
                up(t)
            if 0 <= t - 2:
                down(t - 2)
            if 0 <= t - 1 < len(tiles):
                act(t - 1)

        before(("out", out2.at[0], out_o.at[0]))
        outs.start("out", out2.at[m], out_o.at[m])
        outs.start("hid", hid, hid_o.at[m])

        @pl.when(m == 0)
        def _():
            outs.start("gp", gp, gp_o)

    lane = lax.broadcasted_iota(jnp.int32, (length, 128), 1)
    ones = ((jnp.logical_and(lane >= 64, lane < 66)).astype(F32).astype(BF), (lane < 2).astype(F32).astype(BF))
    low_f = lane < HEAD_DIM
    fill = jnp.zeros((62, length), BF)
    gin_sites = [(f"gin{r}", rs.at[pl.ds(r * quarter, quarter)], gin_o.at[0, pl.ds(r * quarter, quarter)]) for r in range(4)]
    @pl.loop(0, micro)
    def _(step):
        m = micro - 1 - step

        def before(*sites):
            @pl.when(step > 0)
            def _():
                for site, src, dst in sites:
                    outs.wait(site, src, dst)

        loads = [pltpu.make_async_copy(a, b, sem_l.at[i]) for i, (a, b) in enumerate(
            ((gp_o, gp), (rs_o, rs), (mt_o.at[0], mt), (li_o, li), (qkv_o, qkv), (e_o, e_v)))]
        l_gp, l_rs, l_mt, l_li, l_qkv, l_e = loads

        def loaded(*copies):
            @pl.when(step > 0)
            def _():
                for c in copies:
                    c.wait()

        def fetch(*copies):
            @pl.when(step == 0)
            def _():
                for c in copies:
                    c.start()

        @pl.when(sec != 0)
        def _():
            load_cot(m).wait()

        loaded(l_gp)
        before(("ul", ul, ul_o.at[0]))
        for r in range(2):
            @pl.when(sec == 0)
            def _():
                send_grad(m, 2 * r).wait_recv()
                send_grad(m, 2 * r + 1).wait_recv()

            rows = slice(r * half, (r + 1) * half)
            for j in range(chunks):
                cols = slice(j * feats, (j + 1) * feats)
                ul[rows, cols] = (nt(dls[m, rows, :], wdn[cols, :]) * gp[rows, cols].astype(F32)).astype(BF)
        fetch(l_gp)
        before(*gin_sites)

        @pl.when(step > 0)
        def _():
            l_rs.start()

        acc[...] = nt(ul[...], wup[...])
        before(("dl", dls.at[0], dl_o.at[0]), ("rl", rl, rl_o.at[0]), ("ln", ln, ln_o.at[0]))
        outs.start("dl", dls.at[m], dl_o.at[m])
        outs.start("ul", ul, ul_o.at[m])
        loaded(l_rs)
        ln[...] = jnp.zeros_like(ln)

        @pl.loop(0, length // 128)
        def _(i):
            rows = pl.ds(pl.multiple_of(i * 128, 128), 128)
            cot = acc[rows, :]
            dx, gx = norm_back(rs[rows, :], g2[...].astype(F32), cot)
            ln[2:3, :] += jnp.sum(gx, axis=0, keepdims=True)
            ln[3:4, :] += jnp.sum(cot, axis=0, keepdims=True)
            res = dls[m, rows, :].astype(F32) + dx
            rs[rows, :] = res
            rl[rows, :] = res.astype(BF)

        outs.start("rl", rl, rl_o.at[m])
        mlt[...] = nt(wout[...], rl[...]).astype(BF)
        loaded(l_mt, l_li, l_qkv, l_e)
        before(("st", st, st_o.at[0]))
        keep = {}

        def probe(i):
            p, h = divmod(i, 2)
            at = p * 128
            if h == 0:
                k2t_v[p % 2] = qkv[:, feats + at:feats + at + 128].astype(F32).T.astype(BF)
                scale = jnp.concatenate([jnp.broadcast_to(li[i + g:i + g + 1, :], (64, length)) for g in (0, 1)], axis=0)
                dot_v[p % 2] = (mlt[at:at + 128, :].astype(F32) * scale).astype(BF)
            mine = dot_v[p % 2, 64 * h:64 * h + 64, :]
            delta = -jnp.sum(mine.astype(F32) * mt[i * 64:(i + 1) * 64, :].astype(F32), axis=0, keepdims=True)
            d_hi = delta.astype(BF)
            d_lo = (delta - d_hi.astype(F32)).astype(BF)
            extra = jnp.concatenate([d_hi, d_lo, fill], axis=0)
            da = jnp.concatenate((mine, extra) if h == 0 else (extra, mine), axis=0)
            va = qkv[:, 2 * feats + at:2 * feats + at + 128] * lows[h] + ones[h]
            s_v[i % 2] = nn(va, da)

        def scale_back(i):
            ds_v[i % 2] = (e_v[i].astype(F32) * s_v[i % 2]).astype(BF)

        def spread(i):
            p, h = divmod(i, 2)
            at = p * 128
            ds = ds_v[i % 2]
            dv = nt(e_v[i], dot_v[p % 2])
            dk = nn(ds, qkv[:, at:at + 128])
            dq = nn(k2t_v[p % 2], ds)[64 * h:64 * h + 64]
            if h == 0:
                keep[p] = (dv, dk, dq)
                return
            first = keep.pop(p)
            st[:, 2 * feats + at:2 * feats + at + 128] = jnp.where(low_f, first[0], dv).astype(BF)
            st[:, feats + at:feats + at + 128] = jnp.where(low_f, first[1], dk).astype(BF)
            q = jnp.concatenate([first[2], dq], axis=0).astype(BF).astype(F32) * HEAD_DIM ** -0.5
            st[:, at:at + 128] = q.T.astype(BF)

        for t in range(heads + 1):
            if t < heads:
                probe(t)
            if 0 <= t - 1:
                scale_back(t - 1)
                spread(t - 1)

        outs.start("st", st, st_o.at[m])

        @pl.when(step == 0)
        def _():
            outs.wait("mt", mt, mt_o.at[0])

        fetch(l_mt, l_li, l_qkv, l_e)
        for r in range(4):
            rows = slice(r * quarter, (r + 1) * quarter)
            cot = nt(st[rows, :], wqkv[...])
            dx, gx = norm_back(xs[m, rows, :].astype(F32), g1[...].astype(F32), cot)
            ln[0:1, :] += jnp.sum(gx, axis=0, keepdims=True)
            ln[1:2, :] += jnp.sum(cot, axis=0, keepdims=True)
            res = rs[rows, :] + dx
            rs[rows, :] = res
            gs[m, rows, :] = res.astype(BF)

            @pl.when(sec != 0)
            def _():
                send_grad(m, r).start()

            outs.start(f"gin{r}", rs.at[rows], gin_o.at[m, rows])

        outs.start("ln", ln, ln_o.at[m])

    for site, src, dst in (("dl", dls.at[0], dl_o.at[0]), ("rl", rl, rl_o.at[0]), ("ln", ln, ln_o.at[0]), ("st", st, st_o.at[0]),
                           *gin_sites, ("ul", ul, ul_o.at[0]), ("n1", n1, n1_o.at[0]), ("n2", n2, n2_o.at[0]),
                           ("hid", hid, hid_o.at[0]), ("out", out2.at[0], out_o.at[0])):
        outs.wait(site, src, dst)

    @pl.when(sec == 0)
    def _():
        for m in range(micro):
            for r in range(2):
                send_out(m, r).wait_send()

    @pl.when(sec != 0)
    def _():
        for m in range(micro):
            for r in range(4):
                send_grad(m, r).wait_send()


def relay(seg, x, cot, weights, vecs):
    micro, _, length, feats = x.shape
    ff = weights[2].shape[2]
    heads = feats // HEAD_DIM
    sds = jax.ShapeDtypeStruct

    def vmem(dtype, *shape):
        return pltpu.VMEM(shape, dtype)

    outs = [
        sds((micro, length, feats), BF),
        sds((micro, length, feats), F32),
        sds((micro, length, feats), BF),
        sds((micro, length, 3 * feats), BF),
        sds((micro, feats, length), BF),
        sds((micro, length, feats), BF),
        sds((micro, length, feats), BF),
        sds((micro, length, ff), BF),
        sds((micro, length, ff), BF),
        sds((micro, length, feats), BF),
        sds((micro, 8, feats), F32),
        sds((length, 3 * feats), BF),
        sds((heads, length, length), BF),
        sds((16, length), F32),
        sds((length, feats), F32),
        sds((length, ff), BF),
    ]
    dma = pltpu.SemaphoreType.DMA
    return pl.pallas_call(
        relay_kernel,
        out_shape=outs,
        in_specs=[VM] + [ANY] * 6 + [VM] * 9,
        out_specs=[ANY] * len(outs),
        scratch_shapes=[
            vmem(BF, feats, 3 * feats), vmem(BF, feats, feats), vmem(BF, feats, ff), vmem(BF, ff, feats),
            vmem(BF, micro, length, feats), vmem(BF, micro, length, feats), vmem(BF, micro, length, feats), vmem(BF, micro, length, feats),
            vmem(BF, length, feats), vmem(BF, length, 3 * feats), vmem(BF, feats, length), vmem(BF, heads, length, length),
            vmem(F32, 16, length), vmem(BF, feats, length), vmem(F32, length, feats), vmem(BF, length, feats),
            vmem(BF, length, ff), vmem(BF, length, ff), vmem(BF, length, ff), vmem(F32, length, feats), vmem(F32, 2, length // 2, feats),
            vmem(F32, 2, length, length), vmem(BF, length, feats), vmem(BF, feats, length), vmem(BF, length, 3 * feats),
            vmem(BF, 2, length, length), vmem(BF, 2, 128, length), vmem(BF, 2, 128, length), vmem(F32, 8, feats),
            vmem(BF, length, 128), vmem(BF, length, 128),
            dma((4,)), dma((micro,)), dma((20,)), dma((6,)),
            dma((micro, 2)), dma((micro, 2)), dma((micro, 4)), dma((micro, 4)),
        ],
        compiler_params=pltpu.CompilerParams(vmem_limit_bytes=VMEM_LIMIT, collective_id=1, has_side_effects=True),
        name="layer_relay",
    )(seg, x, cot, *weights, *vecs)


INNER = 16
MASKS = (1, 2, 4, 8)
LAG = dict(s1=1, s2=3, line1=4, line2=2, end2=7, ag1=7, age=7, agy2=9, core=12, done=14)


def exchange_kernel(group, n1_hbm, st_hbm, mt_hbm, rl_hbm, n2_hbm, ul_hbm, hid_hbm, dl_hbm, ln_ref, g_o, small_o, xb,
                    a_v, b_v, mt_v, own, sb0, rb0, sby, rby, line1, line2, sbe, rbe, gath, xv, small, rsm, xsm,
                    ld_sem, out_sem, cs, cr, ys, yr, ls, lr, es, er, as_, ar, ms, mr, xs, xr, xl):
    sec = lax.axis_index("section")
    me = lax.axis_index("dp")
    size = gath.shape[1]
    half, wide, q4, q8 = size // 2, size // 2, size // 4, size // 8
    outer = group // INNER
    kq, ku, kd = st_hbm.shape[2] // size, ul_hbm.shape[2] // size, hid_hbm.shape[2] // size
    kinds = (("down", 0, kd), ("up", kd, kd + ku), ("out", kd + ku, kd + ku + 1), ("qkv", kd + ku + 1, kd + ku + 1 + kq))
    count = kinds[-1][2]
    core, y, z = me % 2, (me // 2) % 2, (me // 4) % 4
    left, right = slice(0, wide), slice(wide, size)

    def to(device):
        return dict(device_id=(sec, device), device_id_type=pl.DeviceIdType.MESH)

    def peer(mask):
        return me + mask - 2 * mask * ((me // mask) % 2)

    def outer_peer(k):
        return (me + k * INNER) % group

    barrier = pltpu.get_barrier_semaphore()
    at_end = jnp.logical_or(z == 0, z == 3)
    for mask in MASKS:
        pl.semaphore_signal(barrier, inc=1, **to(peer(mask)))
    for k in range(1, outer):
        pl.semaphore_signal(barrier, inc=1, **to(outer_peer(k)))

    pl.semaphore_signal(barrier, inc=1, **to(me + 12 - 8 * z))

    def remote(src, dst, s_sem, r_sem, device):
        return pltpu.make_async_remote_copy(src_ref=src, dst_ref=dst, send_sem=s_sem, recv_sem=r_sem, **to(device))

    def rows_of(first, rows):
        return pl.ds(pl.multiple_of(first, 16), rows)

    def by_kind(u, fn):
        for kind, low, high in kinds:
            @pl.when(jnp.logical_and(u >= low, u < high))
            def _():
                fn(kind, u - low)

    def block(ref, j, axis):
        cols = pl.ds(pl.multiple_of(j * size, size), size)
        return ref.at[:, :, cols] if axis == 2 else ref.at[:, cols] if axis == 1 else ref.at[cols, :]

    def loads(u):
        def pair(kind, j, act):
            slot = u % 2
            src_a, src_b = {
                "down": lambda: (block(hid_hbm, j, 2), dl_hbm),
                "up": lambda: (n2_hbm, block(ul_hbm, j, 2)),
                "out": lambda: (mt_hbm, rl_hbm),
                "qkv": lambda: (n1_hbm, block(st_hbm, j, 2)),
            }[kind]()
            dst_a = mt_v if kind == "out" else a_v.at[slot]
            act(pltpu.make_async_copy(src_a, dst_a, ld_sem.at[slot, 0]))
            act(pltpu.make_async_copy(src_b, b_v.at[slot], ld_sem.at[slot, 1]))
        return pair

    def start_loads(u):
        by_kind(u, lambda kind, j: loads(u)(kind, j, lambda c: c.start()))

    def core_copy(u):
        return remote(sb0.at[u % 2], rb0.at[u], cs.at[u], cr.at[u], peer(1))

    def y_copy(u):
        return remote(sby.at[u], rby.at[u], ys.at[u], yr.at[u], peer(2))

    def end_copy(u):
        return remote(sbe.at[u], rbe.at[u], es.at[u], er.at[u], peer(2))

    def line_copy(u, part, up):
        ref = line1 if part == 0 else line2
        at = (u, int(up))
        sem = (u, 2 * part + int(up))
        return remote(ref.at[at], ref.at[at], ls.at[sem], lr.at[sem], me + 4 if up else me - 4)

    def compute(u):
        slot = u % 2
        by_kind(u, lambda kind, j: loads(u)(kind, j, lambda c: c.wait()))
        start_loads(u + 1)

        def column():
            return jnp.sum(jnp.sum(b_v[slot].astype(F32), axis=0), axis=0, keepdims=True)

        def products(transposed):
            def product(which):
                cols = pl.ds(pl.multiple_of(which * half, half), half)
                if transposed:
                    total = None
                    for k in range(mt_v.shape[0]):
                        term = nn(mt_v[k, cols, :], b_v[slot, k])
                        total = term if total is None else total + term
                    return total
                value = a_v[slot, :, :, cols]
                tokens = value.shape[0] * value.shape[1]
                return tn(value.reshape(tokens, half), b_v[slot].reshape(tokens, size))

            sb0[slot] = product(1 - core).astype(BF)
            core_copy(u).start()
            own[u % own.shape[0]] = product(core)

        low, high = kinds[2][1], kinds[2][2]
        is_out = jnp.logical_and(u >= low, u < high)

        @pl.when(is_out)
        def _():
            products(True)
            small[5:6, :] = column()

        @pl.when(jnp.logical_not(is_out))
        def _():
            products(False)

        @pl.when(u == 0)
        def _():
            small[4:5, :] = column()

        for j in range(ku):
            @pl.when(u == kinds[1][1] + j)
            def _():
                small[8 + j:9 + j, :] = column()

        for j, at in ((0, 6), (kq - 1, 7)):
            @pl.when(u == kinds[3][1] + j)
            def _():
                small[at:at + 1, :] = column()

    def add_core(u):
        core_copy(u).wait()
        ref = own.at[u % own.shape[0]]
        ref[...] = ref[...] + rb0[u].astype(F32)
        sby[u] = ref[rows_of((1 - y) * q4, q4), left].astype(BF)
        y_copy(u).start()

    def add_y(u):
        y_copy(u).wait()
        ref = own.at[u % own.shape[0]]
        rows = rows_of(y * q4, q4)
        ref[rows, left] = ref[rows, left] + rby[u].astype(F32)

    def along(u, part, up):
        buf = line1 if part == 0 else line2
        ref = own.at[u % own.shape[0]]
        place = z if up else 3 - z
        if part == 0:
            rows, cols = rows_of(y * q4 + (q8 if up else 0), q8), left
        else:
            rows, cols = rows_of(q4 if up else 0, q4), right

        @pl.when(place == 0)
        def _():
            buf[u, int(up)] = ref[rows, cols].astype(BF)

        @pl.when(place > 0)
        def _():
            line_copy(u, part, up).wait_recv()
            total = ref[rows, cols] + buf[u, int(up)].astype(F32)
            ref[rows, cols] = total

            @pl.when(place < 3)
            def _():
                buf[u, int(up)] = total.astype(BF)

        @pl.when(place < 3)
        def _():
            line_copy(u, part, up).start()

        @pl.when(place == 3)
        def _():
            if part == 0:
                rows_up = rows_of(core * half + y * q4 + (q8 if up else 0), q8)
                gath[u, rows_up, left] = over_outer(u, 0, ref[rows, cols]).astype(BF)
            else:
                first = q4 if up else 0
                sbe[u] = ref[rows_of(first + (1 - y) * q8, q8), right].astype(BF)
                end_copy(u).start()

    def over_outer(u, part, total):
        if outer == 1:
            return total
        at = 2 * u + part
        xv[0] = total.astype(BF)
        own_slot = pltpu.make_async_copy(xv.at[0], xb.at[at, 0], xl.at[0])
        own_slot.start()
        copies = [remote(xv.at[0], xb.at[at, k], xs.at[at, k], xr.at[at, k], outer_peer(k)) for k in range(1, outer)]
        for c in copies:
            c.start()
        own_slot.wait()
        for c in copies:
            c.wait()
        back = pltpu.make_async_copy(xb.at[at], xv, xl.at[1])
        back.start()
        back.wait()
        result = None
        for k in range(outer):
            term = xv[(me // INNER - k + outer) % outer].astype(F32)
            result = term if result is None else result + term
        return result

    def part_of(u, part, up):
        if part == 0:
            return gath.at[u, rows_of(core * half + y * q4 + (q8 if up else 0), q8), left]
        return gath.at[u, rows_of(core * half + (q4 if up else 0), q4), right]

    def gather_line(u, part, up):
        ref = part_of(u, part, up)
        sem = (u, 2 * part + int(up))
        return remote(ref, ref, as_.at[sem], ar.at[sem], me - 4 if up else me + 4)

    def gather_y(u, up):
        ref = part_of(u, 0, up)
        sem = (u, 4 + int(up))
        return remote(ref, ref, as_.at[sem], ar.at[sem], peer(2))

    def gather_end(u):
        ref = gath.at[u, rows_of(core * half + (z // 3) * q4 + y * q8, q8), right]
        sem = (u, 6)
        return remote(ref, ref, as_.at[sem], ar.at[sem], peer(2))

    def gather_core(u):
        ref = gath.at[u, rows_of(core * half, half), :]
        sem = (u, 7)
        return remote(ref, ref, as_.at[sem], ar.at[sem], peer(1))

    def finish_end(u):
        @pl.when(at_end)
        def _():
            end_copy(u).wait()
            ref = own.at[u % own.shape[0]]
            total = ref[rows_of((z // 3) * q4 + y * q8, q8), right] + rbe[u].astype(F32)
            gath[u, rows_of(core * half + (z // 3) * q4 + y * q8, q8), right] = over_outer(u, 1, total).astype(BF)

    def end_sent(u):
        @pl.when(at_end)
        def _():
            gather_end(u).start()

    def ends_joined(u):
        @pl.when(at_end)
        def _():
            gather_end(u).wait()

    def back_along(u, part, up):
        place = 3 - z if up else z

        @pl.when(place > 0)
        def _():
            gather_line(u, part, up).wait_recv()

        @pl.when(place < 3)
        def _():
            gather_line(u, part, up).start()

        if part == 0:
            gather_y(u, up).start()

    def to_core(u):
        gather_y(u, False).wait()
        gather_y(u, True).wait()
        gather_core(u).start()

    def out_copy(u):
        return pltpu.make_async_copy(gath.at[u], g_o.at[u], out_sem.at[u])

    def done(u):
        gather_core(u).wait()
        out_copy(u).start()

    def small_copy(stage):
        return remote(small, rsm.at[stage], ms.at[stage], mr.at[stage], peer(MASKS[stage]))

    def small_step(stage):
        small_copy(stage).wait()
        small[...] = small[...] + rsm[stage]
        if stage < 3:
            small_copy(stage + 1).start()
            return
        if outer > 1:
            xsm[0] = small[...]
            copies = [remote(xsm.at[0], xsm.at[k], xs.at[2 * count, k], xr.at[2 * count, k], outer_peer(k)) for k in range(1, outer)]
            for c in copies:
                c.start()
            for c in copies:
                c.wait()
            total = None
            for k in range(outer):
                term = xsm[(me // INNER - k + outer) % outer]
                total = term if total is None else total + term
            small[...] = total
        small_o[...] = small[...]

    start_loads(0)
    small[...] = jnp.zeros_like(small)
    small[0:4, :] = jnp.sum(ln_ref[...], axis=0)[0:4, :]
    pl.semaphore_wait(barrier, len(MASKS) + outer)

    @pl.loop(0, count + LAG["done"])
    def _(tau):
        def at(lag, fn):
            u = tau - lag

            @pl.when(jnp.logical_and(u >= 0, u < count))
            def _():
                fn(u)

        at(LAG["done"], done)
        at(LAG["agy2"], ends_joined)
        at(LAG["s1"], add_core)
        for up in (True, False):
            place = z if up else 3 - z
            at(LAG["line2"] + place, lambda u: along(u, 1, up))
            at(LAG["agy2"] + 3 - place, lambda u: back_along(u, 1, up))
        at(LAG["s2"], add_y)
        for up in (True, False):
            place = z if up else 3 - z
            at(LAG["line1"] + place, lambda u: along(u, 0, up))
        at(LAG["end2"], finish_end)
        at(LAG["age"], end_sent)
        for up in (True, False):
            place = z if up else 3 - z
            at(LAG["ag1"] + 3 - place, lambda u: back_along(u, 0, up))
        at(LAG["core"], to_core)
        at(0, compute)

        @pl.when(tau == count)
        def _():
            small_copy(0).start()

        for stage in range(4):
            @pl.when(tau == count + 2 + 2 * stage)
            def _():
                small_step(stage)

    @pl.loop(0, count)
    def _(u):
        out_copy(u).wait()
        for up in (True, False):
            place = z if up else 3 - z

            @pl.when(place < 3)
            def _():
                for part in (0, 1):
                    line_copy(u, part, up).wait_send()

            @pl.when(place > 0)
            def _():
                for part in (0, 1):
                    gather_line(u, part, up).wait_send()


def exchange(group, n1, st, mt, rl, n2, ul, hid, dl, ln):
    micro, length, feats = n1.shape
    ff = ul.shape[2]
    outer = group // INNER
    count = st.shape[2] // feats + 2 * (ff // feats) + 1
    half, q4, q8 = feats // 2, feats // 4, feats // 8
    sds = jax.ShapeDtypeStruct

    def vmem(dtype, *shape):
        return pltpu.VMEM(shape, dtype)

    dma = pltpu.SemaphoreType.DMA
    return pl.pallas_call(
        functools.partial(exchange_kernel, group),
        out_shape=[sds((count, feats, feats), BF), sds((16, feats), F32),
                   sds((2 * count, outer, q8, half) if outer > 1 else (16, 128), BF)],
        in_specs=[ANY] * 8 + [VM],
        out_specs=[ANY, VM, ANY],
        scratch_shapes=[
            vmem(BF, 2, micro, length, feats),
            vmem(BF, 2, micro, length, feats),
            vmem(BF, micro, feats, length),
            vmem(F32, 8, half, feats),
            vmem(BF, 2, half, feats),
            vmem(BF, count, half, feats),
            vmem(BF, count, q4, half),
            vmem(BF, count, q4, half),
            vmem(BF, count, 2, q8, half),
            vmem(BF, count, 2, q4, half),
            vmem(BF, count, q8, half),
            vmem(BF, count, q8, half),
            vmem(BF, count, feats, feats),
            vmem(BF, outer, q8, half),
            vmem(F32, 16, feats),
            vmem(F32, 4, 16, feats),
            vmem(F32, outer, 16, feats),
            dma((2, 2)),
            dma((count,)),
            dma((count,)), dma((count,)),
            dma((count,)), dma((count,)),
            dma((count, 4)), dma((count, 4)),
            dma((count,)), dma((count,)),
            dma((count, 8)), dma((count, 8)),
            dma((4,)), dma((4,)),
            dma((2 * count + 1, outer)), dma((2 * count + 1, outer)),
            dma((2,)),
        ],
        compiler_params=pltpu.CompilerParams(vmem_limit_bytes=VMEM_LIMIT, collective_id=0, has_side_effects=True),
        name="grad_exchange",
    )(n1, st, mt, rl, n2, ul, hid, dl, ln)[:2]


def finish_kernel(g, small_hbm, block_hbm, gin_hbm, block_o, gin_o, g1_o, s1_o, gq_o, bq_o, bv_o, go_o, bo_o, g2_o, s2_o, gu_o, bu_o, gd_o, bd_o,
                  narrow, stage, small, block, gin, sem_g, sem, sem_b):
    size = g.shape[1]
    loads = [pltpu.make_async_copy(g.at[u], narrow.at[u], sem_g.at[u]) for u in range(g.shape[0])]
    for c in loads:
        c.start()
    load_small = pltpu.make_async_copy(small_hbm, small, sem_b.at[4])
    passing = [pltpu.make_async_copy(block_hbm, block, sem_b.at[0]), pltpu.make_async_copy(gin_hbm, gin, sem_b.at[1])]
    copies = [pltpu.make_async_copy(block, block_o.at[0, :, 0], sem_b.at[2]), pltpu.make_async_copy(gin, gin_o.at[0, :, 0], sem_b.at[3])]
    for c in passing + [load_small]:
        c.start()
    places = [gd_o.at[0, pl.ds(j * size, size), :] for j in range(gd_o.shape[1] // size)]
    for ref in (gu_o, go_o, gq_o):
        places += [ref.at[0, :, pl.ds(j * size, size)] for j in range(ref.shape[2] // size)]
    slots = stage.shape[0]
    running = []
    for u, place in enumerate(places):
        if u >= slots:
            running[u - slots].wait()
        loads[u].wait()
        stage[u % slots] = narrow[u].astype(F32)
        c = pltpu.make_async_copy(stage.at[u % slots], place, sem.at[u])
        c.start()
        running.append(c)
        if u == slots - 1:
            for load, store in zip(passing, copies):
                load.wait()
                store.start()
    load_small.wait()
    for ref, at in ((g1_o, 0), (s1_o, 1), (g2_o, 2), (s2_o, 3), (bd_o, 4), (bo_o, 5), (bq_o, 6), (bv_o, 7)):
        ref[...] = small[at:at + 1, :]
    for j in range(bu_o.shape[1] // size):
        bu_o[:, j * size:(j + 1) * size] = small[8 + j:9 + j, :]
    for c in running[-slots:] + copies:
        c.wait()


def finish(g, small, block_out, gin, ff):
    count, feats, _ = g.shape
    micro, length, _ = block_out.shape
    sds = jax.ShapeDtypeStruct
    vec = sds((1, feats), F32)
    outs = [sds((1, micro, 1, length, feats), BF), sds((1, micro, 1, length, feats), F32), vec, vec, sds((1, feats, 3 * feats), F32), vec, vec,
            sds((1, feats, feats), F32), vec, vec, vec, sds((1, feats, ff), F32), sds((1, ff), F32), sds((1, ff, feats), F32), vec]
    return pl.pallas_call(
        finish_kernel,
        out_shape=outs,
        in_specs=[HBM] * 4,
        out_specs=[ANY if len(o.shape) > 2 else VM for o in outs],
        scratch_shapes=[pltpu.VMEM((count, feats, feats), BF), pltpu.VMEM((4, feats, feats), F32), pltpu.VMEM((16, feats), F32),
                        pltpu.VMEM(block_out.shape, BF), pltpu.VMEM(gin.shape, F32), pltpu.SemaphoreType.DMA((count,)),
                        pltpu.SemaphoreType.DMA((count,)), pltpu.SemaphoreType.DMA((5,))],
        compiler_params=pltpu.CompilerParams(vmem_limit_bytes=40 * 2**20),
        name="finish",
    )(*[pltpu.with_memory_space_constraint(v, pltpu.HBM) for v in (g, small, block_out, gin)])


def per_device(inputs, cotangent, segments, norm1_gain, norm1_shift, w_qkv, bias_query, bias_value, w_out, bias_out,
               norm2_gain, norm2_shift, w_up, bias_up, w_down, bias_down):
    weights = (w_qkv, w_out, w_up, w_down)
    vecs = (norm1_gain, norm1_shift, bias_query, bias_value, bias_out, norm2_gain, norm2_shift, bias_up, bias_down)
    block_out, gin, n1, st, mt, rl, n2, ul, hid, dl, ln = relay(segments, inputs, cotangent, weights, vecs)[:11]
    g, small = exchange(lax.axis_size("dp"), n1, st, mt, rl, n2, ul, hid, dl, ln)
    return tuple(finish(g, small, block_out, gin, w_up.shape[2]))


def solution(mesh):
    data, seg, vec, mat = P(None, "dp", None, None), P(None, "dp", None), P("section", None), P("section", None, None)
    act = P("section", None, "dp", None, None)
    in_specs = (data, data, seg, vec, vec, mat, vec, vec, mat, vec, vec, vec, mat, vec, mat, vec)
    out_specs = (act, act, vec, vec, mat, vec, vec, mat, vec, vec, vec, mat, vec, mat, vec)
    return jax.shard_map(per_device, mesh=mesh, in_specs=in_specs, out_specs=out_specs, check_vma=False)
```

```python
import functools
import math

import jax
import jax.numpy as jnp
from jax import lax
from jax.experimental import pallas as pl
from jax.experimental.pallas import tpu as pltpu
from jax.sharding import PartitionSpec as P

HEAD_DIM = 64
GROUP = 6
BF = jnp.bfloat16
F32 = jnp.float32
FAR = float(2**30)
VMEM_LIMIT = 60 * 2**20
ANY = pl.BlockSpec(memory_space=pl.ANY)
VM = pl.BlockSpec(memory_space=pltpu.VMEM)
HBM = pl.BlockSpec(memory_space=pltpu.HBM)


def nn(left, right):
    return lax.dot_general(left, right, (((1,), (0,)), ((), ())), preferred_element_type=F32)


def nt(left, right):
    return lax.dot_general(left, right, (((1,), (1,)), ((), ())), preferred_element_type=F32)


def tn(left, right):
    return lax.dot_general(left, right, (((0,), (0,)), ((), ())), preferred_element_type=F32)


def gelu_pair(u):
    d = 1.0 + (0.3275911 / math.sqrt(2.0)) * jnp.abs(u)
    t = pl.reciprocal(d, approx=True)
    t = t * (2.0 - d * t)
    e = jnp.exp(u * u * -0.5)
    poly = 0.5 * 1.061405429
    for c in (-1.453152027, 1.421413741, -0.284496736, 0.254829592):
        poly = poly * t + 0.5 * c
    tail = poly * t * e
    cdf = jnp.where(u >= 0, 1.0 - tail, tail)
    return u * cdf, cdf + u * (e * (1.0 / math.sqrt(2.0 * math.pi)))


def normed(x):
    centred = x - jnp.mean(x, axis=-1, keepdims=True)
    rstd = lax.rsqrt(jnp.mean(centred * centred, axis=-1, keepdims=True) + 1e-06)
    return centred * rstd, rstd


def norm_back(x, gain, cot):
    xh, rstd = normed(x)
    dy = cot * gain
    m1 = jnp.mean(dy, axis=-1, keepdims=True)
    m2 = jnp.mean(dy * xh, axis=-1, keepdims=True)
    return rstd * (dy - m1 - xh * m2), cot * xh


def half_masks(length):
    lane = lax.broadcasted_iota(jnp.int32, (length, 128), 1)
    low = (lane < HEAD_DIM).astype(F32)
    return low.astype(BF), (1.0 - low).astype(BF)


class Outs:
    def __init__(self, sems):
        self.sems = sems
        self.sites = {}

    def start(self, site, src, dst):
        self.sites.setdefault(site, len(self.sites))
        copy = pltpu.make_async_copy(src, dst, self.sems.at[self.sites[site]])
        copy.start()

    def wait(self, site, src, dst):
        self.sites.setdefault(site, len(self.sites))
        pltpu.make_async_copy(src, dst, self.sems.at[self.sites[site]]).wait()


def relay_kernel(seg_ref, x_hbm, cot_hbm, wqkv_hbm, wout_hbm, wup_hbm, wdn_hbm, g1, b1, bq, bv, bo, g2, b2, bu, bd,
                 out_o, gin_o, n1_o, st_o, mt_o, rl_o, n2_o, ul_o, hid_o, dl_o, ln_o, qkv_o, e_o, li_o, rs_o, gp_o,
                 wqkv, wout, wup, wdn, xs, dls, out2, gs, n1, qkv, vt, e_v, li, mt, rs, n2, gp, hid, ul, acc, u_v, s_v, rl, mlt, st, ds_v,
                 k2t_v, dot_v, ln, qc, kc, sem_i, sem_x, sem_o, sem_l, sem_g, fs, fr, bs, br):
    sec = lax.axis_index("section")
    other = (1 - sec, lax.axis_index("dp"))
    micro, length, feats = xs.shape
    ff = hid.shape[1]
    heads = feats // HEAD_DIM
    half = length // 2
    quarter = length // 4
    chunks = ff // feats

    def remote(src, dst, s_sem, r_sem):
        return pltpu.make_async_remote_copy(
            src_ref=src, dst_ref=dst, send_sem=s_sem, recv_sem=r_sem, device_id=other, device_id_type=pl.DeviceIdType.MESH)

    def part(r, size):
        return pl.ds(r * size if isinstance(r, int) else pl.multiple_of(r * size, size), size)

    def send_out(m, r):
        rows = part(r, half)
        return remote(out2.at[m, rows], xs.at[m, rows], fs.at[m, r], fr.at[m, r])

    def send_grad(m, r):
        rows = part(r, quarter)
        return remote(gs.at[m, rows], dls.at[m, rows], bs.at[m, r], br.at[m, r])

    def load_x(m):
        return pltpu.make_async_copy(x_hbm.at[m, 0], xs.at[m], sem_x.at[m])

    def load_cot(m):
        return pltpu.make_async_copy(cot_hbm.at[m, 0], dls.at[m], sem_x.at[m])

    barrier = pltpu.get_barrier_semaphore()
    pl.semaphore_signal(barrier, inc=1, device_id=other, device_id_type=pl.DeviceIdType.MESH)
    w_qkv, w_out, w_up, w_dn = [
        pltpu.make_async_copy(src.at[0], dst, sem_i.at[i])
        for i, (src, dst) in enumerate(((wqkv_hbm, wqkv), (wout_hbm, wout), (wup_hbm, wup), (wdn_hbm, wdn)))]

    @pl.when(sec == 0)
    def _():
        load_x(0).start()

    for c in (w_qkv, w_out, w_up, w_dn):
        c.start()

    @pl.when(sec == 0)
    def _():
        for m in range(1, micro):
            load_x(m).start()

    @pl.when(sec != 0)
    def _():
        for m in range(micro):
            load_cot(m).start()

    pl.semaphore_wait(barrier, 1)
    outs = Outs(sem_o)
    lows = half_masks(length)
    row_low = (lax.broadcasted_iota(jnp.int32, (128, length), 0) < HEAD_DIM).astype(F32)
    row_lows = (row_low.astype(BF), (1.0 - row_low).astype(BF))

    @pl.loop(0, micro)
    def _(m):
        def before(*sites):
            @pl.when(m > 0)
            def _():
                for site, src, dst in sites:
                    outs.wait(site, src, dst)

        seg = jnp.broadcast_to(seg_ref[m], (128, length))
        row = lax.broadcasted_iota(jnp.int32, (128, length), 0) % HEAD_DIM
        kcode = (seg == row).astype(F32)
        qcode = jnp.where(row < 4, -FAR * (1.0 - kcode), 0.0)
        kc[...] = kcode.T.astype(BF)
        qc[...] = qcode.T.astype(BF)

        @pl.when(sec == 0)
        def _():
            load_x(m).wait()

        before(("n1", n1, n1_o.at[0]), ("qkv", qkv, qkv_o))
        @pl.loop(0, 2)
        def _(r):
            @pl.when(sec != 0)
            def _():
                send_out(m, r).wait_recv()

            @pl.loop(0, half // 128)
            def _(i):
                rows = pl.ds(pl.multiple_of(r * half + i * 128, 128), 128)
                xh, _ = normed(xs[m, rows, :].astype(F32))
                n1[rows, :] = (xh * g1[...].astype(F32) + b1[...].astype(F32)).astype(BF)

            @pl.when(jnp.logical_and(m == 0, r == 0))
            def _():
                w_qkv.wait()

            rows = part(r, half)
            q = (nn(n1[rows, :], wqkv[:, :feats]) + bq[...].astype(F32)) * HEAD_DIM ** -0.5
            qkv[rows, :feats] = q.astype(BF)
            qkv[rows, feats:2 * feats] = nn(n1[rows, :], wqkv[:, feats:2 * feats]).astype(BF)
            v = nn(n1[rows, :], wqkv[:, 2 * feats:]) + bv[...].astype(F32)
            qkv[rows, 2 * feats:] = v.astype(BF)
            vt[:, rows] = v.T.astype(BF)

        outs.start("n1", n1, n1_o.at[m])
        before(("e", e_v, e_o), ("li", li, li_o), ("mt", mt, mt_o.at[0]))

        @pl.loop(0, heads // GROUP)
        def _(group):
            def spot(i):
                return group * GROUP + i, pl.multiple_of((group * (GROUP // 2) + i // 2) * 128, 128), i % 2

            def score(i):
                _, at, h = spot(i)
                qa = qkv[:, pl.ds(at, 128)] * lows[h] + qc[...] * lows[1 - h]
                ka = qkv[:, pl.ds(feats + at, 128)] * lows[h] + kc[...] * lows[1 - h]
                s_v[i % 2] = nt(ka, qa)

            def expo(i):
                scores = s_v[i % 2]
                e_v[spot(i)[0]] = jnp.exp(scores - jnp.max(scores, axis=0, keepdims=True)).astype(BF)

            def mix(i):
                head, at, h = spot(i)
                ot = nn(vt[pl.ds(at, 128), :] * row_lows[h] + row_lows[1 - h], e_v[head])
                mine, ones = (slice(0, 64), slice(64, 65)) if h == 0 else (slice(64, 128), slice(0, 1))
                inv = 1.0 / ot[ones]
                li[pl.ds(head, 1), :] = inv
                mt[pl.ds(pl.multiple_of(head * HEAD_DIM, HEAD_DIM), HEAD_DIM), :] = (ot[mine] * inv).astype(BF)

            for t in range(GROUP + 2):
                if t < GROUP:
                    score(t)
                if 0 <= t - 2:
                    mix(t - 2)
                if 0 <= t - 1 < GROUP:
                    expo(t - 1)

        outs.start("mt", mt, mt_o.at[m])
        before(("rs", rs, rs_o), ("n2", n2, n2_o.at[0]))

        @pl.when(m == 0)
        def _():
            w_out.wait()

        rs[...] = xs[m].astype(F32) + tn(mt[...], wout[...]) + bo[...].astype(F32)

        @pl.loop(0, length // 128)
        def _(i):
            rows = pl.ds(pl.multiple_of(i * 128, 128), 128)
            xh, _ = normed(rs[rows, :])
            n2[rows, :] = (xh * g2[...].astype(F32) + b2[...].astype(F32)).astype(BF)

        outs.start("n2", n2, n2_o.at[m])
        before(("gp", gp, gp_o), ("hid", hid, hid_o.at[0]))

        @pl.when(m == 0)
        def _():
            w_up.wait()
            w_dn.wait()
            outs.start("qkv", qkv, qkv_o)
            outs.start("e", e_v, e_o)
            outs.start("li", li, li_o)
            outs.start("rs", rs, rs_o)

        tiles = [(r, j) for r in range(2) for j in range(chunks)]

        def place(t):
            r, j = tiles[t]
            return slice(r * half, (r + 1) * half), slice(j * feats, (j + 1) * feats)

        def up(t):
            rows, cols = place(t)
            u_v[t % 2] = nn(n2[rows, :], wup[:, cols])

        def act(t):
            rows, cols = place(t)
            h, g = gelu_pair(u_v[t % 2] + bu[:, cols].astype(F32))
            hid[rows, cols] = h.astype(BF)
            gp[rows, cols] = g.astype(BF)

        def down(t):
            rows, cols = place(t)
            term = nn(hid[rows, cols], wdn[cols, :])
            r, j = tiles[t]
            if j == 0:
                acc[rows, :] = rs[rows, :] + bd[...].astype(F32) + term
            elif j < chunks - 1:
                acc[rows, :] = acc[rows, :] + term
            else:
                out2[m, rows, :] = (acc[rows, :] + term).astype(BF)

                @pl.when(sec == 0)
                def _():
                    send_out(m, r).start()

        for t in range(len(tiles) + 2):
            if t < len(tiles):
                up(t)
            if 0 <= t - 2:
                down(t - 2)
            if 0 <= t - 1 < len(tiles):
                act(t - 1)

        before(("out", out2.at[0], out_o.at[0]))
        outs.start("out", out2.at[m], out_o.at[m])
        outs.start("hid", hid, hid_o.at[m])

        @pl.when(m == 0)
        def _():
            outs.start("gp", gp, gp_o)

    lane = lax.broadcasted_iota(jnp.int32, (length, 128), 1)
    ones = ((jnp.logical_and(lane >= 64, lane < 66)).astype(F32).astype(BF), (lane < 2).astype(F32).astype(BF))
    low_f = lane < HEAD_DIM
    fill = jnp.zeros((62, length), BF)

    def gin_copy(m, r):
        return pltpu.make_async_copy(rs.at[part(r, quarter)], gin_o.at[m, part(r, quarter)], sem_g.at[r])
    @pl.loop(0, micro)
    def _(step):
        m = micro - 1 - step

        def before(*sites):
            @pl.when(step > 0)
            def _():
                for site, src, dst in sites:
                    outs.wait(site, src, dst)

        loads = [pltpu.make_async_copy(a, b, sem_l.at[i]) for i, (a, b) in enumerate(
            ((gp_o, gp), (rs_o, rs), (mt_o.at[0], mt), (li_o, li), (qkv_o, qkv), (e_o, e_v)))]
        l_gp, l_rs, l_mt, l_li, l_qkv, l_e = loads

        def loaded(*copies):
            @pl.when(step > 0)
            def _():
                for c in copies:
                    c.wait()

        def fetch(*copies):
            @pl.when(step == 0)
            def _():
                for c in copies:
                    c.start()

        @pl.when(sec != 0)
        def _():
            load_cot(m).wait()

        loaded(l_gp)
        before(("ul", ul, ul_o.at[0]))
        @pl.loop(0, 2)
        def _(r):
            @pl.when(sec == 0)
            def _():
                send_grad(m, 2 * r).wait_recv()
                send_grad(m, 2 * r + 1).wait_recv()

            rows = part(r, half)
            for j in range(chunks):
                cols = slice(j * feats, (j + 1) * feats)
                ul[rows, cols] = (nt(dls[m, rows, :], wdn[cols, :]) * gp[rows, cols].astype(F32)).astype(BF)
        fetch(l_gp)

        @pl.when(step > 0)
        def _():
            for r in range(4):
                gin_copy(0, r).wait()
            l_rs.start()

        acc[...] = nt(ul[...], wup[...])
        before(("dl", dls.at[0], dl_o.at[0]), ("rl", rl, rl_o.at[0]), ("ln", ln, ln_o.at[0]))
        outs.start("dl", dls.at[m], dl_o.at[m])
        outs.start("ul", ul, ul_o.at[m])
        loaded(l_rs)
        ln[...] = jnp.zeros_like(ln)

        @pl.loop(0, length // 128)
        def _(i):
            rows = pl.ds(pl.multiple_of(i * 128, 128), 128)
            cot = acc[rows, :]
            dx, gx = norm_back(rs[rows, :], g2[...].astype(F32), cot)
            ln[2:3, :] += jnp.sum(gx, axis=0, keepdims=True)
            ln[3:4, :] += jnp.sum(cot, axis=0, keepdims=True)
            res = dls[m, rows, :].astype(F32) + dx
            rs[rows, :] = res
            rl[rows, :] = res.astype(BF)

        outs.start("rl", rl, rl_o.at[m])
        mlt[...] = nt(wout[...], rl[...]).astype(BF)
        loaded(l_mt, l_li, l_qkv, l_e)
        before(("st", st, st_o.at[0]))

        @pl.loop(0, heads // GROUP)
        def _(group):
            keep = {}

            def spot(i):
                return group * GROUP + i, pl.multiple_of((group * (GROUP // 2) + i // 2) * 128, 128), i // 2 % 2, i % 2

            def probe(i):
                head, at, p, h = spot(i)
                if h == 0:
                    k2t_v[p] = qkv[:, pl.ds(feats + at, 128)].astype(F32).T.astype(BF)
                    scale = jnp.concatenate([jnp.broadcast_to(li[pl.ds(head + g, 1), :], (64, length)) for g in (0, 1)], axis=0)
                    dot_v[p] = (mlt[pl.ds(at, 128), :].astype(F32) * scale).astype(BF)
                mine = dot_v[p, 64 * h:64 * h + 64, :]
                mixed = mt[pl.ds(pl.multiple_of(head * HEAD_DIM, HEAD_DIM), HEAD_DIM), :]
                delta = -jnp.sum(mine.astype(F32) * mixed.astype(F32), axis=0, keepdims=True)
                d_hi = delta.astype(BF)
                d_lo = (delta - d_hi.astype(F32)).astype(BF)
                extra = jnp.concatenate([d_hi, d_lo, fill], axis=0)
                da = jnp.concatenate((mine, extra) if h == 0 else (extra, mine), axis=0)
                va = qkv[:, pl.ds(2 * feats + at, 128)] * lows[h] + ones[h]
                s_v[i % 2] = nn(va, da)

            def scale_back(i):
                ds_v[i % 2] = (e_v[spot(i)[0]].astype(F32) * s_v[i % 2]).astype(BF)

            def spread(i):
                head, at, p, h = spot(i)
                ds = ds_v[i % 2]
                dv = nt(e_v[head], dot_v[p])
                dk = nn(ds, qkv[:, pl.ds(at, 128)])
                dq = nn(k2t_v[p], ds)[64 * h:64 * h + 64]
                if h == 0:
                    keep[p] = (dv, dk, dq)
                    return
                first = keep.pop(p)
                st[:, pl.ds(2 * feats + at, 128)] = jnp.where(low_f, first[0], dv).astype(BF)
                st[:, pl.ds(feats + at, 128)] = jnp.where(low_f, first[1], dk).astype(BF)
                q = jnp.concatenate([first[2], dq], axis=0).astype(BF).astype(F32) * HEAD_DIM ** -0.5
                st[:, pl.ds(at, 128)] = q.T.astype(BF)

            for t in range(GROUP + 1):
                if t < GROUP:
                    probe(t)
                if 0 <= t - 1:
                    scale_back(t - 1)
                    spread(t - 1)

        outs.start("st", st, st_o.at[m])

        @pl.when(step == 0)
        def _():
            outs.wait("mt", mt, mt_o.at[0])

        fetch(l_mt, l_li, l_qkv, l_e)
        @pl.loop(0, 4)
        def _(r):
            rows = part(r, quarter)
            cot = nt(st[rows, :], wqkv[...])
            dx, gx = norm_back(xs[m, rows, :].astype(F32), g1[...].astype(F32), cot)
            ln[0:1, :] += jnp.sum(gx, axis=0, keepdims=True)
            ln[1:2, :] += jnp.sum(cot, axis=0, keepdims=True)
            res = rs[rows, :] + dx
            rs[rows, :] = res
            gs[m, rows, :] = res.astype(BF)

            @pl.when(sec != 0)
            def _():
                send_grad(m, r).start()

            gin_copy(m, r).start()


        outs.start("ln", ln, ln_o.at[m])

    for site, src, dst in (("dl", dls.at[0], dl_o.at[0]), ("rl", rl, rl_o.at[0]), ("ln", ln, ln_o.at[0]), ("st", st, st_o.at[0]),
                           ("ul", ul, ul_o.at[0]), ("n1", n1, n1_o.at[0]), ("n2", n2, n2_o.at[0]),
                           ("hid", hid, hid_o.at[0]), ("out", out2.at[0], out_o.at[0])):
        outs.wait(site, src, dst)
    for r in range(4):
        gin_copy(0, r).wait()

    @pl.when(sec == 0)
    def _():
        for m in range(micro):
            for r in range(2):
                send_out(m, r).wait_send()

    @pl.when(sec != 0)
    def _():
        for m in range(micro):
            for r in range(4):
                send_grad(m, r).wait_send()


def relay(seg, x, cot, weights, vecs):
    micro, _, length, feats = x.shape
    ff = weights[2].shape[2]
    heads = feats // HEAD_DIM
    sds = jax.ShapeDtypeStruct

    def vmem(dtype, *shape):
        return pltpu.VMEM(shape, dtype)

    outs = [
        sds((micro, length, feats), BF),
        sds((micro, length, feats), F32),
        sds((micro, length, feats), BF),
        sds((micro, length, 3 * feats), BF),
        sds((micro, feats, length), BF),
        sds((micro, length, feats), BF),
        sds((micro, length, feats), BF),
        sds((micro, length, ff), BF),
        sds((micro, length, ff), BF),
        sds((micro, length, feats), BF),
        sds((micro, 8, feats), F32),
        sds((length, 3 * feats), BF),
        sds((heads, length, length), BF),
        sds((16, length), F32),
        sds((length, feats), F32),
        sds((length, ff), BF),
    ]
    dma = pltpu.SemaphoreType.DMA
    return pl.pallas_call(
        relay_kernel,
        out_shape=outs,
        in_specs=[VM] + [ANY] * 6 + [VM] * 9,
        out_specs=[ANY] * len(outs),
        scratch_shapes=[
            vmem(BF, feats, 3 * feats), vmem(BF, feats, feats), vmem(BF, feats, ff), vmem(BF, ff, feats),
            vmem(BF, micro, length, feats), vmem(BF, micro, length, feats), vmem(BF, micro, length, feats), vmem(BF, micro, length, feats),
            vmem(BF, length, feats), vmem(BF, length, 3 * feats), vmem(BF, feats, length), vmem(BF, heads, length, length),
            vmem(F32, 16, length), vmem(BF, feats, length), vmem(F32, length, feats), vmem(BF, length, feats),
            vmem(BF, length, ff), vmem(BF, length, ff), vmem(BF, length, ff), vmem(F32, length, feats), vmem(F32, 2, length // 2, feats),
            vmem(F32, 2, length, length), vmem(BF, length, feats), vmem(BF, feats, length), vmem(BF, length, 3 * feats),
            vmem(BF, 2, length, length), vmem(BF, 2, 128, length), vmem(BF, 2, 128, length), vmem(F32, 8, feats),
            vmem(BF, length, 128), vmem(BF, length, 128),
            dma((4,)), dma((micro,)), dma((16,)), dma((6,)), dma((4,)),
            dma((micro, 2)), dma((micro, 2)), dma((micro, 4)), dma((micro, 4)),
        ],
        compiler_params=pltpu.CompilerParams(vmem_limit_bytes=VMEM_LIMIT, collective_id=1, has_side_effects=True),
        name="layer_relay",
    )(seg, x, cot, *weights, *vecs)


INNER = 16
MASKS = (1, 2, 4, 8)
LAG = dict(s1=1, s2=3, line1=4, line2=2, end2=7, ag1=7, age=7, agy2=9, core=12, done=14)


def exchange_kernel(group, n1_hbm, st_hbm, mt_hbm, rl_hbm, n2_hbm, ul_hbm, hid_hbm, dl_hbm, ln_ref, g_o, small_o, xb,
                    a_v, b_v, mt_v, own, sb0, rb0, sby, rby, line1, line2, sbe, rbe, gath, xv, small, rsm, xsm,
                    ld_sem, out_sem, cs, cr, ys, yr, ls, lr, es, er, as_, ar, ms, mr, xs, xr, xl):
    sec = lax.axis_index("section")
    me = lax.axis_index("dp")
    size = gath.shape[1]
    half, wide, q4, q8 = size // 2, size // 2, size // 4, size // 8
    outer = group // INNER
    kq, ku, kd = st_hbm.shape[2] // size, ul_hbm.shape[2] // size, hid_hbm.shape[2] // size
    kinds = (("down", 0, kd), ("up", kd, kd + ku), ("out", kd + ku, kd + ku + 1), ("qkv", kd + ku + 1, kd + ku + 1 + kq))
    count = kinds[-1][2]
    core, y, z = me % 2, (me // 2) % 2, (me // 4) % 4
    left, right = slice(0, wide), slice(wide, size)

    def to(device):
        return dict(device_id=(sec, device), device_id_type=pl.DeviceIdType.MESH)

    def peer(mask):
        return me + mask - 2 * mask * ((me // mask) % 2)

    def outer_peer(k):
        return (me + k * INNER) % group

    barrier = pltpu.get_barrier_semaphore()
    at_end = jnp.logical_or(z == 0, z == 3)
    for mask in MASKS:
        pl.semaphore_signal(barrier, inc=1, **to(peer(mask)))
    for k in range(1, outer):
        pl.semaphore_signal(barrier, inc=1, **to(outer_peer(k)))

    pl.semaphore_signal(barrier, inc=1, **to(me + 12 - 8 * z))

    def remote(src, dst, s_sem, r_sem, device):
        return pltpu.make_async_remote_copy(src_ref=src, dst_ref=dst, send_sem=s_sem, recv_sem=r_sem, **to(device))

    def rows_of(first, rows):
        return pl.ds(pl.multiple_of(first, 16), rows)

    def by_kind(u, fn):
        for kind, low, high in kinds:
            @pl.when(jnp.logical_and(u >= low, u < high))
            def _():
                fn(kind, u - low)

    def block(ref, j, axis):
        cols = pl.ds(pl.multiple_of(j * size, size), size)
        return ref.at[:, :, cols] if axis == 2 else ref.at[:, cols] if axis == 1 else ref.at[cols, :]

    def loads(u):
        def pair(kind, j, act):
            slot = u % 2
            src_a, src_b = {
                "down": lambda: (block(hid_hbm, j, 2), dl_hbm),
                "up": lambda: (n2_hbm, block(ul_hbm, j, 2)),
                "out": lambda: (mt_hbm, rl_hbm),
                "qkv": lambda: (n1_hbm, block(st_hbm, j, 2)),
            }[kind]()
            dst_a = mt_v if kind == "out" else a_v.at[slot]
            act(pltpu.make_async_copy(src_a, dst_a, ld_sem.at[slot, 0]))
            act(pltpu.make_async_copy(src_b, b_v.at[slot], ld_sem.at[slot, 1]))
        return pair

    def start_loads(u):
        by_kind(u, lambda kind, j: loads(u)(kind, j, lambda c: c.start()))

    def core_copy(u):
        return remote(sb0.at[u % 2], rb0.at[u], cs.at[u], cr.at[u], peer(1))

    def y_copy(u):
        return remote(sby.at[u], rby.at[u], ys.at[u], yr.at[u], peer(2))

    def end_copy(u):
        return remote(sbe.at[u], rbe.at[u], es.at[u], er.at[u], peer(2))

    def line_copy(u, part, up):
        ref = line1 if part == 0 else line2
        at = (u, int(up))
        sem = (u, 2 * part + int(up))
        return remote(ref.at[at], ref.at[at], ls.at[sem], lr.at[sem], me + 4 if up else me - 4)

    def compute(u):
        slot = u % 2
        by_kind(u, lambda kind, j: loads(u)(kind, j, lambda c: c.wait()))
        start_loads(u + 1)

        def column():
            return jnp.sum(jnp.sum(b_v[slot].astype(F32), axis=0), axis=0, keepdims=True)

        def products(transposed):
            def product(which):
                cols = pl.ds(pl.multiple_of(which * half, half), half)
                if transposed:
                    total = None
                    for k in range(mt_v.shape[0]):
                        term = nn(mt_v[k, cols, :], b_v[slot, k])
                        total = term if total is None else total + term
                    return total
                value = a_v[slot, :, :, cols]
                tokens = value.shape[0] * value.shape[1]
                return tn(value.reshape(tokens, half), b_v[slot].reshape(tokens, size))

            sb0[slot] = product(1 - core).astype(BF)
            core_copy(u).start()
            own[u % own.shape[0]] = product(core)

        low, high = kinds[2][1], kinds[2][2]
        is_out = jnp.logical_and(u >= low, u < high)

        @pl.when(is_out)
        def _():
            products(True)
            small[5:6, :] = column()

        @pl.when(jnp.logical_not(is_out))
        def _():
            products(False)

        @pl.when(u == 0)
        def _():
            small[4:5, :] = column()

        for j in range(ku):
            @pl.when(u == kinds[1][1] + j)
            def _():
                small[8 + j:9 + j, :] = column()

        for j, at in ((0, 6), (kq - 1, 7)):
            @pl.when(u == kinds[3][1] + j)
            def _():
                small[at:at + 1, :] = column()

    def add_core(u):
        core_copy(u).wait()
        ref = own.at[u % own.shape[0]]
        ref[...] = ref[...] + rb0[u].astype(F32)
        sby[u] = ref[rows_of((1 - y) * q4, q4), left].astype(BF)
        y_copy(u).start()

    def add_y(u):
        y_copy(u).wait()
        ref = own.at[u % own.shape[0]]
        rows = rows_of(y * q4, q4)
        ref[rows, left] = ref[rows, left] + rby[u].astype(F32)

    def along(u, part, up):
        buf = line1 if part == 0 else line2
        ref = own.at[u % own.shape[0]]
        place = z if up else 3 - z
        if part == 0:
            rows, cols = rows_of(y * q4 + (q8 if up else 0), q8), left
        else:
            rows, cols = rows_of(q4 if up else 0, q4), right

        @pl.when(place == 0)
        def _():
            buf[u, int(up)] = ref[rows, cols].astype(BF)

        @pl.when(place > 0)
        def _():
            line_copy(u, part, up).wait_recv()
            total = ref[rows, cols] + buf[u, int(up)].astype(F32)
            ref[rows, cols] = total

            @pl.when(place < 3)
            def _():
                buf[u, int(up)] = total.astype(BF)

        @pl.when(place < 3)
        def _():
            line_copy(u, part, up).start()

        @pl.when(place == 3)
        def _():
            if part == 0:
                rows_up = rows_of(core * half + y * q4 + (q8 if up else 0), q8)
                gath[u, rows_up, left] = over_outer(u, 0, ref[rows, cols]).astype(BF)
            else:
                first = q4 if up else 0
                sbe[u] = ref[rows_of(first + (1 - y) * q8, q8), right].astype(BF)
                end_copy(u).start()

    def over_outer(u, part, total):
        if outer == 1:
            return total
        at = 2 * u + part
        xv[0] = total.astype(BF)
        own_slot = pltpu.make_async_copy(xv.at[0], xb.at[at, 0], xl.at[0])
        own_slot.start()
        copies = [remote(xv.at[0], xb.at[at, k], xs.at[at, k], xr.at[at, k], outer_peer(k)) for k in range(1, outer)]
        for c in copies:
            c.start()
        own_slot.wait()
        for c in copies:
            c.wait()
        back = pltpu.make_async_copy(xb.at[at], xv, xl.at[1])
        back.start()
        back.wait()
        result = None
        for k in range(outer):
            term = xv[(me // INNER - k + outer) % outer].astype(F32)
            result = term if result is None else result + term
        return result

    def part_of(u, part, up):
        if part == 0:
            return gath.at[u, rows_of(core * half + y * q4 + (q8 if up else 0), q8), left]
        return gath.at[u, rows_of(core * half + (q4 if up else 0), q4), right]

    def gather_line(u, part, up):
        ref = part_of(u, part, up)
        sem = (u, 2 * part + int(up))
        return remote(ref, ref, as_.at[sem], ar.at[sem], me - 4 if up else me + 4)

    def gather_y(u, up):
        ref = part_of(u, 0, up)
        sem = (u, 4 + int(up))
        return remote(ref, ref, as_.at[sem], ar.at[sem], peer(2))

    def gather_end(u):
        ref = gath.at[u, rows_of(core * half + (z // 3) * q4 + y * q8, q8), right]
        sem = (u, 6)
        return remote(ref, ref, as_.at[sem], ar.at[sem], peer(2))

    def gather_core(u):
        ref = gath.at[u, rows_of(core * half, half), :]
        sem = (u, 7)
        return remote(ref, ref, as_.at[sem], ar.at[sem], peer(1))

    def finish_end(u):
        @pl.when(at_end)
        def _():
            end_copy(u).wait()
            ref = own.at[u % own.shape[0]]
            total = ref[rows_of((z // 3) * q4 + y * q8, q8), right] + rbe[u].astype(F32)
            gath[u, rows_of(core * half + (z // 3) * q4 + y * q8, q8), right] = over_outer(u, 1, total).astype(BF)

    def end_sent(u):
        @pl.when(at_end)
        def _():
            gather_end(u).start()

    def ends_joined(u):
        @pl.when(at_end)
        def _():
            gather_end(u).wait()

    def back_along(u, part, up):
        place = 3 - z if up else z

        @pl.when(place > 0)
        def _():
            gather_line(u, part, up).wait_recv()

        @pl.when(place < 3)
        def _():
            gather_line(u, part, up).start()

        if part == 0:
            gather_y(u, up).start()

    def to_core(u):
        gather_y(u, False).wait()
        gather_y(u, True).wait()
        gather_core(u).start()

    def out_copy(u):
        return pltpu.make_async_copy(gath.at[u], g_o.at[u], out_sem.at[u])

    def done(u):
        gather_core(u).wait()
        out_copy(u).start()

    def small_copy(stage):
        return remote(small, rsm.at[stage], ms.at[stage], mr.at[stage], peer(MASKS[stage]))

    def small_step(stage):
        small_copy(stage).wait()
        small[...] = small[...] + rsm[stage]
        if stage < 3:
            small_copy(stage + 1).start()
            return
        if outer > 1:
            xsm[0] = small[...]
            copies = [remote(xsm.at[0], xsm.at[k], xs.at[2 * count, k], xr.at[2 * count, k], outer_peer(k)) for k in range(1, outer)]
            for c in copies:
                c.start()
            for c in copies:
                c.wait()
            total = None
            for k in range(outer):
                term = xsm[(me // INNER - k + outer) % outer]
                total = term if total is None else total + term
            small[...] = total
        small_o[...] = small[...]

    start_loads(0)
    small[...] = jnp.zeros_like(small)
    small[0:4, :] = jnp.sum(ln_ref[...], axis=0)[0:4, :]
    pl.semaphore_wait(barrier, len(MASKS) + outer)

    @pl.loop(0, count + LAG["done"])
    def _(tau):
        def at(lag, fn):
            u = tau - lag

            @pl.when(jnp.logical_and(u >= 0, u < count))
            def _():
                fn(u)

        at(LAG["done"], done)
        at(LAG["agy2"], ends_joined)
        at(LAG["s1"], add_core)
        for up in (True, False):
            place = z if up else 3 - z
            at(LAG["line2"] + place, lambda u: along(u, 1, up))
            at(LAG["agy2"] + 3 - place, lambda u: back_along(u, 1, up))
        at(LAG["s2"], add_y)
        for up in (True, False):
            place = z if up else 3 - z
            at(LAG["line1"] + place, lambda u: along(u, 0, up))
        at(LAG["end2"], finish_end)
        at(LAG["age"], end_sent)
        for up in (True, False):
            place = z if up else 3 - z
            at(LAG["ag1"] + 3 - place, lambda u: back_along(u, 0, up))
        at(LAG["core"], to_core)
        at(0, compute)

        @pl.when(tau == count)
        def _():
            small_copy(0).start()

        for stage in range(4):
            @pl.when(tau == count + 2 + 2 * stage)
            def _():
                small_step(stage)

    @pl.loop(0, count)
    def _(u):
        out_copy(u).wait()
        for up in (True, False):
            place = z if up else 3 - z

            @pl.when(place < 3)
            def _():
                for part in (0, 1):
                    line_copy(u, part, up).wait_send()

            @pl.when(place > 0)
            def _():
                for part in (0, 1):
                    gather_line(u, part, up).wait_send()


def exchange(group, n1, st, mt, rl, n2, ul, hid, dl, ln):
    micro, length, feats = n1.shape
    ff = ul.shape[2]
    outer = group // INNER
    count = st.shape[2] // feats + 2 * (ff // feats) + 1
    half, q4, q8 = feats // 2, feats // 4, feats // 8
    sds = jax.ShapeDtypeStruct

    def vmem(dtype, *shape):
        return pltpu.VMEM(shape, dtype)

    dma = pltpu.SemaphoreType.DMA
    return pl.pallas_call(
        functools.partial(exchange_kernel, group),
        out_shape=[sds((count, feats, feats), BF), sds((16, feats), F32),
                   sds((2 * count, outer, q8, half) if outer > 1 else (16, 128), BF)],
        in_specs=[ANY] * 8 + [VM],
        out_specs=[ANY, VM, ANY],
        scratch_shapes=[
            vmem(BF, 2, micro, length, feats),
            vmem(BF, 2, micro, length, feats),
            vmem(BF, micro, feats, length),
            vmem(F32, 8, half, feats),
            vmem(BF, 2, half, feats),
            vmem(BF, count, half, feats),
            vmem(BF, count, q4, half),
            vmem(BF, count, q4, half),
            vmem(BF, count, 2, q8, half),
            vmem(BF, count, 2, q4, half),
            vmem(BF, count, q8, half),
            vmem(BF, count, q8, half),
            vmem(BF, count, feats, feats),
            vmem(BF, outer, q8, half),
            vmem(F32, 16, feats),
            vmem(F32, 4, 16, feats),
            vmem(F32, outer, 16, feats),
            dma((2, 2)),
            dma((count,)),
            dma((count,)), dma((count,)),
            dma((count,)), dma((count,)),
            dma((count, 4)), dma((count, 4)),
            dma((count,)), dma((count,)),
            dma((count, 8)), dma((count, 8)),
            dma((4,)), dma((4,)),
            dma((2 * count + 1, outer)), dma((2 * count + 1, outer)),
            dma((2,)),
        ],
        compiler_params=pltpu.CompilerParams(vmem_limit_bytes=VMEM_LIMIT, collective_id=0, has_side_effects=True),
        name="grad_exchange",
    )(n1, st, mt, rl, n2, ul, hid, dl, ln)[:2]


def finish_kernel(g, small_hbm, block_hbm, gin_hbm, block_o, gin_o, g1_o, s1_o, gq_o, bq_o, bv_o, go_o, bo_o, g2_o, s2_o, gu_o, bu_o, gd_o, bd_o,
                  narrow, stage, small, block, gin, sem_g, sem, sem_b):
    size = g.shape[1]
    loads = [pltpu.make_async_copy(g.at[u], narrow.at[u], sem_g.at[u]) for u in range(g.shape[0])]
    for c in loads:
        c.start()
    load_small = pltpu.make_async_copy(small_hbm, small, sem_b.at[4])
    passing = [pltpu.make_async_copy(block_hbm, block, sem_b.at[0]), pltpu.make_async_copy(gin_hbm, gin, sem_b.at[1])]
    copies = [pltpu.make_async_copy(block, block_o.at[0, :, 0], sem_b.at[2]), pltpu.make_async_copy(gin, gin_o.at[0, :, 0], sem_b.at[3])]
    for c in passing + [load_small]:
        c.start()
    places = [gd_o.at[0, pl.ds(j * size, size), :] for j in range(gd_o.shape[1] // size)]
    for ref in (gu_o, go_o, gq_o):
        places += [ref.at[0, :, pl.ds(j * size, size)] for j in range(ref.shape[2] // size)]
    slots = stage.shape[0]
    running = []
    for u, place in enumerate(places):
        if u >= slots:
            running[u - slots].wait()
        loads[u].wait()
        stage[u % slots] = narrow[u].astype(F32)
        c = pltpu.make_async_copy(stage.at[u % slots], place, sem.at[u])
        c.start()
        running.append(c)
        if u == slots - 1:
            for load, store in zip(passing, copies):
                load.wait()
                store.start()
    load_small.wait()
    for ref, at in ((g1_o, 0), (s1_o, 1), (g2_o, 2), (s2_o, 3), (bd_o, 4), (bo_o, 5), (bq_o, 6), (bv_o, 7)):
        ref[...] = small[at:at + 1, :]
    for j in range(bu_o.shape[1] // size):
        bu_o[:, j * size:(j + 1) * size] = small[8 + j:9 + j, :]
    for c in running[-slots:] + copies:
        c.wait()


def finish(g, small, block_out, gin, ff):
    count, feats, _ = g.shape
    micro, length, _ = block_out.shape
    sds = jax.ShapeDtypeStruct
    vec = sds((1, feats), F32)
    outs = [sds((1, micro, 1, length, feats), BF), sds((1, micro, 1, length, feats), F32), vec, vec, sds((1, feats, 3 * feats), F32), vec, vec,
            sds((1, feats, feats), F32), vec, vec, vec, sds((1, feats, ff), F32), sds((1, ff), F32), sds((1, ff, feats), F32), vec]
    return pl.pallas_call(
        finish_kernel,
        out_shape=outs,
        in_specs=[HBM] * 4,
        out_specs=[ANY if len(o.shape) > 2 else VM for o in outs],
        scratch_shapes=[pltpu.VMEM((count, feats, feats), BF), pltpu.VMEM((4, feats, feats), F32), pltpu.VMEM((16, feats), F32),
                        pltpu.VMEM(block_out.shape, BF), pltpu.VMEM(gin.shape, F32), pltpu.SemaphoreType.DMA((count,)),
                        pltpu.SemaphoreType.DMA((count,)), pltpu.SemaphoreType.DMA((5,))],
        compiler_params=pltpu.CompilerParams(vmem_limit_bytes=40 * 2**20),
        name="finish",
    )(*[pltpu.with_memory_space_constraint(v, pltpu.HBM) for v in (g, small, block_out, gin)])


def per_device(inputs, cotangent, segments, norm1_gain, norm1_shift, w_qkv, bias_query, bias_value, w_out, bias_out,
               norm2_gain, norm2_shift, w_up, bias_up, w_down, bias_down):
    weights = (w_qkv, w_out, w_up, w_down)
    vecs = (norm1_gain, norm1_shift, bias_query, bias_value, bias_out, norm2_gain, norm2_shift, bias_up, bias_down)
    block_out, gin, n1, st, mt, rl, n2, ul, hid, dl, ln = relay(segments, inputs, cotangent, weights, vecs)[:11]
    g, small = exchange(lax.axis_size("dp"), n1, st, mt, rl, n2, ul, hid, dl, ln)
    return tuple(finish(g, small, block_out, gin, w_up.shape[2]))


def solution(mesh):
    data, seg, vec, mat = P(None, "dp", None, None), P(None, "dp", None), P("section", None), P("section", None, None)
    act = P("section", None, "dp", None, None)
    in_specs = (data, data, seg, vec, vec, mat, vec, vec, mat, vec, vec, vec, mat, vec, mat, vec)
    out_specs = (act, act, vec, vec, mat, vec, vec, mat, vec, vec, vec, mat, vec, mat, vec)
    return jax.shard_map(per_device, mesh=mesh, in_specs=in_specs, out_specs=out_specs, check_vma=False)
```

```python
import functools
import math

import jax
import jax.numpy as jnp
from jax import lax
from jax.experimental import pallas as pl
from jax.experimental.pallas import tpu as pltpu
from jax.sharding import PartitionSpec as P

HEAD_DIM = 64
GROUP = 6
BF = jnp.bfloat16
F32 = jnp.float32
FAR = float(2**30)
VMEM_LIMIT = 60 * 2**20
ANY = pl.BlockSpec(memory_space=pl.ANY)
VM = pl.BlockSpec(memory_space=pltpu.VMEM)
HBM = pl.BlockSpec(memory_space=pltpu.HBM)


def nn(left, right):
    return lax.dot_general(left, right, (((1,), (0,)), ((), ())), preferred_element_type=F32)


def nt(left, right):
    return lax.dot_general(left, right, (((1,), (1,)), ((), ())), preferred_element_type=F32)


def tn(left, right):
    return lax.dot_general(left, right, (((0,), (0,)), ((), ())), preferred_element_type=F32)


def gelu_pair(u):
    d = 1.0 + (0.3275911 / math.sqrt(2.0)) * jnp.abs(u)
    t = pl.reciprocal(d, approx=True)
    t = t * (2.0 - d * t)
    e = jnp.exp(u * u * -0.5)
    poly = 0.5 * 1.061405429
    for c in (-1.453152027, 1.421413741, -0.284496736, 0.254829592):
        poly = poly * t + 0.5 * c
    tail = poly * t * e
    cdf = jnp.where(u >= 0, 1.0 - tail, tail)
    return u * cdf, cdf + u * (e * (1.0 / math.sqrt(2.0 * math.pi)))


def normed(x):
    centred = x - jnp.mean(x, axis=-1, keepdims=True)
    rstd = lax.rsqrt(jnp.mean(centred * centred, axis=-1, keepdims=True) + 1e-06)
    return centred * rstd, rstd


def norm_back(x, gain, cot):
    xh, rstd = normed(x)
    dy = cot * gain
    m1 = jnp.mean(dy, axis=-1, keepdims=True)
    m2 = jnp.mean(dy * xh, axis=-1, keepdims=True)
    return rstd * (dy - m1 - xh * m2), cot * xh


def half_masks(length):
    lane = lax.broadcasted_iota(jnp.int32, (length, 128), 1)
    low = (lane < HEAD_DIM).astype(F32)
    return low.astype(BF), (1.0 - low).astype(BF)


class Outs:
    def __init__(self, sems):
        self.sems = sems
        self.sites = {}

    def start(self, site, src, dst):
        self.sites.setdefault(site, len(self.sites))
        copy = pltpu.make_async_copy(src, dst, self.sems.at[self.sites[site]])
        copy.start()

    def wait(self, site, src, dst):
        self.sites.setdefault(site, len(self.sites))
        pltpu.make_async_copy(src, dst, self.sems.at[self.sites[site]]).wait()


def relay_kernel(seg_ref, x_hbm, cot_hbm, wqkv_hbm, wout_hbm, wup_hbm, wdn_hbm, g1, b1, bq, bv, bo, g2, b2, bu, bd,
                 out_o, gin_o, n1_o, st_o, mt_o, rl_o, n2_o, ul_o, hid_o, dl_o, ln_o, qkv_o, e_o, li_o, rs_o, gp_o,
                 wqkv, wout, wup, wdn, xs, dls, out2, gs, n1, qkv, vt, e_v, li, mt, rs, n2, gp, hid, ul, acc, u_v, s_v, rl, mlt, st, ds_v,
                 k2t_v, dot_v, ln, qc, kc, sem_i, sem_x, sem_o, sem_l, sem_g, fs, fr, bs, br):
    sec = lax.axis_index("section")
    other = (1 - sec, lax.axis_index("dp"))
    micro, length, feats = xs.shape
    ff = hid.shape[1]
    heads = feats // HEAD_DIM
    half = length // 2
    quarter = length // 4
    chunks = ff // feats

    def remote(src, dst, s_sem, r_sem):
        return pltpu.make_async_remote_copy(
            src_ref=src, dst_ref=dst, send_sem=s_sem, recv_sem=r_sem, device_id=other, device_id_type=pl.DeviceIdType.MESH)

    def part(r, size):
        return pl.ds(r * size if isinstance(r, int) else pl.multiple_of(r * size, size), size)

    def send_out(m, r):
        rows = part(r, half)
        return remote(out2.at[m, rows], xs.at[m, rows], fs.at[m, r], fr.at[m, r])

    def send_grad(m, r):
        rows = part(r, quarter)
        return remote(gs.at[m, rows], dls.at[m, rows], bs.at[m, r], br.at[m, r])

    def load_x(m):
        return pltpu.make_async_copy(x_hbm.at[m, 0], xs.at[m], sem_x.at[m])

    def load_cot(m):
        return pltpu.make_async_copy(cot_hbm.at[m, 0], dls.at[m], sem_x.at[m])

    barrier = pltpu.get_barrier_semaphore()
    pl.semaphore_signal(barrier, inc=1, device_id=other, device_id_type=pl.DeviceIdType.MESH)
    w_qkv, w_out, w_up, w_dn = [
        pltpu.make_async_copy(src.at[0], dst, sem_i.at[i])
        for i, (src, dst) in enumerate(((wqkv_hbm, wqkv), (wout_hbm, wout), (wup_hbm, wup), (wdn_hbm, wdn)))]

    @pl.when(sec == 0)
    def _():
        load_x(0).start()

    for c in (w_qkv, w_out, w_up, w_dn):
        c.start()

    @pl.when(sec == 0)
    def _():
        for m in range(1, micro):
            load_x(m).start()

    @pl.when(sec != 0)
    def _():
        for m in range(micro):
            load_cot(m).start()

    pl.semaphore_wait(barrier, 1)
    outs = Outs(sem_o)
    lows = half_masks(length)
    row_low = (lax.broadcasted_iota(jnp.int32, (128, length), 0) < HEAD_DIM).astype(F32)
    row_lows = (row_low.astype(BF), (1.0 - row_low).astype(BF))

    @pl.loop(0, micro)
    def _(m):
        def before(*sites):
            @pl.when(m > 0)
            def _():
                for site, src, dst in sites:
                    outs.wait(site, src, dst)

        seg = jnp.broadcast_to(seg_ref[m], (128, length))
        row = lax.broadcasted_iota(jnp.int32, (128, length), 0) % HEAD_DIM
        kcode = (seg == row).astype(F32)
        qcode = jnp.where(row < 4, -FAR * (1.0 - kcode), 0.0)
        kc[...] = kcode.T.astype(BF)
        qc[...] = qcode.T.astype(BF)

        @pl.when(sec == 0)
        def _():
            load_x(m).wait()

        before(("n1", n1, n1_o.at[0]), ("qkv", qkv, qkv_o))
        @pl.loop(0, 2)
        def _(r):
            @pl.when(sec != 0)
            def _():
                send_out(m, r).wait_recv()

            @pl.loop(0, half // 128)
            def _(i):
                rows = pl.ds(pl.multiple_of(r * half + i * 128, 128), 128)
                xh, _ = normed(xs[m, rows, :].astype(F32))
                n1[rows, :] = (xh * g1[...].astype(F32) + b1[...].astype(F32)).astype(BF)

            @pl.when(jnp.logical_and(m == 0, r == 0))
            def _():
                w_qkv.wait()

            rows = part(r, half)
            q = (nn(n1[rows, :], wqkv[:, :feats]) + bq[...].astype(F32)) * HEAD_DIM ** -0.5
            qkv[rows, :feats] = q.astype(BF)
            qkv[rows, feats:2 * feats] = nn(n1[rows, :], wqkv[:, feats:2 * feats]).astype(BF)
            v = nn(n1[rows, :], wqkv[:, 2 * feats:]) + bv[...].astype(F32)
            qkv[rows, 2 * feats:] = v.astype(BF)
            vt[:, rows] = v.T.astype(BF)

        outs.start("n1", n1, n1_o.at[m])
        before(("e", e_v, e_o), ("li", li, li_o), ("mt", mt, mt_o.at[0]))

        @pl.loop(0, heads // heads)
        def _(group):
            def spot(i):
                return group * heads + i, pl.multiple_of((group * (heads // 2) + i // 2) * 128, 128), i % 2

            def score(i):
                _, at, h = spot(i)
                qa = qkv[:, pl.ds(at, 128)] * lows[h] + qc[...] * lows[1 - h]
                ka = qkv[:, pl.ds(feats + at, 128)] * lows[h] + kc[...] * lows[1 - h]
                s_v[i % 2] = nt(ka, qa)

            def expo(i):
                scores = s_v[i % 2]
                e_v[spot(i)[0]] = jnp.exp(scores - jnp.max(scores, axis=0, keepdims=True)).astype(BF)

            def mix(i):
                head, at, h = spot(i)
                ot = nn(vt[pl.ds(at, 128), :] * row_lows[h] + row_lows[1 - h], e_v[head])
                mine, ones = (slice(0, 64), slice(64, 65)) if h == 0 else (slice(64, 128), slice(0, 1))
                inv = 1.0 / ot[ones]
                li[pl.ds(head, 1), :] = inv
                mt[pl.ds(pl.multiple_of(head * HEAD_DIM, HEAD_DIM), HEAD_DIM), :] = (ot[mine] * inv).astype(BF)

            for t in range(heads + 2):
                if t < heads:
                    score(t)
                if 0 <= t - 2:
                    mix(t - 2)
                if 0 <= t - 1 < heads:
                    expo(t - 1)

        outs.start("mt", mt, mt_o.at[m])
        before(("rs", rs, rs_o), ("n2", n2, n2_o.at[0]))

        @pl.when(m == 0)
        def _():
            w_out.wait()

        rs[...] = xs[m].astype(F32) + tn(mt[...], wout[...]) + bo[...].astype(F32)

        @pl.loop(0, length // 128)
        def _(i):
            rows = pl.ds(pl.multiple_of(i * 128, 128), 128)
            xh, _ = normed(rs[rows, :])
            n2[rows, :] = (xh * g2[...].astype(F32) + b2[...].astype(F32)).astype(BF)

        outs.start("n2", n2, n2_o.at[m])
        before(("gp", gp, gp_o), ("hid", hid, hid_o.at[0]))

        @pl.when(m == 0)
        def _():
            w_up.wait()
            w_dn.wait()
            outs.start("qkv", qkv, qkv_o)
            outs.start("e", e_v, e_o)
            outs.start("li", li, li_o)
            outs.start("rs", rs, rs_o)

        tiles = [(r, j) for r in range(2) for j in range(chunks)]

        def place(t):
            r, j = tiles[t]
            return slice(r * half, (r + 1) * half), slice(j * feats, (j + 1) * feats)

        def up(t):
            rows, cols = place(t)
            u_v[t % 2] = nn(n2[rows, :], wup[:, cols])

        def act(t):
            rows, cols = place(t)
            h, g = gelu_pair(u_v[t % 2] + bu[:, cols].astype(F32))
            hid[rows, cols] = h.astype(BF)
            gp[rows, cols] = g.astype(BF)

        def down(t):
            rows, cols = place(t)
            term = nn(hid[rows, cols], wdn[cols, :])
            r, j = tiles[t]
            if j == 0:
                acc[rows, :] = rs[rows, :] + bd[...].astype(F32) + term
            elif j < chunks - 1:
                acc[rows, :] = acc[rows, :] + term
            else:
                out2[m, rows, :] = (acc[rows, :] + term).astype(BF)

                @pl.when(sec == 0)
                def _():
                    send_out(m, r).start()

        for t in range(len(tiles) + 2):
            if t < len(tiles):
                up(t)
            if 0 <= t - 2:
                down(t - 2)
            if 0 <= t - 1 < len(tiles):
                act(t - 1)

        before(("out", out2.at[0], out_o.at[0]))
        outs.start("out", out2.at[m], out_o.at[m])
        outs.start("hid", hid, hid_o.at[m])

        @pl.when(m == 0)
        def _():
            outs.start("gp", gp, gp_o)

    lane = lax.broadcasted_iota(jnp.int32, (length, 128), 1)
    ones = ((jnp.logical_and(lane >= 64, lane < 66)).astype(F32).astype(BF), (lane < 2).astype(F32).astype(BF))
    low_f = lane < HEAD_DIM
    fill = jnp.zeros((62, length), BF)

    def gin_copy(m, r):
        return pltpu.make_async_copy(rs.at[part(r, quarter)], gin_o.at[m, part(r, quarter)], sem_g.at[r])
    @pl.loop(0, micro)
    def _(step):
        m = micro - 1 - step

        def before(*sites):
            @pl.when(step > 0)
            def _():
                for site, src, dst in sites:
                    outs.wait(site, src, dst)

        loads = [pltpu.make_async_copy(a, b, sem_l.at[i]) for i, (a, b) in enumerate(
            ((gp_o, gp), (rs_o, rs), (mt_o.at[0], mt), (li_o, li), (qkv_o, qkv), (e_o, e_v)))]
        l_gp, l_rs, l_mt, l_li, l_qkv, l_e = loads

        def loaded(*copies):
            @pl.when(step > 0)
            def _():
                for c in copies:
                    c.wait()

        def fetch(*copies):
            @pl.when(step == 0)
            def _():
                for c in copies:
                    c.start()

        @pl.when(sec != 0)
        def _():
            load_cot(m).wait()

        loaded(l_gp)
        before(("ul", ul, ul_o.at[0]))
        @pl.loop(0, 2)
        def _(r):
            @pl.when(sec == 0)
            def _():
                send_grad(m, 2 * r).wait_recv()
                send_grad(m, 2 * r + 1).wait_recv()

            rows = part(r, half)
            for j in range(chunks):
                cols = slice(j * feats, (j + 1) * feats)
                ul[rows, cols] = (nt(dls[m, rows, :], wdn[cols, :]) * gp[rows, cols].astype(F32)).astype(BF)
        fetch(l_gp)

        @pl.when(step > 0)
        def _():
            for r in range(4):
                gin_copy(0, r).wait()
            l_rs.start()

        acc[...] = nt(ul[...], wup[...])
        before(("dl", dls.at[0], dl_o.at[0]), ("rl", rl, rl_o.at[0]), ("ln", ln, ln_o.at[0]))
        outs.start("dl", dls.at[m], dl_o.at[m])
        outs.start("ul", ul, ul_o.at[m])
        loaded(l_rs)
        ln[...] = jnp.zeros_like(ln)

        @pl.loop(0, length // 128)
        def _(i):
            rows = pl.ds(pl.multiple_of(i * 128, 128), 128)
            cot = acc[rows, :]
            dx, gx = norm_back(rs[rows, :], g2[...].astype(F32), cot)
            ln[2:3, :] += jnp.sum(gx, axis=0, keepdims=True)
            ln[3:4, :] += jnp.sum(cot, axis=0, keepdims=True)
            res = dls[m, rows, :].astype(F32) + dx
            rs[rows, :] = res
            rl[rows, :] = res.astype(BF)

        outs.start("rl", rl, rl_o.at[m])
        mlt[...] = nt(wout[...], rl[...]).astype(BF)
        loaded(l_mt, l_li, l_qkv, l_e)
        before(("st", st, st_o.at[0]))

        @pl.loop(0, heads // GROUP)
        def _(group):
            keep = {}

            def spot(i):
                return group * GROUP + i, pl.multiple_of((group * (GROUP // 2) + i // 2) * 128, 128), i // 2 % 2, i % 2

            def probe(i):
                head, at, p, h = spot(i)
                if h == 0:
                    k2t_v[p] = qkv[:, pl.ds(feats + at, 128)].astype(F32).T.astype(BF)
                    scale = jnp.concatenate([jnp.broadcast_to(li[pl.ds(head + g, 1), :], (64, length)) for g in (0, 1)], axis=0)
                    dot_v[p] = (mlt[pl.ds(at, 128), :].astype(F32) * scale).astype(BF)
                mine = dot_v[p, 64 * h:64 * h + 64, :]
                mixed = mt[pl.ds(pl.multiple_of(head * HEAD_DIM, HEAD_DIM), HEAD_DIM), :]
                delta = -jnp.sum(mine.astype(F32) * mixed.astype(F32), axis=0, keepdims=True)
                d_hi = delta.astype(BF)
                d_lo = (delta - d_hi.astype(F32)).astype(BF)
                extra = jnp.concatenate([d_hi, d_lo, fill], axis=0)
                da = jnp.concatenate((mine, extra) if h == 0 else (extra, mine), axis=0)
                va = qkv[:, pl.ds(2 * feats + at, 128)] * lows[h] + ones[h]
                s_v[i % 2] = nn(va, da)

            def scale_back(i):
                ds_v[i % 2] = (e_v[spot(i)[0]].astype(F32) * s_v[i % 2]).astype(BF)

            def spread(i):
                head, at, p, h = spot(i)
                ds = ds_v[i % 2]
                dv = nt(e_v[head], dot_v[p])
                dk = nn(ds, qkv[:, pl.ds(at, 128)])
                dq = nn(k2t_v[p], ds)[64 * h:64 * h + 64]
                if h == 0:
                    keep[p] = (dv, dk, dq)
                    return
                first = keep.pop(p)
                st[:, pl.ds(2 * feats + at, 128)] = jnp.where(low_f, first[0], dv).astype(BF)
                st[:, pl.ds(feats + at, 128)] = jnp.where(low_f, first[1], dk).astype(BF)
                q = jnp.concatenate([first[2], dq], axis=0).astype(BF).astype(F32) * HEAD_DIM ** -0.5
                st[:, pl.ds(at, 128)] = q.T.astype(BF)

            for t in range(GROUP + 1):
                if t < GROUP:
                    probe(t)
                if 0 <= t - 1:
                    scale_back(t - 1)
                    spread(t - 1)

        outs.start("st", st, st_o.at[m])

        @pl.when(step == 0)
        def _():
            outs.wait("mt", mt, mt_o.at[0])

        fetch(l_mt, l_li, l_qkv, l_e)
        @pl.loop(0, 4)
        def _(r):
            rows = part(r, quarter)
            cot = nt(st[rows, :], wqkv[...])
            dx, gx = norm_back(xs[m, rows, :].astype(F32), g1[...].astype(F32), cot)
            ln[0:1, :] += jnp.sum(gx, axis=0, keepdims=True)
            ln[1:2, :] += jnp.sum(cot, axis=0, keepdims=True)
            res = rs[rows, :] + dx
            rs[rows, :] = res
            gs[m, rows, :] = res.astype(BF)

            @pl.when(sec != 0)
            def _():
                send_grad(m, r).start()

            gin_copy(m, r).start()


        outs.start("ln", ln, ln_o.at[m])

    for site, src, dst in (("dl", dls.at[0], dl_o.at[0]), ("rl", rl, rl_o.at[0]), ("ln", ln, ln_o.at[0]), ("st", st, st_o.at[0]),
                           ("ul", ul, ul_o.at[0]), ("n1", n1, n1_o.at[0]), ("n2", n2, n2_o.at[0]),
                           ("hid", hid, hid_o.at[0]), ("out", out2.at[0], out_o.at[0])):
        outs.wait(site, src, dst)
    for r in range(4):
        gin_copy(0, r).wait()

    @pl.when(sec == 0)
    def _():
        for m in range(micro):
            for r in range(2):
                send_out(m, r).wait_send()

    @pl.when(sec != 0)
    def _():
        for m in range(micro):
            for r in range(4):
                send_grad(m, r).wait_send()


def relay(seg, x, cot, weights, vecs):
    micro, _, length, feats = x.shape
    ff = weights[2].shape[2]
    heads = feats // HEAD_DIM
    sds = jax.ShapeDtypeStruct

    def vmem(dtype, *shape):
        return pltpu.VMEM(shape, dtype)

    outs = [
        sds((micro, length, feats), BF),
        sds((micro, length, feats), F32),
        sds((micro, length, feats), BF),
        sds((micro, length, 3 * feats), BF),
        sds((micro, feats, length), BF),
        sds((micro, length, feats), BF),
        sds((micro, length, feats), BF),
        sds((micro, length, ff), BF),
        sds((micro, length, ff), BF),
        sds((micro, length, feats), BF),
        sds((micro, 8, feats), F32),
        sds((length, 3 * feats), BF),
        sds((heads, length, length), BF),
        sds((16, length), F32),
        sds((length, feats), F32),
        sds((length, ff), BF),
    ]
    dma = pltpu.SemaphoreType.DMA
    return pl.pallas_call(
        relay_kernel,
        out_shape=outs,
        in_specs=[VM] + [ANY] * 6 + [VM] * 9,
        out_specs=[ANY] * len(outs),
        scratch_shapes=[
            vmem(BF, feats, 3 * feats), vmem(BF, feats, feats), vmem(BF, feats, ff), vmem(BF, ff, feats),
            vmem(BF, micro, length, feats), vmem(BF, micro, length, feats), vmem(BF, micro, length, feats), vmem(BF, micro, length, feats),
            vmem(BF, length, feats), vmem(BF, length, 3 * feats), vmem(BF, feats, length), vmem(BF, heads, length, length),
            vmem(F32, 16, length), vmem(BF, feats, length), vmem(F32, length, feats), vmem(BF, length, feats),
            vmem(BF, length, ff), vmem(BF, length, ff), vmem(BF, length, ff), vmem(F32, length, feats), vmem(F32, 2, length // 2, feats),
            vmem(F32, 2, length, length), vmem(BF, length, feats), vmem(BF, feats, length), vmem(BF, length, 3 * feats),
            vmem(BF, 2, length, length), vmem(BF, 2, 128, length), vmem(BF, 2, 128, length), vmem(F32, 8, feats),
            vmem(BF, length, 128), vmem(BF, length, 128),
            dma((4,)), dma((micro,)), dma((16,)), dma((6,)), dma((4,)),
            dma((micro, 2)), dma((micro, 2)), dma((micro, 4)), dma((micro, 4)),
        ],
        compiler_params=pltpu.CompilerParams(vmem_limit_bytes=VMEM_LIMIT, collective_id=1, has_side_effects=True),
        name="layer_relay",
    )(seg, x, cot, *weights, *vecs)


INNER = 16
MASKS = (1, 2, 4, 8)
LAG = dict(s1=1, s2=3, line1=4, line2=2, end2=7, ag1=7, age=7, agy2=9, core=12, done=14)


def exchange_kernel(group, n1_hbm, st_hbm, mt_hbm, rl_hbm, n2_hbm, ul_hbm, hid_hbm, dl_hbm, ln_ref, g_o, small_o, xb,
                    a_v, b_v, mt_v, own, sb0, rb0, sby, rby, line1, line2, sbe, rbe, gath, xv, small, rsm, xsm,
                    ld_sem, out_sem, cs, cr, ys, yr, ls, lr, es, er, as_, ar, ms, mr, xs, xr, xl):
    sec = lax.axis_index("section")
    me = lax.axis_index("dp")
    size = gath.shape[1]
    half, wide, q4, q8 = size // 2, size // 2, size // 4, size // 8
    outer = group // INNER
    kq, ku, kd = st_hbm.shape[2] // size, ul_hbm.shape[2] // size, hid_hbm.shape[2] // size
    kinds = (("down", 0, kd), ("up", kd, kd + ku), ("out", kd + ku, kd + ku + 1), ("qkv", kd + ku + 1, kd + ku + 1 + kq))
    count = kinds[-1][2]
    core, y, z = me % 2, (me // 2) % 2, (me // 4) % 4
    left, right = slice(0, wide), slice(wide, size)

    def to(device):
        return dict(device_id=(sec, device), device_id_type=pl.DeviceIdType.MESH)

    def peer(mask):
        return me + mask - 2 * mask * ((me // mask) % 2)

    def outer_peer(k):
        return (me + k * INNER) % group

    barrier = pltpu.get_barrier_semaphore()
    at_end = jnp.logical_or(z == 0, z == 3)
    for mask in MASKS:
        pl.semaphore_signal(barrier, inc=1, **to(peer(mask)))
    for k in range(1, outer):
        pl.semaphore_signal(barrier, inc=1, **to(outer_peer(k)))

    pl.semaphore_signal(barrier, inc=1, **to(me + 12 - 8 * z))

    def remote(src, dst, s_sem, r_sem, device):
        return pltpu.make_async_remote_copy(src_ref=src, dst_ref=dst, send_sem=s_sem, recv_sem=r_sem, **to(device))

    def rows_of(first, rows):
        return pl.ds(pl.multiple_of(first, 16), rows)

    def by_kind(u, fn):
        for kind, low, high in kinds:
            @pl.when(jnp.logical_and(u >= low, u < high))
            def _():
                fn(kind, u - low)

    def block(ref, j, axis):
        cols = pl.ds(pl.multiple_of(j * size, size), size)
        return ref.at[:, :, cols] if axis == 2 else ref.at[:, cols] if axis == 1 else ref.at[cols, :]

    def loads(u):
        def pair(kind, j, act):
            slot = u % 2
            src_a, src_b = {
                "down": lambda: (block(hid_hbm, j, 2), dl_hbm),
                "up": lambda: (n2_hbm, block(ul_hbm, j, 2)),
                "out": lambda: (mt_hbm, rl_hbm),
                "qkv": lambda: (n1_hbm, block(st_hbm, j, 2)),
            }[kind]()
            dst_a = mt_v if kind == "out" else a_v.at[slot]
            act(pltpu.make_async_copy(src_a, dst_a, ld_sem.at[slot, 0]))
            act(pltpu.make_async_copy(src_b, b_v.at[slot], ld_sem.at[slot, 1]))
        return pair

    def start_loads(u):
        by_kind(u, lambda kind, j: loads(u)(kind, j, lambda c: c.start()))

    def core_copy(u):
        return remote(sb0.at[u % 2], rb0.at[u], cs.at[u], cr.at[u], peer(1))

    def y_copy(u):
        return remote(sby.at[u], rby.at[u], ys.at[u], yr.at[u], peer(2))

    def end_copy(u):
        return remote(sbe.at[u], rbe.at[u], es.at[u], er.at[u], peer(2))

    def line_copy(u, part, up):
        ref = line1 if part == 0 else line2
        at = (u, int(up))
        sem = (u, 2 * part + int(up))
        return remote(ref.at[at], ref.at[at], ls.at[sem], lr.at[sem], me + 4 if up else me - 4)

    def compute(u):
        slot = u % 2
        by_kind(u, lambda kind, j: loads(u)(kind, j, lambda c: c.wait()))
        start_loads(u + 1)

        def column():
            return jnp.sum(jnp.sum(b_v[slot].astype(F32), axis=0), axis=0, keepdims=True)

        def products(transposed):
            def product(which):
                cols = pl.ds(pl.multiple_of(which * half, half), half)
                if transposed:
                    total = None
                    for k in range(mt_v.shape[0]):
                        term = nn(mt_v[k, cols, :], b_v[slot, k])
                        total = term if total is None else total + term
                    return total
                value = a_v[slot, :, :, cols]
                tokens = value.shape[0] * value.shape[1]
                return tn(value.reshape(tokens, half), b_v[slot].reshape(tokens, size))

            sb0[slot] = product(1 - core).astype(BF)
            core_copy(u).start()
            own[u % own.shape[0]] = product(core)

        low, high = kinds[2][1], kinds[2][2]
        is_out = jnp.logical_and(u >= low, u < high)

        @pl.when(is_out)
        def _():
            products(True)
            small[5:6, :] = column()

        @pl.when(jnp.logical_not(is_out))
        def _():
            products(False)

        @pl.when(u == 0)
        def _():
            small[4:5, :] = column()

        for j in range(ku):
            @pl.when(u == kinds[1][1] + j)
            def _():
                small[8 + j:9 + j, :] = column()

        for j, at in ((0, 6), (kq - 1, 7)):
            @pl.when(u == kinds[3][1] + j)
            def _():
                small[at:at + 1, :] = column()

    def add_core(u):
        core_copy(u).wait()
        ref = own.at[u % own.shape[0]]
        ref[...] = ref[...] + rb0[u].astype(F32)
        sby[u] = ref[rows_of((1 - y) * q4, q4), left].astype(BF)
        y_copy(u).start()

    def add_y(u):
        y_copy(u).wait()
        ref = own.at[u % own.shape[0]]
        rows = rows_of(y * q4, q4)
        ref[rows, left] = ref[rows, left] + rby[u].astype(F32)

    def along(u, part, up):
        buf = line1 if part == 0 else line2
        ref = own.at[u % own.shape[0]]
        place = z if up else 3 - z
        if part == 0:
            rows, cols = rows_of(y * q4 + (q8 if up else 0), q8), left
        else:
            rows, cols = rows_of(q4 if up else 0, q4), right

        @pl.when(place == 0)
        def _():
            buf[u, int(up)] = ref[rows, cols].astype(BF)

        @pl.when(place > 0)
        def _():
            line_copy(u, part, up).wait_recv()
            total = ref[rows, cols] + buf[u, int(up)].astype(F32)
            ref[rows, cols] = total

            @pl.when(place < 3)
            def _():
                buf[u, int(up)] = total.astype(BF)

        @pl.when(place < 3)
        def _():
            line_copy(u, part, up).start()

        @pl.when(place == 3)
        def _():
            if part == 0:
                rows_up = rows_of(core * half + y * q4 + (q8 if up else 0), q8)
                gath[u, rows_up, left] = over_outer(u, 0, ref[rows, cols]).astype(BF)
            else:
                first = q4 if up else 0
                sbe[u] = ref[rows_of(first + (1 - y) * q8, q8), right].astype(BF)
                end_copy(u).start()

    def over_outer(u, part, total):
        if outer == 1:
            return total
        at = 2 * u + part
        xv[0] = total.astype(BF)
        own_slot = pltpu.make_async_copy(xv.at[0], xb.at[at, 0], xl.at[0])
        own_slot.start()
        copies = [remote(xv.at[0], xb.at[at, k], xs.at[at, k], xr.at[at, k], outer_peer(k)) for k in range(1, outer)]
        for c in copies:
            c.start()
        own_slot.wait()
        for c in copies:
            c.wait()
        back = pltpu.make_async_copy(xb.at[at], xv, xl.at[1])
        back.start()
        back.wait()
        result = None
        for k in range(outer):
            term = xv[(me // INNER - k + outer) % outer].astype(F32)
            result = term if result is None else result + term
        return result

    def part_of(u, part, up):
        if part == 0:
            return gath.at[u, rows_of(core * half + y * q4 + (q8 if up else 0), q8), left]
        return gath.at[u, rows_of(core * half + (q4 if up else 0), q4), right]

    def gather_line(u, part, up):
        ref = part_of(u, part, up)
        sem = (u, 2 * part + int(up))
        return remote(ref, ref, as_.at[sem], ar.at[sem], me - 4 if up else me + 4)

    def gather_y(u, up):
        ref = part_of(u, 0, up)
        sem = (u, 4 + int(up))
        return remote(ref, ref, as_.at[sem], ar.at[sem], peer(2))

    def gather_end(u):
        ref = gath.at[u, rows_of(core * half + (z // 3) * q4 + y * q8, q8), right]
        sem = (u, 6)
        return remote(ref, ref, as_.at[sem], ar.at[sem], peer(2))

    def gather_core(u):
        ref = gath.at[u, rows_of(core * half, half), :]
        sem = (u, 7)
        return remote(ref, ref, as_.at[sem], ar.at[sem], peer(1))

    def finish_end(u):
        @pl.when(at_end)
        def _():
            end_copy(u).wait()
            ref = own.at[u % own.shape[0]]
            total = ref[rows_of((z // 3) * q4 + y * q8, q8), right] + rbe[u].astype(F32)
            gath[u, rows_of(core * half + (z // 3) * q4 + y * q8, q8), right] = over_outer(u, 1, total).astype(BF)

    def end_sent(u):
        @pl.when(at_end)
        def _():
            gather_end(u).start()

    def ends_joined(u):
        @pl.when(at_end)
        def _():
            gather_end(u).wait()

    def back_along(u, part, up):
        place = 3 - z if up else z

        @pl.when(place > 0)
        def _():
            gather_line(u, part, up).wait_recv()

        @pl.when(place < 3)
        def _():
            gather_line(u, part, up).start()

        if part == 0:
            gather_y(u, up).start()

    def to_core(u):
        gather_y(u, False).wait()
        gather_y(u, True).wait()
        gather_core(u).start()

    def out_copy(u):
        return pltpu.make_async_copy(gath.at[u], g_o.at[u], out_sem.at[u])

    def done(u):
        gather_core(u).wait()
        out_copy(u).start()

    def small_copy(stage):
        return remote(small, rsm.at[stage], ms.at[stage], mr.at[stage], peer(MASKS[stage]))

    def small_step(stage):
        small_copy(stage).wait()
        small[...] = small[...] + rsm[stage]
        if stage < 3:
            small_copy(stage + 1).start()
            return
        if outer > 1:
            xsm[0] = small[...]
            copies = [remote(xsm.at[0], xsm.at[k], xs.at[2 * count, k], xr.at[2 * count, k], outer_peer(k)) for k in range(1, outer)]
            for c in copies:
                c.start()
            for c in copies:
                c.wait()
            total = None
            for k in range(outer):
                term = xsm[(me // INNER - k + outer) % outer]
                total = term if total is None else total + term
            small[...] = total
        small_o[...] = small[...]

    start_loads(0)
    small[...] = jnp.zeros_like(small)
    small[0:4, :] = jnp.sum(ln_ref[...], axis=0)[0:4, :]
    pl.semaphore_wait(barrier, len(MASKS) + outer)

    @pl.loop(0, count + LAG["done"])
    def _(tau):
        def at(lag, fn):
            u = tau - lag

            @pl.when(jnp.logical_and(u >= 0, u < count))
            def _():
                fn(u)

        at(LAG["done"], done)
        at(LAG["agy2"], ends_joined)
        at(LAG["s1"], add_core)
        for up in (True, False):
            place = z if up else 3 - z
            at(LAG["line2"] + place, lambda u: along(u, 1, up))
            at(LAG["agy2"] + 3 - place, lambda u: back_along(u, 1, up))
        at(LAG["s2"], add_y)
        for up in (True, False):
            place = z if up else 3 - z
            at(LAG["line1"] + place, lambda u: along(u, 0, up))
        at(LAG["end2"], finish_end)
        at(LAG["age"], end_sent)
        for up in (True, False):
            place = z if up else 3 - z
            at(LAG["ag1"] + 3 - place, lambda u: back_along(u, 0, up))
        at(LAG["core"], to_core)
        at(0, compute)

        @pl.when(tau == count)
        def _():
            small_copy(0).start()

        for stage in range(4):
            @pl.when(tau == count + 2 + 2 * stage)
            def _():
                small_step(stage)

    @pl.loop(0, count)
    def _(u):
        out_copy(u).wait()
        for up in (True, False):
            place = z if up else 3 - z

            @pl.when(place < 3)
            def _():
                for part in (0, 1):
                    line_copy(u, part, up).wait_send()

            @pl.when(place > 0)
            def _():
                for part in (0, 1):
                    gather_line(u, part, up).wait_send()


def exchange(group, n1, st, mt, rl, n2, ul, hid, dl, ln):
    micro, length, feats = n1.shape
    ff = ul.shape[2]
    outer = group // INNER
    count = st.shape[2] // feats + 2 * (ff // feats) + 1
    half, q4, q8 = feats // 2, feats // 4, feats // 8
    sds = jax.ShapeDtypeStruct

    def vmem(dtype, *shape):
        return pltpu.VMEM(shape, dtype)

    dma = pltpu.SemaphoreType.DMA
    return pl.pallas_call(
        functools.partial(exchange_kernel, group),
        out_shape=[sds((count, feats, feats), BF), sds((16, feats), F32),
                   sds((2 * count, outer, q8, half) if outer > 1 else (16, 128), BF)],
        in_specs=[ANY] * 8 + [VM],
        out_specs=[ANY, VM, ANY],
        scratch_shapes=[
            vmem(BF, 2, micro, length, feats),
            vmem(BF, 2, micro, length, feats),
            vmem(BF, micro, feats, length),
            vmem(F32, 8, half, feats),
            vmem(BF, 2, half, feats),
            vmem(BF, count, half, feats),
            vmem(BF, count, q4, half),
            vmem(BF, count, q4, half),
            vmem(BF, count, 2, q8, half),
            vmem(BF, count, 2, q4, half),
            vmem(BF, count, q8, half),
            vmem(BF, count, q8, half),
            vmem(BF, count, feats, feats),
            vmem(BF, outer, q8, half),
            vmem(F32, 16, feats),
            vmem(F32, 4, 16, feats),
            vmem(F32, outer, 16, feats),
            dma((2, 2)),
            dma((count,)),
            dma((count,)), dma((count,)),
            dma((count,)), dma((count,)),
            dma((count, 4)), dma((count, 4)),
            dma((count,)), dma((count,)),
            dma((count, 8)), dma((count, 8)),
            dma((4,)), dma((4,)),
            dma((2 * count + 1, outer)), dma((2 * count + 1, outer)),
            dma((2,)),
        ],
        compiler_params=pltpu.CompilerParams(vmem_limit_bytes=VMEM_LIMIT, collective_id=0, has_side_effects=True),
        name="grad_exchange",
    )(n1, st, mt, rl, n2, ul, hid, dl, ln)[:2]


def finish_kernel(g, small_hbm, block_hbm, gin_hbm, block_o, gin_o, g1_o, s1_o, gq_o, bq_o, bv_o, go_o, bo_o, g2_o, s2_o, gu_o, bu_o, gd_o, bd_o,
                  narrow, stage, small, block, gin, sem_g, sem, sem_b):
    size = g.shape[1]
    loads = [pltpu.make_async_copy(g.at[u], narrow.at[u], sem_g.at[u]) for u in range(g.shape[0])]
    for c in loads:
        c.start()
    load_small = pltpu.make_async_copy(small_hbm, small, sem_b.at[4])
    passing = [pltpu.make_async_copy(block_hbm, block, sem_b.at[0]), pltpu.make_async_copy(gin_hbm, gin, sem_b.at[1])]
    copies = [pltpu.make_async_copy(block, block_o.at[0, :, 0], sem_b.at[2]), pltpu.make_async_copy(gin, gin_o.at[0, :, 0], sem_b.at[3])]
    for c in passing + [load_small]:
        c.start()
    places = [gd_o.at[0, pl.ds(j * size, size), :] for j in range(gd_o.shape[1] // size)]
    for ref in (gu_o, go_o, gq_o):
        places += [ref.at[0, :, pl.ds(j * size, size)] for j in range(ref.shape[2] // size)]
    slots = stage.shape[0]
    running = []
    for u, place in enumerate(places):
        if u >= slots:
            running[u - slots].wait()
        loads[u].wait()
        stage[u % slots] = narrow[u].astype(F32)
        c = pltpu.make_async_copy(stage.at[u % slots], place, sem.at[u])
        c.start()
        running.append(c)
        if u == slots - 1:
            for load, store in zip(passing, copies):
                load.wait()
                store.start()
    load_small.wait()
    for ref, at in ((g1_o, 0), (s1_o, 1), (g2_o, 2), (s2_o, 3), (bd_o, 4), (bo_o, 5), (bq_o, 6), (bv_o, 7)):
        ref[...] = small[at:at + 1, :]
    for j in range(bu_o.shape[1] // size):
        bu_o[:, j * size:(j + 1) * size] = small[8 + j:9 + j, :]
    for c in running[-slots:] + copies:
        c.wait()


def finish(g, small, block_out, gin, ff):
    count, feats, _ = g.shape
    micro, length, _ = block_out.shape
    sds = jax.ShapeDtypeStruct
    vec = sds((1, feats), F32)
    outs = [sds((1, micro, 1, length, feats), BF), sds((1, micro, 1, length, feats), F32), vec, vec, sds((1, feats, 3 * feats), F32), vec, vec,
            sds((1, feats, feats), F32), vec, vec, vec, sds((1, feats, ff), F32), sds((1, ff), F32), sds((1, ff, feats), F32), vec]
    return pl.pallas_call(
        finish_kernel,
        out_shape=outs,
        in_specs=[HBM] * 4,
        out_specs=[ANY if len(o.shape) > 2 else VM for o in outs],
        scratch_shapes=[pltpu.VMEM((count, feats, feats), BF), pltpu.VMEM((4, feats, feats), F32), pltpu.VMEM((16, feats), F32),
                        pltpu.VMEM(block_out.shape, BF), pltpu.VMEM(gin.shape, F32), pltpu.SemaphoreType.DMA((count,)),
                        pltpu.SemaphoreType.DMA((count,)), pltpu.SemaphoreType.DMA((5,))],
        compiler_params=pltpu.CompilerParams(vmem_limit_bytes=40 * 2**20),
        name="finish",
    )(*[pltpu.with_memory_space_constraint(v, pltpu.HBM) for v in (g, small, block_out, gin)])


def per_device(inputs, cotangent, segments, norm1_gain, norm1_shift, w_qkv, bias_query, bias_value, w_out, bias_out,
               norm2_gain, norm2_shift, w_up, bias_up, w_down, bias_down):
    weights = (w_qkv, w_out, w_up, w_down)
    vecs = (norm1_gain, norm1_shift, bias_query, bias_value, bias_out, norm2_gain, norm2_shift, bias_up, bias_down)
    block_out, gin, n1, st, mt, rl, n2, ul, hid, dl, ln = relay(segments, inputs, cotangent, weights, vecs)[:11]
    g, small = exchange(lax.axis_size("dp"), n1, st, mt, rl, n2, ul, hid, dl, ln)
    return tuple(finish(g, small, block_out, gin, w_up.shape[2]))


def solution(mesh):
    data, seg, vec, mat = P(None, "dp", None, None), P(None, "dp", None), P("section", None), P("section", None, None)
    act = P("section", None, "dp", None, None)
    in_specs = (data, data, seg, vec, vec, mat, vec, vec, mat, vec, vec, vec, mat, vec, mat, vec)
    out_specs = (act, act, vec, vec, mat, vec, vec, mat, vec, vec, vec, mat, vec, mat, vec)
    return jax.shard_map(per_device, mesh=mesh, in_specs=in_specs, out_specs=out_specs, check_vma=False)
```
